512 devices in a mesh: row: 16 (over z_lo, x, core), col: 32 (over y, z_hi).
Axes of the slice: x: 4, y: 8, z: 8 (z_hi: 4, z_lo: 2; z = z_hi * 2 + z_lo), core: 2. Of those that a mesh axis runs over, the one named last changes fastest.
Arguments:
- pair: bfloat16 [512, 512, 128], P('row', 'col'), may hold values from -6 to 6
- pair_mask: int32 [512, 512], P('row', 'col'), may hold values from 0 to 1, as said below
- gain_tri: float32 [128], replicated, may hold values from 0.1 to 1.9
- w_left: bfloat16 [128, 256], replicated, may hold values from -0.5 to 0.5
- w_right: bfloat16 [128, 256], replicated, may hold values from -0.5 to 0.5
- w_tri_gate: bfloat16 [128, 128], replicated, may hold values from -0.5 to 0.5
- gain_mid: float32 [128], replicated, may hold values from 0.1 to 1.9
- w_tri_out: bfloat16 [128, 128], replicated, may hold values from -0.5 to 0.5
- gain_att: float32 [128], replicated, may hold values from 0.1 to 1.9
- w_attend: bfloat16 [128, 512], replicated, may hold values from -0.5 to 0.5
- w_bias: bfloat16 [128, 4], replicated, may hold values from -2 to 2
- w_attend_out: bfloat16 [128, 128], replicated, may hold values from -0.5 to 0.5
- gain_trans: float32 [128], replicated, may hold values from 0.1 to 1.9
- w_trans_in: bfloat16 [128, 1024], replicated, may hold values from -0.5 to 0.5
- w_trans_out: bfloat16 [512, 128], replicated, may hold values from -0.25 to 0.25
Outputs:
- pair_out: bfloat16 [512, 512, 128], P('row', 'col')
The draws below stay inside these ranges and needn't reach their ends.
Inputs may be any that keep to these rules, and one draw needn't show every extreme that they name: `pair_mask`: 1 where the pair of tokens is present and observed, else 0; tokens from some position on to the end are padding, and their rows and columns are 0.
All inputs are finite; a program needn't handle non-finite values.
Results may differ from the reference program's by a relative error of at most 0.025.
Values may be sent and summed in bfloat16 or wider, within the bound.
A program may use at most 64 MiB of HBM per device.

```python
import math
import jax
import jax.numpy as jnp
from jax import lax

C = 128
HEADS = 4
HEAD_DIM = 32
TRANS = 512
N = 512


def draw_pair_mask(key, part):
    key = jax.random.fold_in(key, 7)
    length_key, missing_key = jax.random.split(key)
    present = jax.random.randint(length_key, (), N // 2, N + 1)
    valid = jnp.arange(N) < present
    observed = jax.random.randint(missing_key, (N, N), 0, 8) > 0
    return (valid[:, None] & valid[None, :] & observed).astype(jnp.int32)


def level_of(key, extent, shards, smallest, largest):
    factor_of = 1.0
    for axis_at, shards_of in shards:
        heights = jax.random.uniform(jax.random.fold_in(jax.random.fold_in(key, 6), axis_at), (shards_of,), jnp.float32, smallest / len(shards), largest / len(shards))
        factor_of = factor_of * jnp.repeat(jnp.exp(heights), extent[axis_at] // shards_of).reshape((-1,) + (1,) * (len(extent) - 1 - axis_at))
    return factor_of


def noise(own_key, shape, scale, most, pieces=(), kind=jnp.bfloat16):
    result = jax.random.normal(own_key, shape, jnp.float32) * scale
    if len(pieces) > 0:
        result = level_of(own_key, shape, pieces, -0.22, 0.18) * result
    return jnp.clip(result, min=-most, max=most).astype(kind)


def setup_inputs(seed: int = 0) -> dict:
    keys = jax.random.split(jax.random.key(seed), 16)
    pair = noise(keys[0], (N, N, C), 1.0, 6.0, ((0, 16), (1, 32)))
    pair_mask = draw_pair_mask(jax.random.fold_in(keys[15], 71), 0)
    gain_tri = jnp.clip(1.0 + 0.18 * jax.random.normal(keys[2], (C,), jnp.float32), 0.1, 1.9)
    w_left = noise(keys[3], (C, 2 * C), C ** -0.5, 0.5)
    w_right = noise(keys[4], (C, 2 * C), C ** -0.5, 0.5)
    w_tri_gate = noise(keys[5], (C, C), C ** -0.5, 0.5)
    gain_mid = jnp.clip(1.0 + 0.18 * jax.random.normal(keys[6], (C,), jnp.float32), 0.1, 1.9)
    w_tri_out = noise(keys[7], (C, C), C ** -0.5, 0.5)
    gain_att = jnp.clip(1.0 + 0.18 * jax.random.normal(keys[8], (C,), jnp.float32), 0.1, 1.9)
    w_attend = noise(keys[9], (C, 4 * C), C ** -0.5, 0.5)
    w_bias = noise(keys[10], (C, HEADS), (C // 16) ** -0.5, 2.0)
    w_attend_out = noise(keys[11], (C, C), C ** -0.5, 0.5)
    gain_trans = jnp.clip(1.0 + 0.18 * jax.random.normal(keys[12], (C,), jnp.float32), 0.1, 1.9)
    w_trans_in = noise(keys[13], (C, 2 * TRANS), C ** -0.5, 0.5)
    w_trans_out = noise(keys[14], (TRANS, C), TRANS ** -0.5, 0.25)
    return {"pair": pair, "pair_mask": pair_mask, "gain_tri": gain_tri, "w_left": w_left, "w_right": w_right, "w_tri_gate": w_tri_gate, "gain_mid": gain_mid, "w_tri_out": w_tri_out, "gain_att": gain_att, "w_attend": w_attend, "w_bias": w_bias, "w_attend_out": w_attend_out, "gain_trans": gain_trans, "w_trans_in": w_trans_in, "w_trans_out": w_trans_out}


EPS = 1e-05
MASKED = -1000000000.0

def layer_norm(inputs, gain_vec):
    inputs = inputs.astype(jnp.float32)
    center = inputs - lax.optimization_barrier(jnp.mean(inputs, -1, keepdims=True))
    spread = lax.optimization_barrier(jnp.mean(center * center, -1, keepdims=True))
    return center * lax.rsqrt(spread + EPS) * gain_vec

def edges(normed, mask_flat, weight, channels):
    projected = jnp.dot(normed, weight, preferred_element_type=jnp.float32)
    return (mask_flat * jax.nn.sigmoid(projected[:, :channels]) * projected[:, channels:]).astype(jnp.bfloat16)

def reference(pair, pair_mask, gain_tri, w_left, w_right, w_tri_gate, gain_mid, w_tri_out, gain_att, w_attend, w_bias, w_attend_out, gain_trans, w_trans_in, w_trans_out):
    length = pair.shape[0]
    channels = pair.shape[2]
    cell_count = length * length
    flat_pair = pair.reshape(cell_count, channels)
    mask_flat = pair_mask.astype(jnp.float32).reshape(cell_count, 1)
    normed = layer_norm(flat_pair, gain_tri).astype(jnp.bfloat16)
    left_side = edges(normed, mask_flat, w_left, channels).reshape(length, length, channels)
    right_side = edges(normed, mask_flat, w_right, channels).reshape(length, length, channels)
    triangle = jnp.einsum('kic,kjc->ijc', left_side.astype(jnp.float32), right_side.astype(jnp.float32), precision=lax.Precision.HIGHEST)
    tri_gate = jax.nn.sigmoid(jnp.dot(normed, w_tri_gate, preferred_element_type=jnp.float32))
    tri_normed = layer_norm(triangle.reshape(cell_count, channels), gain_mid).astype(jnp.bfloat16)
    tri_update = tri_gate * jnp.dot(tri_normed, w_tri_out, preferred_element_type=jnp.float32)
    pair_one = (flat_pair.astype(jnp.float32) + tri_update).astype(jnp.bfloat16)
    normed_two = layer_norm(pair_one, gain_att).astype(jnp.bfloat16)
    projected = jnp.dot(normed_two, w_attend, preferred_element_type=jnp.float32)
    queries = projected[:, :channels].astype(jnp.bfloat16).reshape(length, length, HEADS, HEAD_DIM)
    key_vectors = projected[:, channels:2 * channels].astype(jnp.bfloat16).reshape(length, length, HEADS, HEAD_DIM)
    values = projected[:, 2 * channels:3 * channels].astype(jnp.bfloat16).reshape(length, length, HEADS, HEAD_DIM)
    att_gate = jax.nn.sigmoid(projected[:, 3 * channels:])
    pair_bias = jnp.dot(normed_two, w_bias, preferred_element_type=jnp.float32).astype(jnp.bfloat16).reshape(length, length, HEADS)
    bias_ik = jnp.transpose(pair_bias, (2, 1, 0)).astype(jnp.float32)
    score_scale = 1.0 / math.sqrt(HEAD_DIM)
    block_cols = 16

    def column_block(offset):
        query_block = lax.dynamic_slice_in_dim(queries, offset, block_cols, 1).astype(jnp.float32)
        key_block = lax.dynamic_slice_in_dim(key_vectors, offset, block_cols, 1).astype(jnp.float32)
        value_block = lax.dynamic_slice_in_dim(values, offset, block_cols, 1).astype(jnp.float32)
        mask_block = lax.dynamic_slice_in_dim(pair_mask, offset, block_cols, 1)
        scores = jnp.einsum('ijhd,kjhd->hijk', query_block, key_block, precision=lax.Precision.HIGHEST) * score_scale
        scores = scores + bias_ik[:, :, None, :]
        scores = jnp.where(jnp.transpose(mask_block)[None, None] > 0, scores, MASKED)
        probs = jax.nn.softmax(scores, -1).astype(jnp.bfloat16)
        return jnp.einsum('hijk,kjhd->ijhd', probs.astype(jnp.float32), value_block, precision=lax.Precision.HIGHEST)
    offsets = jnp.arange(0, length, block_cols).astype(jnp.int32)
    blocks = lax.map(column_block, offsets)
    attended = jnp.transpose(blocks, (1, 0, 2, 3, 4)).reshape(cell_count, channels)
    gated = (att_gate * attended).astype(jnp.bfloat16)
    pair_two = (pair_one.astype(jnp.float32) + jnp.dot(gated, w_attend_out, preferred_element_type=jnp.float32)).astype(jnp.bfloat16)
    normed_three = layer_norm(pair_two, gain_trans).astype(jnp.bfloat16)
    expanded = jnp.dot(normed_three, w_trans_in, preferred_element_type=jnp.float32)
    trans_width = w_trans_out.shape[0]
    hidden = (jax.nn.silu(expanded[:, :trans_width]) * expanded[:, trans_width:]).astype(jnp.bfloat16)
    pair_out = (pair_two.astype(jnp.float32) + jnp.dot(hidden, w_trans_out, preferred_element_type=jnp.float32)).astype(jnp.bfloat16)
    return pair_out.reshape(length, length, channels)
```

```python
import math

import jax
import jax.numpy as jnp
from jax import lax
from jax.sharding import PartitionSpec as P

HEADS = 4
HEAD_DIM = 32


EPS = 1e-05
MASKED = -1000000000.0
ROWS = 16
BY_ZH = [[y * 4 + z for z in range(4)] for y in range(8)]
BY_Y = [[y * 4 + z for y in range(8)] for z in range(4)]


def layer_norm(inputs, gain_vec):
    inputs = inputs.astype(jnp.float32)
    center = inputs - jnp.mean(inputs, -1, keepdims=True)
    spread = jnp.mean(center * center, -1, keepdims=True)
    return center * lax.rsqrt(spread + EPS) * gain_vec


def edges(normed, mask_flat, weight, channels):
    projected = jnp.dot(normed, weight, preferred_element_type=jnp.float32)
    return (mask_flat * jax.nn.sigmoid(projected[:, :channels]) * projected[:, channels:]).astype(
        jnp.bfloat16
    )


def per_device(
    pair,
    pair_mask,
    gain_tri,
    w_left,
    w_right,
    w_tri_gate,
    gain_mid,
    w_tri_out,
    gain_att,
    w_attend,
    w_bias,
    w_attend_out,
    gain_trans,
    w_trans_in,
    w_trans_out,
):
    rows_here, cols_here, channels = pair.shape
    cell_count = rows_here * cols_here
    flat_pair = pair.reshape(cell_count, channels)
    mask_flat = pair_mask.astype(jnp.float32).reshape(cell_count, 1)
    normed = layer_norm(flat_pair, gain_tri).astype(jnp.bfloat16)
    left_side = edges(normed, mask_flat, w_left, channels).reshape(rows_here, cols_here, channels)
    right_side = edges(normed, mask_flat, w_right, channels).reshape(rows_here, cols_here, channels)
    groups = channels // ROWS
    both = jnp.stack([left_side, right_side])
    both = both.reshape(2, rows_here, cols_here, ROWS, groups)
    both = jnp.transpose(both, (3, 0, 4, 1, 2))
    both = lax.all_to_all(both, "row", 0, 0)
    both = jnp.transpose(both, (1, 2, 4, 0, 3)).reshape(2, groups, cols_here, ROWS * rows_here)
    left_here = lax.all_gather(both[0], "col", axis=1, tiled=True, axis_index_groups=BY_ZH)
    right_here = lax.all_gather(both[1], "col", axis=1, tiled=True, axis_index_groups=BY_Y)
    part = jnp.einsum("cik,cjk->cij", left_here, right_here, preferred_element_type=jnp.float32)
    part = part.astype(jnp.bfloat16).reshape(groups, 64, 8, cols_here)
    part = jnp.transpose(part, (2, 0, 1, 3))
    part = lax.all_to_all(part, "col", 0, 0, axis_index_groups=BY_Y)
    part = part.reshape(8, groups, 2, rows_here, cols_here)
    part = jnp.transpose(part, (0, 2, 1, 3, 4)).reshape(ROWS, groups, rows_here, cols_here)
    part = lax.all_to_all(part, "row", 0, 0)
    triangle = jnp.transpose(part.astype(jnp.float32), (2, 3, 0, 1))
    tri_gate = jax.nn.sigmoid(jnp.dot(normed, w_tri_gate, preferred_element_type=jnp.float32))
    tri_normed = layer_norm(triangle.reshape(cell_count, channels), gain_mid).astype(jnp.bfloat16)
    tri_update = tri_gate * jnp.dot(tri_normed, w_tri_out, preferred_element_type=jnp.float32)
    pair_one = (flat_pair.astype(jnp.float32) + tri_update).astype(jnp.bfloat16)
    normed_two = layer_norm(pair_one, gain_att).astype(jnp.bfloat16)
    projected = jnp.dot(normed_two, w_attend, preferred_element_type=jnp.float32)
    att_gate = jax.nn.sigmoid(projected[:, 3 * channels :])
    pair_bias = jnp.dot(normed_two, w_bias, preferred_element_type=jnp.float32).astype(jnp.bfloat16)
    qkv = projected[:, : 3 * channels].astype(jnp.bfloat16)
    qkv = qkv.reshape(rows_here, 4, cols_here // 4, 3, HEADS, HEAD_DIM)
    qkv = jnp.transpose(qkv, (4, 1, 3, 5, 2, 0)).reshape(ROWS, 3 * HEAD_DIM * 128)
    bias_send = jnp.transpose(pair_bias.reshape(rows_here, cols_here, HEADS), (2, 1, 0))
    bias_send = jnp.broadcast_to(bias_send.reshape(HEADS, 1, 512), (HEADS, 4, 512)).reshape(ROWS, 512)
    mask_send = jnp.transpose(pair_mask.astype(jnp.bfloat16).reshape(rows_here, 4, 4), (1, 2, 0))
    mask_send = jnp.broadcast_to(mask_send.reshape(1, 4, 128), (HEADS, 4, 128)).reshape(ROWS, 128)
    message = jnp.concatenate([qkv, bias_send, mask_send], 1)
    message = lax.all_to_all(message, "row", 0, 0)
    width = 3 * HEAD_DIM * 128
    qkv = message[:, :width].reshape(ROWS, 3, HEAD_DIM, 4, rows_here)
    qkv = jnp.transpose(qkv, (1, 3, 2, 0, 4)).reshape(3, 4, HEAD_DIM, 512)
    bias = message[:, width : width + 512].reshape(ROWS, cols_here, rows_here)
    bias = jnp.transpose(bias, (1, 0, 2)).reshape(cols_here, 512)
    bias = lax.all_gather(bias, "col", axis=0, tiled=True)
    mask = message[:, width + 512 :].reshape(ROWS, 4, rows_here)
    mask = jnp.transpose(mask, (1, 0, 2)).reshape(4, 1, 512)
    scores = jnp.einsum("jdi,jdk->jik", qkv[0], qkv[1], preferred_element_type=jnp.float32)
    scores = scores * (1.0 / math.sqrt(HEAD_DIM)) + bias.astype(jnp.float32)[None]
    scores = jnp.where(mask > 0.5, scores, MASKED)
    weight = jnp.exp(scores - jnp.max(scores, -1, keepdims=True))
    total = jnp.sum(weight, -1)
    weighted = jnp.einsum(
        "jdk,jik->jdi", qkv[2], weight.astype(jnp.bfloat16), preferred_element_type=jnp.float32
    )
    attended = (weighted / total[:, None, :]).astype(jnp.bfloat16)
    attended = attended.reshape(4, HEAD_DIM, ROWS, rows_here)
    attended = jnp.transpose(attended, (2, 0, 1, 3))
    attended = lax.all_to_all(attended, "row", 0, 0)
    attended = attended.reshape(HEADS, 4, 4, HEAD_DIM, rows_here)
    attended = jnp.transpose(attended, (4, 1, 2, 0, 3)).reshape(cell_count, channels)
    attended = attended.astype(jnp.float32)
    gated = (att_gate * attended).astype(jnp.bfloat16)
    pair_two = (
        pair_one.astype(jnp.float32)
        + jnp.dot(gated, w_attend_out, preferred_element_type=jnp.float32)
    ).astype(jnp.bfloat16)
    normed_three = layer_norm(pair_two, gain_trans).astype(jnp.bfloat16)
    expanded = jnp.dot(normed_three, w_trans_in, preferred_element_type=jnp.float32)
    trans_width = w_trans_out.shape[0]
    hidden = (jax.nn.silu(expanded[:, :trans_width]) * expanded[:, trans_width:]).astype(
        jnp.bfloat16
    )
    pair_out = (
        pair_two.astype(jnp.float32)
        + jnp.dot(hidden, w_trans_out, preferred_element_type=jnp.float32)
    ).astype(jnp.bfloat16)
    return pair_out.reshape(rows_here, cols_here, channels)


def solution(mesh):
    in_specs = (
        P("row", "col", None),
        P("row", "col"),
        P(),
        P(),
        P(),
        P(),
        P(),
        P(),
        P(),
        P(),
        P(),
        P(),
        P(),
        P(),
        P(),
    )
    out_specs = P("row", "col", None)
    return jax.shard_map(
        per_device, mesh=mesh, in_specs=in_specs, out_specs=out_specs, check_vma=False
    )
```

```python
import functools
import math

import jax
import jax.numpy as jnp
from jax import lax
from jax.experimental import pallas as pl
from jax.experimental.pallas import tpu as pltpu
from jax.sharding import PartitionSpec as P

HEADS = 4
HEAD_DIM = 32
EPS = 1e-05
MASKED = -1000000000.0
LOG2E = math.log2(math.e)
ROWS = 16
YS = 8
ZS = 4
VMEM_LIMIT = 63 * 1024 * 1024
MESH = pl.DeviceIdType.MESH
F32 = jnp.float32
BF16 = jnp.bfloat16


def dot(lhs, rhs, lhs_dim, rhs_dim):
    return lax.dot_general(
        lhs, rhs, (((lhs_dim,), (rhs_dim,)), ((), ())), preferred_element_type=F32
    )


def layer_norm(inputs, gain_vec, axis=-1):
    center = inputs - jnp.mean(inputs, axis, keepdims=True)
    spread = jnp.mean(center * center, axis, keepdims=True)
    return center * lax.rsqrt(spread + EPS) * gain_vec


def swap_blocks(arrays, width):
    arrays = list(arrays)
    lane = lax.broadcasted_iota(jnp.int32, arrays[0].shape, 1)
    step = 1
    while step < len(arrays):
        shift = width * step
        odd = (lane & shift) != 0
        fresh = list(arrays)
        for low in range(len(arrays)):
            if low & step == 0:
                high = low | step
                fresh[low] = jnp.where(odd, pltpu.roll(arrays[high], shift, 1), arrays[low])
                fresh[high] = jnp.where(odd, arrays[high], pltpu.roll(arrays[low], 128 - shift, 1))
        arrays = fresh
        step *= 2
    return arrays


def kernel(
    pair_hbm, mask_hbm, gain_tri_hbm, w_left_hbm, w_right_hbm, w_tri_gate_hbm, gain_mid_hbm,
    w_tri_out_hbm, gain_att_hbm, w_attend_hbm, w_bias_hbm, w_attend_out_hbm, gain_trans_hbm,
    w_trans_in_hbm, w_trans_out_hbm,
    out_ref,
    pair_ref, mask_ref, gain_tri, w_left, w_right, w_tri_gate, gain_mid, w_tri_out, gain_att,
    w_attend, w_bias, w_attend_out, gain_trans, w_trans_in, w_trans_out, load_sems,
    work, edge_send, edge_recv, edge_work, left_all, right_all, gate_tri, tri_work, tri_send,
    tri_recv, bias_send, bias_recv, bias_work, bias_all, bias_full, mask_cols, pair_one_t, gate_att,
    qkv_send, qkv_recv, query_buf, key_buf, value_buf, att_send, att_recv,
    edge_ss, edge_rs, left_ss, left_rs, right_ss, right_rs, tri_ss, tri_rs, bias_ss, bias_rs,
    biasz_ss, biasz_rs, biasy_ss, biasy_rs, qkv_ss, qkv_rs, att_ss, att_rs,
):
    r = lax.axis_index("row")
    c = lax.axis_index("col")
    y = c // ZS
    z = c % ZS
    up = ((y + 1) % YS) * ZS + z
    down = ((y + YS - 1) % YS) * ZS + z

    def send(src, dst, ssem, rsem, row, col):
        pltpu.make_async_remote_copy(
            src_ref=src, dst_ref=dst, send_sem=ssem, recv_sem=rsem,
            device_id=(row, col), device_id_type=MESH,
        ).start()

    def wait(ref, sem):
        pltpu.make_async_copy(ref, ref, sem).wait()

    loads = [
        pltpu.make_async_copy(src, dst, load_sems.at[at])
        for at, (src, dst) in enumerate(
            [
                (pair_hbm, pair_ref), (gain_tri_hbm, gain_tri), (mask_hbm, mask_ref),
                (w_left_hbm, w_left), (w_right_hbm, w_right), (w_tri_gate_hbm, w_tri_gate),
                (gain_mid_hbm, gain_mid), (w_tri_out_hbm, w_tri_out), (gain_att_hbm, gain_att),
                (w_bias_hbm, w_bias), (w_attend_hbm, w_attend), (w_attend_out_hbm, w_attend_out),
                (gain_trans_hbm, gain_trans), (w_trans_in_hbm, w_trans_in),
                (w_trans_out_hbm, w_trans_out),
            ]
        )
    ]
    for load in loads:
        load.start()

    barrier = pltpu.get_barrier_semaphore()

    def hello(row, col):
        pl.semaphore_signal(barrier, inc=1, device_id=(row, col), device_id_type=MESH)

    @pl.loop(1, ROWS)
    def _(s):
        hello((r + s) % ROWS, c)

    @pl.loop(1, ZS)
    def _(s):
        hello(r, y * ZS + (z + s) % ZS)

    hello(r, up)
    hello(r, down)

    @pl.loop(0, 2 * YS)
    def _(s):
        row, yy = 2 * y + s // YS, s % YS

        @pl.when(jnp.logical_or(row != r, yy != y))
        def _():
            hello(row, yy * ZS + z)

    @pl.loop(0, ROWS)
    def _(s):
        @pl.when(jnp.logical_or(s != r, r // 2 != y))
        def _():
            hello(s, (r // 2) * ZS + z)

    for load in loads[:5]:
        load.wait()
    pair = pair_ref[...].astype(F32).reshape(512, 128)
    normed = layer_norm(pair, gain_tri[...]).astype(BF16)
    work[...] = normed.astype(F32)
    normed_t = jnp.concatenate([work[pl.ds(j, 32, stride=16), :] for j in range(16)], 0).astype(BF16)
    lane = lax.broadcasted_iota(jnp.int32, (32, 512), 1)
    spread = lax.broadcasted_iota(jnp.int32, (32, 512), 0) == (lane & 31)
    mask = dot(mask_ref[...].astype(F32).astype(BF16), spread.astype(F32).astype(BF16), 1, 0)
    lane = lax.broadcasted_iota(jnp.int32, (16, 512), 1)
    own = lax.broadcasted_iota(jnp.int32, (16, 512), 0) == (lane >> 5)
    mask = jnp.sum(jnp.where(own, mask, 0.0), 0, keepdims=True)
    sides = []
    for weight in (w_left, w_right):
        projected = dot(weight[...], normed_t, 0, 1)
        sides.append((mask * jax.nn.sigmoid(projected[:128]) * projected[128:]).reshape(ROWS, 8, 512))
    edge_send[...] = jnp.concatenate(sides, 1).astype(BF16)
    edge_recv[r] = edge_send[r]

    pl.semaphore_wait(
        barrier,
        (ROWS - 1) + (ZS - 1) + 2 + 2 * (2 * YS) - jnp.where(r // 2 == y, 2, 0),
    )

    @pl.loop(1, ROWS)
    def _(s):
        to = (r + s) % ROWS
        send(edge_send.at[to], edge_recv.at[r], edge_ss.at[to], edge_rs.at[r], to, c)

    for load in loads[5:]:
        load.wait()
    gate_tri[...] = jax.nn.sigmoid(dot(normed, w_tri_gate[...], 1, 0))

    @pl.loop(1, ROWS)
    def _(s):
        of = (r + s) % ROWS
        wait(edge_recv.at[of], edge_rs.at[of])

    for v in range(4):
        pieces = [
            jnp.concatenate(
                [edge_recv[4 * a + b, :, 128 * v : 128 * v + 128].astype(F32) for a in range(4)], 0
            )
            for b in range(4)
        ]
        for q, piece in enumerate(swap_blocks(pieces, 32)):
            for a in range(4):
                edge_work.at[a][pl.ds(4 * v + q, 16, stride=16), :] = piece[16 * a : 16 * a + 16]
    for a in range(4):
        block = edge_work[a].astype(BF16).reshape(2, 8, 16, 128)
        left_all[z, :, :, 128 * a : 128 * a + 128] = block[0]
        right_all[y, :, :, 128 * a : 128 * a + 128] = block[1]

    class Ring:
        def __init__(self, buf, ss, rs, size, me, to):
            self.buf, self.ss, self.rs, self.size, self.me, self.to = buf, ss, rs, size, me, to
            self.half = buf.shape[1] // 2

        def part(self, block, chunk):
            return self.buf.at[block % self.size, pl.ds(chunk * self.half, self.half)]

        def send(self, step, chunk, way):
            block = self.me + self.size - step + 1 if way == 0 else self.me + step - 1
            part = self.part(block, chunk)
            row, col = self.to[way]
            send(part, part, self.ss.at[way, step, chunk], self.rs.at[way, step, chunk], row, col)

        def land(self, step, chunk, way):
            block = self.me + self.size - step if way == 0 else self.me + step
            wait(self.part(block, chunk), self.rs.at[way, step, chunk])

        def start(self):
            for chunk in range(2):
                for way in range(2):
                    self.send(1, chunk, way)

        def turn(self, step, chunks=(0, 1)):
            last = self.size // 2
            for chunk in chunks:
                for way in range(2):
                    if step == last and way != chunk:
                        continue
                    self.land(step, chunk, way)
                    if step < last - 1 or (step == last - 1 and way == chunk):
                        self.send(step + 1, chunk, way)

        def sent(self):
            for step in range(1, self.size // 2 + 1):
                for chunk in range(2):
                    for way in range(2):
                        if step < self.size // 2 or way == chunk:
                            wait(self.part(0, 0), self.ss.at[way, step, chunk])

    y_ring = ((r, up), (r, down))
    rights_ring = Ring(right_all, right_ss, right_rs, YS, y, y_ring)
    lefts_ring = Ring(
        left_all, left_ss, left_rs, ZS, z,
        ((r, y * ZS + (z + 1) % ZS), (r, y * ZS + (z + ZS - 1) % ZS)),
    )
    bias_ring = Ring(bias_all, biasy_ss, biasy_rs, YS, y, y_ring)
    rights_ring.start()
    lefts_ring.start()
    rights_ring.turn(1)
    lefts_ring.turn(1, (0,))
    rights_ring.turn(2)
    lefts_ring.turn(1, (1,))
    rights_ring.turn(3)
    lefts_ring.turn(2)
    rights_ring.turn(4)

    for ch in range(8):
        lefts = jnp.concatenate([left_all[s, ch] for s in range(ZS)], 0)
        rights = jnp.concatenate([right_all[s, ch] for s in range(YS)], 0)
        tri_work[64 * ch : 64 * ch + 64, :] = dot(lefts, rights, 1, 1)
    pieces = [
        jnp.concatenate([tri_work[pl.ds(8 * g + m, 8, stride=64), :] for g in range(8)], 0)
        for m in range(8)
    ]
    pieces = swap_blocks(pieces, 16)
    for s in range(YS):
        for h in range(2):
            four = [pieces[s][8 * (4 * h + g) : 8 * (4 * h + g) + 8] for g in range(4)]
            rows = [jnp.concatenate(four[:2], 1), jnp.concatenate(four[2:], 1)]
            tri_send[h * YS + s] = jnp.concatenate(rows, 0).astype(BF16)

    @pl.loop(0, 2 * YS)
    def _(s):
        h = s // YS
        row, yy = 2 * y + h, (y + s) % YS
        itself = jnp.logical_and(row == r, yy == y)
        at = h * YS + yy

        @pl.when(jnp.logical_not(itself))
        def _():
            send(tri_send.at[at], tri_recv.at[r], tri_ss.at[at], tri_rs.at[r], row, yy * ZS + z)

        @pl.when(itself)
        def _():
            tri_recv[r] = tri_send[at]

    @pl.loop(0, ROWS)
    def _(s):
        @pl.when(jnp.logical_or(s != r, r // 2 != y))
        def _():
            wait(tri_recv.at[s], tri_rs.at[s])

    arrived = tri_recv[...].astype(F32)
    tri_t = jnp.concatenate(
        [arrived[:, :8].reshape(128, 256), arrived[:, 8:].reshape(128, 256)], 1
    )
    gain_col = jnp.broadcast_to(gain_mid[...], (128, 128)).T
    tri_normed = layer_norm(tri_t, jnp.concatenate([gain_col] * 4, 1), 0).astype(BF16)
    update = gate_tri[...] * dot(tri_normed, w_tri_out[...], 0, 0)
    pair_one = (pair_ref[...].astype(F32).reshape(512, 128) + update).astype(BF16)
    work[...] = pair_one.astype(F32)
    pair_t = jnp.concatenate([work[pl.ds(j, 32, stride=16), :] for j in range(16)], 0)
    pair_one_t[...] = pair_t

    normed_two = layer_norm(pair_t, gain_att[...]).astype(BF16)
    bias_t = dot(w_bias[...], normed_two, 1, 1)
    sub = lax.broadcasted_iota(jnp.int32, (16, 128), 0)
    for h in range(HEADS):
        base = jnp.zeros((16, 128), F32)
        for v in range(4):
            base = jnp.where(
                sub == v,
                jnp.broadcast_to(bias_t[h : h + 1, 128 * v : 128 * v + 128], (16, 128)),
                base,
            )
        for g in range(4):
            row = jnp.broadcast_to(mask[:, 128 * g : 128 * g + 128], (16, 128))
            bias_send[4 * h + g] = jnp.where(sub == 4, row, base).astype(BF16)
    bias_recv[r] = bias_send[r]

    @pl.loop(1, ROWS)
    def _(s):
        to = (r + s) % ROWS
        send(bias_send.at[to], bias_recv.at[r], bias_ss.at[to], bias_rs.at[r], to, c)

    projected = dot(w_attend[...], normed_two, 0, 1)
    for h in range(HEADS):
        for part in range(3):
            rows = projected[128 * part + 32 * h : 128 * part + 32 * h + 32]
            if part == 0:
                rows = rows * (LOG2E / math.sqrt(HEAD_DIM))
            for g in range(4):
                qkv_send[4 * h + g, 32 * part : 32 * part + 32, :] = rows[
                    :, 128 * g : 128 * g + 128
                ].astype(BF16)
    qkv_recv[r] = qkv_send[r]

    @pl.loop(1, ROWS)
    def _(s):
        to = (r + s) % ROWS
        send(qkv_send.at[to], qkv_recv.at[r], qkv_ss.at[to], qkv_rs.at[r], to, c)

    gate_att[...] = jax.nn.sigmoid(projected[384:])

    @pl.loop(1, ROWS)
    def _(s):
        of = (r + s) % ROWS
        wait(bias_recv.at[of], bias_rs.at[of])

    pieces = [
        jnp.concatenate([bias_recv[4 * a + b].astype(F32) for a in range(4)], 0) for b in range(4)
    ]
    for q, piece in enumerate(swap_blocks(pieces, 32)):
        for a in range(4):
            for v in range(4):
                bias_work[a, 4 * v + q : 4 * v + q + 1, :] = piece[16 * a + v : 16 * a + v + 1]
            mask_cols[q, 0:1, 128 * a : 128 * a + 128] = piece[16 * a + 4 : 16 * a + 5]
    for a in range(4):
        bias_all[y, z, :, 128 * a : 128 * a + 128] = bias_work[a].astype(BF16)

    @pl.loop(1, ZS)
    def _(s):
        to = (z + s) % ZS
        send(bias_all.at[y, z], bias_all.at[y, z], biasz_ss.at[to], biasz_rs.at[z], r, y * ZS + to)

    @pl.loop(1, ZS)
    def _(s):
        of = (z + s) % ZS
        wait(bias_all.at[y, of], biasz_rs.at[of])

    bias_ring.start()

    @pl.loop(1, ROWS)
    def _(s):
        of = (r + s) % ROWS
        wait(qkv_recv.at[of], qkv_rs.at[of])

    tail = (lax.broadcasted_iota(jnp.int32, (16, 512), 0) == 0).astype(BF16)
    for q in range(4):
        value_buf[q, 32:48, :] = tail
    for a in range(4):
        pieces = [qkv_recv[4 * a + b].astype(F32) for b in range(4)]
        for q, piece in enumerate(swap_blocks(pieces, 32)):
            piece = piece.astype(BF16)
            query_buf[q, a] = piece[:32]
            key_buf[q, :, 128 * a : 128 * a + 128] = piece[32:64]
            value_buf[q, 0:32, 128 * a : 128 * a + 128] = piece[64:]

    side = 1 - 2 * (y % 2)
    for step, apart in enumerate((0, -side, side, 2)):
        bias_ring.turn(step + 1)
        a = (y // 2 + 4 + apart) % 4
        bias_full[...] = bias_all[pl.ds(2 * a, 2)].astype(F32).reshape(128, 512) * LOG2E
        pieces = []
        for q in range(4):
            scores = dot(query_buf[q, a], key_buf[q], 0, 0) + bias_full[...]
            scores = jnp.where(mask_cols[q, 0:1, :] > 0.5, scores, MASKED)
            weight = jnp.exp2(scores - jnp.max(scores, 1, keepdims=True)).astype(BF16)
            total = dot(value_buf[q], weight, 1, 1)
            pieces.append(total[:32] / total[32:33])
        for b, piece in enumerate(swap_blocks(pieces, 32)):
            at = 4 * a + b
            att_send[at] = piece.astype(BF16)

            @pl.when(r != at)
            def _():
                send(att_send.at[at], att_recv.at[r], att_ss.at[at], att_rs.at[r], at, c)

            @pl.when(r == at)
            def _():
                att_recv[r] = att_send[at]

    @pl.loop(1, ROWS)
    def _(s):
        of = (r + s) % ROWS
        wait(att_recv.at[of], att_rs.at[of])

    attended = jnp.concatenate(
        [
            jnp.concatenate([att_recv[4 * h + g].astype(F32) for g in range(4)], 1)
            for h in range(HEADS)
        ],
        0,
    )
    gated = (gate_att[...] * attended).astype(BF16)
    pair_two = (pair_one_t[...] + dot(gated, w_attend_out[...], 0, 0)).astype(BF16).astype(F32)
    normed_three = layer_norm(pair_two, gain_trans[...]).astype(BF16)
    for part in range(4):
        rows = slice(128 * part, 128 * part + 128)
        expanded = dot(normed_three[rows], w_trans_in[...], 1, 0)
        hidden = (jax.nn.silu(expanded[:, :512]) * expanded[:, 512:]).astype(BF16)
        work[rows, :] = pair_two[rows] + dot(hidden, w_trans_out[...], 1, 0)
    for i in range(32):
        out_ref[i] = work[pl.ds(i, 16, stride=32), :].astype(BF16)

    @pl.loop(1, ROWS)
    def _(s):
        to = (r + s) % ROWS
        wait(edge_send.at[to], edge_ss.at[to])
        wait(bias_send.at[to], bias_ss.at[to])
        wait(qkv_send.at[to], qkv_ss.at[to])
        wait(att_send.at[to], att_ss.at[to])

    @pl.loop(1, ZS)
    def _(s):
        to = (z + s) % ZS
        wait(bias_all.at[0, 0], biasz_ss.at[to])

    @pl.loop(0, 2 * YS)
    def _(s):
        @pl.when(jnp.logical_or(2 * y + s // YS != r, s % YS != y))
        def _():
            wait(tri_send.at[s], tri_ss.at[s])

    for each in (rights_ring, lefts_ring, bias_ring):
        each.sent()


def per_device(
    pair, pair_mask, gain_tri, w_left, w_right, w_tri_gate, gain_mid, w_tri_out, gain_att, w_attend,
    w_bias, w_attend_out, gain_trans, w_trans_in, w_trans_out,
):
    vmem = pl.BlockSpec(memory_space=pltpu.VMEM)
    dma = pltpu.SemaphoreType.DMA
    row = lambda gain: gain.reshape(1, 128)
    return pl.pallas_call(
        kernel,
        out_shape=jax.ShapeDtypeStruct((32, 16, 128), BF16),
        in_specs=[pl.BlockSpec(memory_space=pltpu.HBM)] * 15,
        out_specs=vmem,
        scratch_shapes=[
            pltpu.VMEM((32, 16, 128), BF16),
            pltpu.VMEM((16, 32), jnp.int32),
            pltpu.VMEM((1, 128), F32),
            pltpu.VMEM((128, 256), BF16),
            pltpu.VMEM((128, 256), BF16),
            pltpu.VMEM((128, 128), BF16),
            pltpu.VMEM((1, 128), F32),
            pltpu.VMEM((128, 128), BF16),
            pltpu.VMEM((1, 128), F32),
            pltpu.VMEM((128, 512), BF16),
            pltpu.VMEM((4, 128), BF16),
            pltpu.VMEM((128, 128), BF16),
            pltpu.VMEM((1, 128), F32),
            pltpu.VMEM((128, 1024), BF16),
            pltpu.VMEM((512, 128), BF16),
            dma((15,)),
            pltpu.VMEM((512, 128), F32),
            pltpu.VMEM((16, 16, 512), BF16),
            pltpu.VMEM((16, 16, 512), BF16),
            pltpu.VMEM((4, 256, 128), F32),
            pltpu.VMEM((ZS, 8, 16, 512), BF16),
            pltpu.VMEM((YS, 8, 16, 512), BF16),
            pltpu.VMEM((512, 128), F32),
            pltpu.VMEM((512, 128), F32),
            pltpu.VMEM((16, 16, 256), BF16),
            pltpu.VMEM((16, 16, 256), BF16),
            pltpu.VMEM((16, 16, 128), BF16),
            pltpu.VMEM((16, 16, 128), BF16),
            pltpu.VMEM((4, 16, 128), F32),
            pltpu.VMEM((YS, ZS, 16, 512), BF16),
            pltpu.VMEM((128, 512), F32),
            pltpu.VMEM((4, 8, 512), F32),
            pltpu.VMEM((512, 128), F32),
            pltpu.VMEM((128, 512), F32),
            pltpu.VMEM((16, 96, 128), BF16),
            pltpu.VMEM((16, 96, 128), BF16),
            pltpu.VMEM((4, 4, 32, 128), BF16),
            pltpu.VMEM((4, 32, 512), BF16),
            pltpu.VMEM((4, 48, 512), BF16),
            pltpu.VMEM((16, 32, 128), BF16),
            pltpu.VMEM((16, 32, 128), BF16),
            dma((16,)), dma((16,)),
            dma((2, 5, 2)), dma((2, 5, 2)),
            dma((2, 5, 2)), dma((2, 5, 2)),
            dma((16,)), dma((16,)),
            dma((16,)), dma((16,)),
            dma((ZS,)), dma((ZS,)),
            dma((2, 5, 2)), dma((2, 5, 2)),
            dma((16,)), dma((16,)),
            dma((16,)), dma((16,)),
        ],
        compiler_params=pltpu.CompilerParams(
            collective_id=0, has_side_effects=True, vmem_limit_bytes=VMEM_LIMIT
        ),
    )(
        pair, pair_mask.T, row(gain_tri), w_left, w_right, w_tri_gate, row(gain_mid),
        w_tri_out, row(gain_att), w_attend, w_bias.T, w_attend_out, row(gain_trans), w_trans_in,
        w_trans_out,
    )


def solution(mesh):
    in_specs = (P("row", "col", None), P("row", "col")) + (P(),) * 13
    return jax.shard_map(
        per_device, mesh=mesh, in_specs=in_specs, out_specs=P("row", "col", None), check_vma=False
    )
```

```python
import functools
import math

import jax
import jax.numpy as jnp
from jax import lax
from jax.experimental import pallas as pl
from jax.experimental.pallas import tpu as pltpu
from jax.sharding import PartitionSpec as P

HEADS = 4
HEAD_DIM = 32
EPS = 1e-05
MASKED = -1000000000.0
LOG2E = math.log2(math.e)
ROWS = 16
YS = 8
ZS = 4
VMEM_LIMIT = 63 * 1024 * 1024
MESH = pl.DeviceIdType.MESH
F32 = jnp.float32
BF16 = jnp.bfloat16


def dot(lhs, rhs, lhs_dim, rhs_dim):
    return lax.dot_general(
        lhs, rhs, (((lhs_dim,), (rhs_dim,)), ((), ())), preferred_element_type=F32
    )


def layer_norm(inputs, gain_vec, axis=-1):
    center = inputs - jnp.mean(inputs, axis, keepdims=True)
    spread = jnp.mean(center * center, axis, keepdims=True)
    return center * lax.rsqrt(spread + EPS) * gain_vec


def swap_blocks(arrays, width):
    arrays = list(arrays)
    lane = lax.broadcasted_iota(jnp.int32, arrays[0].shape, 1)
    step = 1
    while step < len(arrays):
        shift = width * step
        odd = (lane & shift) != 0
        fresh = list(arrays)
        for low in range(len(arrays)):
            if low & step == 0:
                high = low | step
                fresh[low] = jnp.where(odd, pltpu.roll(arrays[high], shift, 1), arrays[low])
                fresh[high] = jnp.where(odd, arrays[high], pltpu.roll(arrays[low], 128 - shift, 1))
        arrays = fresh
        step *= 2
    return arrays


def kernel(
    pair_hbm, mask_hbm, gain_tri_hbm, w_left_hbm, w_right_hbm, w_tri_gate_hbm, gain_mid_hbm,
    w_tri_out_hbm, gain_att_hbm, w_attend_hbm, w_bias_hbm, w_attend_out_hbm, gain_trans_hbm,
    w_trans_in_hbm, w_trans_out_hbm,
    out_ref,
    pair_ref, mask_ref, gain_tri, w_left, w_right, w_tri_gate, gain_mid, w_tri_out, gain_att,
    w_attend, w_bias, w_attend_out, gain_trans, w_trans_in, w_trans_out, load_sems,
    work, edge_send, edge_recv, edge_work, left_all, right_all, gate_tri, tri_work, tri_send,
    tri_recv, bias_send, bias_recv, bias_work, bias_all, bias_full, mask_cols, pair_one_t, gate_att,
    qkv_send, qkv_recv, query_buf, key_buf, value_buf, att_send, att_recv,
    edge_ss, edge_rs, left_ss, left_rs, right_ss, right_rs, tri_ss, tri_rs, bias_ss, bias_rs,
    biasz_ss, biasz_rs, biasy_ss, biasy_rs, qkv_ss, qkv_rs, att_ss, att_rs,
):
    r = lax.axis_index("row")
    c = lax.axis_index("col")
    y = c // ZS
    z = c % ZS
    up = ((y + 1) % YS) * ZS + z
    down = ((y + YS - 1) % YS) * ZS + z

    def send(src, dst, ssem, rsem, row, col):
        pltpu.make_async_remote_copy(
            src_ref=src, dst_ref=dst, send_sem=ssem, recv_sem=rsem,
            device_id=(row, col), device_id_type=MESH,
        ).start()

    def wait(ref, sem):
        pltpu.make_async_copy(ref, ref, sem).wait()

    loads = [
        pltpu.make_async_copy(src, dst, load_sems.at[at])
        for at, (src, dst) in enumerate(
            [
                (pair_hbm, pair_ref), (gain_tri_hbm, gain_tri), (mask_hbm, mask_ref),
                (w_left_hbm, w_left), (w_right_hbm, w_right), (w_tri_gate_hbm, w_tri_gate),
                (gain_mid_hbm, gain_mid), (w_tri_out_hbm, w_tri_out), (gain_att_hbm, gain_att),
                (w_bias_hbm, w_bias), (w_attend_hbm, w_attend), (w_attend_out_hbm, w_attend_out),
                (gain_trans_hbm, gain_trans), (w_trans_in_hbm, w_trans_in),
                (w_trans_out_hbm, w_trans_out),
            ]
        )
    ]
    for load in loads:
        load.start()

    barrier = pltpu.get_barrier_semaphore()

    def hello(row, col):
        pl.semaphore_signal(barrier, inc=1, device_id=(row, col), device_id_type=MESH)

    @pl.loop(1, ROWS)
    def _(s):
        hello((r + s) % ROWS, c)

    @pl.loop(1, ZS)
    def _(s):
        hello(r, y * ZS + (z + s) % ZS)

    hello(r, up)
    hello(r, down)

    @pl.loop(0, 2 * YS)
    def _(s):
        row, yy = 2 * y + s // YS, s % YS

        @pl.when(jnp.logical_or(row != r, yy != y))
        def _():
            hello(row, yy * ZS + z)

    @pl.loop(0, ROWS)
    def _(s):
        @pl.when(jnp.logical_or(s != r, r // 2 != y))
        def _():
            hello(s, (r // 2) * ZS + z)

    for load in loads[:5]:
        load.wait()
    pair = pair_ref[...].astype(F32).reshape(512, 128)
    normed = layer_norm(pair, gain_tri[...]).astype(BF16)
    work[...] = normed.astype(F32)
    normed_t = jnp.concatenate([work[pl.ds(j, 32, stride=16), :] for j in range(16)], 0).astype(BF16)
    lane = lax.broadcasted_iota(jnp.int32, (32, 512), 1)
    spread = lax.broadcasted_iota(jnp.int32, (32, 512), 0) == (lane & 31)
    mask = dot(mask_ref[...].astype(F32).astype(BF16), spread.astype(F32).astype(BF16), 1, 0)
    lane = lax.broadcasted_iota(jnp.int32, (16, 512), 1)
    own = lax.broadcasted_iota(jnp.int32, (16, 512), 0) == (lane >> 5)
    mask = jnp.sum(jnp.where(own, mask, 0.0), 0, keepdims=True)
    sides = []
    for weight in (w_left, w_right):
        projected = dot(weight[...], normed_t, 0, 1)
        sides.append((mask * jax.nn.sigmoid(projected[:128]) * projected[128:]).reshape(ROWS, 8, 512))
    edge_send[...] = jnp.concatenate(sides, 1).astype(BF16)
    edge_recv[r] = edge_send[r]

    pl.semaphore_wait(
        barrier,
        (ROWS - 1) + (ZS - 1) + 2 + 2 * (2 * YS) - jnp.where(r // 2 == y, 2, 0),
    )

    @pl.loop(1, ROWS)
    def _(s):
        to = (r + s) % ROWS
        send(edge_send.at[to], edge_recv.at[r], edge_ss.at[to], edge_rs.at[r], to, c)

    for load in loads[5:]:
        load.wait()
    gate_tri[...] = jax.nn.sigmoid(dot(normed, w_tri_gate[...], 1, 0))

    @pl.loop(1, ROWS)
    def _(s):
        of = (r + s) % ROWS
        wait(edge_recv.at[of], edge_rs.at[of])

    for v in range(4):
        pieces = [
            jnp.concatenate(
                [edge_recv[4 * a + b, :, 128 * v : 128 * v + 128].astype(F32) for a in range(4)], 0
            )
            for b in range(4)
        ]
        for q, piece in enumerate(swap_blocks(pieces, 32)):
            for a in range(4):
                edge_work.at[a][pl.ds(4 * v + q, 16, stride=16), :] = piece[16 * a : 16 * a + 16]
    for a in range(4):
        block = edge_work[a].astype(BF16).reshape(2, 8, 16, 128)
        left_all[z, :, :, 128 * a : 128 * a + 128] = block[0]
        right_all[y, :, :, 128 * a : 128 * a + 128] = block[1]

    class Ring:
        def __init__(self, buf, ss, rs, size, me, to):
            self.buf, self.ss, self.rs, self.size, self.me, self.to = buf, ss, rs, size, me, to
            self.half = buf.shape[1] // 2

        def part(self, block, chunk):
            return self.buf.at[block % self.size, pl.ds(chunk * self.half, self.half)]

        def send(self, step, chunk, way):
            block = self.me + self.size - step + 1 if way == 0 else self.me + step - 1
            part = self.part(block, chunk)
            row, col = self.to[way]
            send(part, part, self.ss.at[way, step, chunk], self.rs.at[way, step, chunk], row, col)

        def land(self, step, chunk, way):
            block = self.me + self.size - step if way == 0 else self.me + step
            wait(self.part(block, chunk), self.rs.at[way, step, chunk])

        def start(self):
            for chunk in range(2):
                for way in range(2):
                    self.send(1, chunk, way)

        def turn(self, step, chunks=(0, 1)):
            last = self.size // 2
            for chunk in chunks:
                for way in range(2):
                    if step == last and way != chunk:
                        continue
                    self.land(step, chunk, way)
                    if step < last - 1 or (step == last - 1 and way == chunk):
                        self.send(step + 1, chunk, way)

        def sent(self):
            for step in range(1, self.size // 2 + 1):
                for chunk in range(2):
                    for way in range(2):
                        if step < self.size // 2 or way == chunk:
                            wait(self.part(0, 0), self.ss.at[way, step, chunk])

    y_ring = ((r, up), (r, down))
    rights_ring = Ring(right_all, right_ss, right_rs, YS, y, y_ring)
    lefts_ring = Ring(
        left_all, left_ss, left_rs, ZS, z,
        ((r, y * ZS + (z + 1) % ZS), (r, y * ZS + (z + ZS - 1) % ZS)),
    )
    bias_ring = Ring(bias_all, biasy_ss, biasy_rs, YS, y, y_ring)
    rights_ring.start()
    lefts_ring.start()
    rights_ring.turn(1)
    lefts_ring.turn(1, (0,))
    rights_ring.turn(2)
    lefts_ring.turn(1, (1,))
    rights_ring.turn(3)
    lefts_ring.turn(2)
    def reply(slot, piece):
        yy = (y + YS + slot - 3) % YS
        for h in range(2):
            four = [piece[8 * (4 * h + g) : 8 * (4 * h + g) + 8] for g in range(4)]
            rows = [jnp.concatenate(four[:2], 1), jnp.concatenate(four[2:], 1)]
            at = h * YS + yy
            tri_send[at] = jnp.concatenate(rows, 0).astype(BF16)
            row = 2 * y + h
            if slot == 3:

                @pl.when(row != r)
                def _():
                    send(tri_send.at[at], tri_recv.at[r], tri_ss.at[at], tri_rs.at[r], row, c)

                @pl.when(row == r)
                def _():
                    tri_recv[r] = tri_send[at]

            else:
                send(
                    tri_send.at[at], tri_recv.at[r], tri_ss.at[at], tri_rs.at[r], row, yy * ZS + z
                )

    def products(slots):
        for ch in range(8):
            lefts = jnp.concatenate([left_all[s, ch] for s in range(ZS)], 0)
            rights = [right_all[(y + YS + s - 3) % YS, ch] for s in slots]
            found = dot(lefts, jnp.concatenate(rights, 0), 1, 1)
            tri_work[64 * ch : 64 * ch + 64, 0 : 16 * len(rights)] = found
        return [
            jnp.concatenate([tri_work[pl.ds(8 * g + m, 8, stride=64), :] for g in range(8)], 0)
            for m in range(8)
        ]

    tri_work[...] = jnp.zeros_like(tri_work)
    pieces = swap_blocks(products(range(7)), 16)
    for slot in (2, 4, 1, 5, 0, 6, 3):
        reply(slot, pieces[slot])
    rights_ring.turn(4)
    pieces = products([7])
    lane = lax.broadcasted_iota(jnp.int32, pieces[0].shape, 1) >> 4
    merged = pieces[0]
    for m in range(1, 8):
        merged = jnp.where(lane == m, pltpu.roll(pieces[m], 16 * m, 1), merged)
    reply(7, merged)

    @pl.loop(0, ROWS)
    def _(s):
        @pl.when(jnp.logical_or(s != r, r // 2 != y))
        def _():
            wait(tri_recv.at[s], tri_rs.at[s])

    arrived = tri_recv[...].astype(F32)
    tri_t = jnp.concatenate(
        [arrived[:, :8].reshape(128, 256), arrived[:, 8:].reshape(128, 256)], 1
    )
    gain_col = jnp.broadcast_to(gain_mid[...], (128, 128)).T
    tri_normed = layer_norm(tri_t, jnp.concatenate([gain_col] * 4, 1), 0).astype(BF16)
    update = gate_tri[...] * dot(tri_normed, w_tri_out[...], 0, 0)
    pair_one = (pair_ref[...].astype(F32).reshape(512, 128) + update).astype(BF16)
    work[...] = pair_one.astype(F32)
    pair_t = jnp.concatenate([work[pl.ds(j, 32, stride=16), :] for j in range(16)], 0)
    pair_one_t[...] = pair_t

    normed_two = layer_norm(pair_t, gain_att[...]).astype(BF16)
    bias_t = dot(w_bias[...], normed_two, 1, 1)
    sub = lax.broadcasted_iota(jnp.int32, (16, 128), 0)
    for h in range(HEADS):
        base = jnp.zeros((16, 128), F32)
        for v in range(4):
            base = jnp.where(
                sub == v,
                jnp.broadcast_to(bias_t[h : h + 1, 128 * v : 128 * v + 128], (16, 128)),
                base,
            )
        for g in range(4):
            row = jnp.broadcast_to(mask[:, 128 * g : 128 * g + 128], (16, 128))
            bias_send[4 * h + g] = jnp.where(sub == 4, row, base).astype(BF16)
    bias_recv[r] = bias_send[r]

    @pl.loop(1, ROWS)
    def _(s):
        to = (r + s) % ROWS
        send(bias_send.at[to], bias_recv.at[r], bias_ss.at[to], bias_rs.at[r], to, c)

    projected = dot(w_attend[...], normed_two, 0, 1)
    for h in range(HEADS):
        for part in range(3):
            rows = projected[128 * part + 32 * h : 128 * part + 32 * h + 32]
            if part == 0:
                rows = rows * (LOG2E / math.sqrt(HEAD_DIM))
            for g in range(4):
                qkv_send[4 * h + g, 32 * part : 32 * part + 32, :] = rows[
                    :, 128 * g : 128 * g + 128
                ].astype(BF16)
    qkv_recv[r] = qkv_send[r]

    @pl.loop(1, ROWS)
    def _(s):
        to = (r + s) % ROWS
        send(qkv_send.at[to], qkv_recv.at[r], qkv_ss.at[to], qkv_rs.at[r], to, c)

    gate_att[...] = jax.nn.sigmoid(projected[384:])

    @pl.loop(1, ROWS)
    def _(s):
        of = (r + s) % ROWS
        wait(bias_recv.at[of], bias_rs.at[of])

    pieces = [
        jnp.concatenate([bias_recv[4 * a + b].astype(F32) for a in range(4)], 0) for b in range(4)
    ]
    for q, piece in enumerate(swap_blocks(pieces, 32)):
        for a in range(4):
            for v in range(4):
                bias_work[a, 4 * v + q : 4 * v + q + 1, :] = piece[16 * a + v : 16 * a + v + 1]
            mask_cols[q, 0:1, 128 * a : 128 * a + 128] = piece[16 * a + 4 : 16 * a + 5]
    for a in range(4):
        bias_all[y, z, :, 128 * a : 128 * a + 128] = bias_work[a].astype(BF16)

    @pl.loop(1, ZS)
    def _(s):
        to = (z + s) % ZS
        send(bias_all.at[y, z], bias_all.at[y, z], biasz_ss.at[to], biasz_rs.at[z], r, y * ZS + to)

    @pl.loop(1, ZS)
    def _(s):
        of = (z + s) % ZS
        wait(bias_all.at[y, of], biasz_rs.at[of])

    bias_ring.start()
    bias_ring.turn(1)

    @pl.loop(1, ROWS)
    def _(s):
        of = (r + s) % ROWS
        wait(qkv_recv.at[of], qkv_rs.at[of])

    bias_ring.turn(2)
    tail = (lax.broadcasted_iota(jnp.int32, (16, 512), 0) == 0).astype(BF16)
    for q in range(4):
        value_buf[q, 32:48, :] = tail
    for a in range(4):
        pieces = [qkv_recv[4 * a + b].astype(F32) for b in range(4)]
        for q, piece in enumerate(swap_blocks(pieces, 32)):
            piece = piece.astype(BF16)
            query_buf[q, a] = piece[:32]
            key_buf[q, :, 128 * a : 128 * a + 128] = piece[32:64]
            value_buf[q, 0:32, 128 * a : 128 * a + 128] = piece[64:]

    side = 1 - 2 * (y % 2)
    for step, apart in enumerate((0, -side, side, 2)):
        if step in (1, 3):
            bias_ring.turn(3 + step // 2)
        a = (y // 2 + 4 + apart) % 4
        bias_full[...] = bias_all[pl.ds(2 * a, 2)].astype(F32).reshape(128, 512) * LOG2E
        pieces = []
        for q in range(4):
            scores = dot(query_buf[q, a], key_buf[q], 0, 0) + bias_full[...]
            scores = jnp.where(mask_cols[q, 0:1, :] > 0.5, scores, MASKED)
            weight = jnp.exp2(scores - jnp.max(scores, 1, keepdims=True)).astype(BF16)
            total = dot(value_buf[q], weight, 1, 1)
            pieces.append(total[:32] / total[32:33])
        for b, piece in enumerate(swap_blocks(pieces, 32)):
            at = 4 * a + b
            att_send[at] = piece.astype(BF16)

            @pl.when(r != at)
            def _():
                send(att_send.at[at], att_recv.at[r], att_ss.at[at], att_rs.at[r], at, c)

            @pl.when(r == at)
            def _():
                att_recv[r] = att_send[at]

    @pl.loop(1, ROWS)
    def _(s):
        of = (r + s) % ROWS
        wait(att_recv.at[of], att_rs.at[of])

    attended = jnp.concatenate(
        [
            jnp.concatenate([att_recv[4 * h + g].astype(F32) for g in range(4)], 1)
            for h in range(HEADS)
        ],
        0,
    )
    gated = (gate_att[...] * attended).astype(BF16)
    pair_two = (pair_one_t[...] + dot(gated, w_attend_out[...], 0, 0)).astype(BF16).astype(F32)
    normed_three = layer_norm(pair_two, gain_trans[...]).astype(BF16)
    for part in range(4):
        rows = slice(128 * part, 128 * part + 128)
        expanded = dot(normed_three[rows], w_trans_in[...], 1, 0)
        hidden = (jax.nn.silu(expanded[:, :512]) * expanded[:, 512:]).astype(BF16)
        work[rows, :] = pair_two[rows] + dot(hidden, w_trans_out[...], 1, 0)
    for i in range(32):
        out_ref[i] = work[pl.ds(i, 16, stride=32), :].astype(BF16)

    @pl.loop(1, ROWS)
    def _(s):
        to = (r + s) % ROWS
        wait(edge_send.at[to], edge_ss.at[to])
        wait(bias_send.at[to], bias_ss.at[to])
        wait(qkv_send.at[to], qkv_ss.at[to])
        wait(att_send.at[to], att_ss.at[to])

    @pl.loop(1, ZS)
    def _(s):
        to = (z + s) % ZS
        wait(bias_all.at[0, 0], biasz_ss.at[to])

    @pl.loop(0, 2 * YS)
    def _(s):
        @pl.when(jnp.logical_or(2 * y + s // YS != r, s % YS != y))
        def _():
            wait(tri_send.at[s], tri_ss.at[s])

    for each in (rights_ring, lefts_ring, bias_ring):
        each.sent()


def per_device(
    pair, pair_mask, gain_tri, w_left, w_right, w_tri_gate, gain_mid, w_tri_out, gain_att, w_attend,
    w_bias, w_attend_out, gain_trans, w_trans_in, w_trans_out,
):
    vmem = pl.BlockSpec(memory_space=pltpu.VMEM)
    dma = pltpu.SemaphoreType.DMA
    row = lambda gain: gain.reshape(1, 128)
    return pl.pallas_call(
        kernel,
        out_shape=pltpu.VMEM((32, 16, 128), BF16),
        in_specs=[pl.BlockSpec(memory_space=pltpu.HBM)] * 15,
        out_specs=vmem,
        scratch_shapes=[
            pltpu.VMEM((32, 16, 128), BF16),
            pltpu.VMEM((16, 32), jnp.int32),
            pltpu.VMEM((1, 128), F32),
            pltpu.VMEM((128, 256), BF16),
            pltpu.VMEM((128, 256), BF16),
            pltpu.VMEM((128, 128), BF16),
            pltpu.VMEM((1, 128), F32),
            pltpu.VMEM((128, 128), BF16),
            pltpu.VMEM((1, 128), F32),
            pltpu.VMEM((128, 512), BF16),
            pltpu.VMEM((4, 128), BF16),
            pltpu.VMEM((128, 128), BF16),
            pltpu.VMEM((1, 128), F32),
            pltpu.VMEM((128, 1024), BF16),
            pltpu.VMEM((512, 128), BF16),
            dma((15,)),
            pltpu.VMEM((512, 128), F32),
            pltpu.VMEM((16, 16, 512), BF16),
            pltpu.VMEM((16, 16, 512), BF16),
            pltpu.VMEM((4, 256, 128), F32),
            pltpu.VMEM((ZS, 8, 16, 512), BF16),
            pltpu.VMEM((YS, 8, 16, 512), BF16),
            pltpu.VMEM((512, 128), F32),
            pltpu.VMEM((512, 128), F32),
            pltpu.VMEM((16, 16, 256), BF16),
            pltpu.VMEM((16, 16, 256), BF16),
            pltpu.VMEM((16, 16, 128), BF16),
            pltpu.VMEM((16, 16, 128), BF16),
            pltpu.VMEM((4, 16, 128), F32),
            pltpu.VMEM((YS, ZS, 16, 512), BF16),
            pltpu.VMEM((128, 512), F32),
            pltpu.VMEM((4, 8, 512), F32),
            pltpu.VMEM((512, 128), F32),
            pltpu.VMEM((128, 512), F32),
            pltpu.VMEM((16, 96, 128), BF16),
            pltpu.VMEM((16, 96, 128), BF16),
            pltpu.VMEM((4, 4, 32, 128), BF16),
            pltpu.VMEM((4, 32, 512), BF16),
            pltpu.VMEM((4, 48, 512), BF16),
            pltpu.VMEM((16, 32, 128), BF16),
            pltpu.VMEM((16, 32, 128), BF16),
            dma((16,)), dma((16,)),
            dma((2, 5, 2)), dma((2, 5, 2)),
            dma((2, 5, 2)), dma((2, 5, 2)),
            dma((16,)), dma((16,)),
            dma((16,)), dma((16,)),
            dma((ZS,)), dma((ZS,)),
            dma((2, 5, 2)), dma((2, 5, 2)),
            dma((16,)), dma((16,)),
            dma((16,)), dma((16,)),
        ],
        compiler_params=pltpu.CompilerParams(
            collective_id=0, has_side_effects=True, vmem_limit_bytes=VMEM_LIMIT
        ),
    )(
        pair, pair_mask.T, row(gain_tri), w_left, w_right, w_tri_gate, row(gain_mid),
        w_tri_out, row(gain_att), w_attend, w_bias.T, w_attend_out, row(gain_trans), w_trans_in,
        w_trans_out,
    )


def solution(mesh):
    in_specs = (P("row", "col", None), P("row", "col")) + (P(),) * 13
    return jax.shard_map(
        per_device, mesh=mesh, in_specs=in_specs, out_specs=P("row", "col", None), check_vma=False
    )
```

```python
import functools
import math

import jax
import jax.numpy as jnp
from jax import lax
from jax.experimental import pallas as pl
from jax.experimental.pallas import tpu as pltpu
from jax.sharding import PartitionSpec as P

HEADS = 4
HEAD_DIM = 32
EPS = 1e-05
MASKED = -1000000000.0
LOG2E = math.log2(math.e)
ROWS = 16
YS = 8
ZS = 4
VMEM_LIMIT = 63 * 1024 * 1024
MESH = pl.DeviceIdType.MESH
F32 = jnp.float32
BF16 = jnp.bfloat16


def dot(lhs, rhs, lhs_dim, rhs_dim):
    return lax.dot_general(
        lhs, rhs, (((lhs_dim,), (rhs_dim,)), ((), ())), preferred_element_type=F32
    )


def layer_norm(inputs, gain_vec, axis=-1):
    center = inputs - jnp.mean(inputs, axis, keepdims=True)
    spread = jnp.mean(center * center, axis, keepdims=True)
    return center * lax.rsqrt(spread + EPS) * gain_vec


def swap_blocks(arrays, width):
    arrays = list(arrays)
    lane = lax.broadcasted_iota(jnp.int32, arrays[0].shape, 1)
    step = 1
    while step < len(arrays):
        shift = width * step
        odd = (lane & shift) != 0
        fresh = list(arrays)
        for low in range(len(arrays)):
            if low & step == 0:
                high = low | step
                fresh[low] = jnp.where(odd, pltpu.roll(arrays[high], shift, 1), arrays[low])
                fresh[high] = jnp.where(odd, arrays[high], pltpu.roll(arrays[low], 128 - shift, 1))
        arrays = fresh
        step *= 2
    return arrays


def kernel(
    pair_hbm, mask_hbm, gain_tri_hbm, w_left_hbm, w_right_hbm, w_tri_gate_hbm, gain_mid_hbm,
    w_tri_out_hbm, gain_att_hbm, w_attend_hbm, w_bias_hbm, w_attend_out_hbm, gain_trans_hbm,
    w_trans_in_hbm, w_trans_out_hbm,
    out_ref,
    pair_ref, mask_ref, gain_tri, w_left, w_right, w_tri_gate, gain_mid, w_tri_out, gain_att,
    w_attend, w_bias, w_attend_out, gain_trans, w_trans_in, w_trans_out, load_sems,
    work, edge_send, edge_recv, edge_work, near_all, far_all, gate_tri, tri_work, tri_send,
    tri_recv, bias_send, bias_recv, bias_work, bias_all, bias_full, mask_cols, pair_one_t, gate_att,
    qkv_send, qkv_recv, query_buf, key_buf, value_buf, att_send, att_recv,
    edge_ss, edge_rs, near_ss, near_rs, far_ss, far_rs, tri_ss, tri_rs, bias_ss, bias_rs,
    biasz_ss, biasz_rs, biasy_ss, biasy_rs, qkv_ss, qkv_rs, att_ss, att_rs,
):
    r = lax.axis_index("row")
    c = lax.axis_index("col")
    y = c >> 2
    z = c & (ZS - 1)
    up = ((y + 1) & (YS - 1)) * ZS + z
    down = ((y + YS - 1) & (YS - 1)) * ZS + z

    def send(src, dst, ssem, rsem, row, col):
        pltpu.make_async_remote_copy(
            src_ref=src, dst_ref=dst, send_sem=ssem, recv_sem=rsem,
            device_id=(row, col), device_id_type=MESH,
        ).start()

    def wait(ref, sem):
        pltpu.make_async_copy(ref, ref, sem).wait()

    loads = [
        pltpu.make_async_copy(src, dst, load_sems.at[at])
        for at, (src, dst) in enumerate(
            [
                (pair_hbm, pair_ref), (gain_tri_hbm, gain_tri), (mask_hbm, mask_ref),
                (w_left_hbm, w_left), (w_right_hbm, w_right), (w_tri_gate_hbm, w_tri_gate),
                (gain_mid_hbm, gain_mid), (w_tri_out_hbm, w_tri_out), (gain_att_hbm, gain_att),
                (w_bias_hbm, w_bias), (w_attend_hbm, w_attend), (w_attend_out_hbm, w_attend_out),
                (gain_trans_hbm, gain_trans), (w_trans_in_hbm, w_trans_in),
                (w_trans_out_hbm, w_trans_out),
            ]
        )
    ]
    for load in loads:
        load.start()

    barrier = pltpu.get_barrier_semaphore()

    def hello(row, col):
        pl.semaphore_signal(barrier, inc=1, device_id=(row, col), device_id_type=MESH)

    @pl.loop(1, ROWS)
    def _(s):
        hello((r + s) & (ROWS - 1), c)

    @pl.loop(1, ZS)
    def _(s):
        hello(r, y * ZS + ((z + s) & (ZS - 1)))

    hello(r, up)
    hello(r, down)

    for load in loads[:5]:
        load.wait()
    work[...] = pair_ref[...].astype(F32).reshape(512, 128)
    pair_t = jnp.concatenate([work[pl.ds(j, 32, stride=16), :] for j in range(16)], 0)
    pair_one_t[...] = pair_t
    normed_t = layer_norm(pair_t, gain_tri[...]).astype(BF16)
    lane = lax.broadcasted_iota(jnp.int32, (32, 512), 1)
    spread = lax.broadcasted_iota(jnp.int32, (32, 512), 0) == (lane & 31)
    mask = dot(mask_ref[...].astype(F32).astype(BF16), spread.astype(F32).astype(BF16), 1, 0)
    lane = lax.broadcasted_iota(jnp.int32, (16, 512), 1)
    own = lax.broadcasted_iota(jnp.int32, (16, 512), 0) == (lane >> 5)
    mask = jnp.sum(jnp.where(own, mask, 0.0), 0, keepdims=True)
    sides = []
    for weight in (w_right, w_left):
        projected = dot(weight[...], normed_t, 0, 1)
        sides.append((mask * jax.nn.sigmoid(projected[:128]) * projected[128:]).reshape(ROWS, 8, 512))
    edge_send[...] = jnp.concatenate(sides, 1).astype(BF16)
    edge_recv[r] = edge_send[r]

    pl.semaphore_wait(barrier, (ROWS - 1) + (ZS - 1) + 2)

    @pl.loop(1, ROWS)
    def _(s):
        to = (r + s) & (ROWS - 1)
        send(edge_send.at[to], edge_recv.at[r], edge_ss.at[to], edge_rs.at[r], to, c)

    for load in loads[5:]:
        load.wait()
    gate_tri[...] = jax.nn.sigmoid(dot(normed_t, w_tri_gate[...], 1, 0))

    @pl.loop(1, ROWS)
    def _(s):
        of = (r + s) & (ROWS - 1)
        wait(edge_recv.at[of], edge_rs.at[of])

    for v in range(4):
        pieces = [
            jnp.concatenate(
                [edge_recv[4 * a + b, :, 128 * v : 128 * v + 128].astype(F32) for a in range(4)], 0
            )
            for b in range(4)
        ]
        for q, piece in enumerate(swap_blocks(pieces, 32)):
            for a in range(4):
                edge_work.at[a][pl.ds(4 * v + q, 16, stride=16), :] = piece[16 * a : 16 * a + 16]
    for a in range(4):
        block = edge_work[a].astype(BF16).reshape(2, 8, 16, 128)
        near_all[z, :, :, 128 * a : 128 * a + 128] = block[0]
        far_all[y, :, :, 128 * a : 128 * a + 128] = block[1]

    class Ring:
        def __init__(self, buf, ss, rs, size, me, to):
            self.buf, self.ss, self.rs, self.size, self.me, self.to = buf, ss, rs, size, me, to
            self.half = buf.shape[1] // 2

        def part(self, block, chunk):
            return self.buf.at[block & (self.size - 1), pl.ds(chunk * self.half, self.half)]

        def send(self, step, chunk, way):
            block = self.me + self.size - step + 1 if way == 0 else self.me + step - 1
            part = self.part(block, chunk)
            row, col = self.to[way]
            send(part, part, self.ss.at[way, step, chunk], self.rs.at[way, step, chunk], row, col)

        def land(self, step, chunk, way):
            block = self.me + self.size - step if way == 0 else self.me + step
            wait(self.part(block, chunk), self.rs.at[way, step, chunk])

        def start(self):
            for chunk in range(2):
                for way in range(2):
                    self.send(1, chunk, way)

        def turn(self, step, chunks=(0, 1)):
            last = self.size // 2
            for chunk in chunks:
                for way in range(2):
                    if step == last and way != chunk:
                        continue
                    self.land(step, chunk, way)
                    if step < last - 1 or (step == last - 1 and way == chunk):
                        self.send(step + 1, chunk, way)

        def sent(self):
            for step in range(1, self.size // 2 + 1):
                for chunk in range(2):
                    for way in range(2):
                        if step < self.size // 2 or way == chunk:
                            wait(self.part(0, 0), self.ss.at[way, step, chunk])

    y_ring = ((r, up), (r, down))
    far_ring = Ring(far_all, far_ss, far_rs, YS, y, y_ring)
    near_ring = Ring(
        near_all, near_ss, near_rs, ZS, z,
        ((r, y * ZS + ((z + 1) & (ZS - 1))), (r, y * ZS + ((z + ZS - 1) & (ZS - 1)))),
    )
    bias_ring = Ring(bias_all, biasy_ss, biasy_rs, YS, y, y_ring)
    far_ring.start()
    near_ring.start()
    far_ring.turn(1)
    near_ring.turn(1, (0,))
    far_ring.turn(2)
    near_ring.turn(1, (1,))
    far_ring.turn(3)
    near_ring.turn(2)
    def reply(slot, piece):
        yy = (y + YS + slot - 3) & (YS - 1)
        tri_send[yy] = piece.astype(BF16).reshape(ZS, 16, 128)
        row = 2 * yy + (z >> 1)
        half = z & 1
        for t in (1, 2, 3):
            zz = (z + t) & (ZS - 1)
            send(
                tri_send.at[yy, zz], tri_recv.at[half, r], tri_ss.at[yy, zz], tri_rs.at[half, r],
                row, y * ZS + zz,
            )

        @pl.when(row != r)
        def _():
            send(
                tri_send.at[yy, z], tri_recv.at[half, r], tri_ss.at[yy, z], tri_rs.at[half, r],
                row, c,
            )

        @pl.when(row == r)
        def _():
            tri_recv[half, r] = tri_send[yy, z]

    def products(slots):
        for ch in range(8):
            rights = jnp.concatenate([near_all[s, ch] for s in range(ZS)], 0)
            lefts = [far_all[(y + YS + s - 3) & (YS - 1), ch] for s in slots]
            found = dot(rights, jnp.concatenate(lefts, 0), 1, 1)
            tri_work[64 * ch : 64 * ch + 64, 0 : 16 * len(lefts)] = found
        return [
            jnp.concatenate([tri_work[pl.ds(8 * g + m, 8, stride=64), :] for g in range(8)], 0)
            for m in range(8)
        ]

    tri_work[...] = jnp.zeros_like(tri_work)
    pieces = swap_blocks(products(range(7)), 16)
    for slot in (2, 4, 1, 5, 0, 6, 3):
        reply(slot, pieces[slot])
    far_ring.turn(4)
    pieces = products([7])
    lane = lax.broadcasted_iota(jnp.int32, pieces[0].shape, 1) >> 4
    merged = pieces[0]
    for m in range(1, 8):
        merged = jnp.where(lane == m, pltpu.roll(pieces[m], 16 * m, 1), merged)
    reply(7, merged)

    @pl.loop(0, ROWS)
    def _(s):
        for half in range(2):

            @pl.when(jnp.logical_or(s != r, z != 2 * (r & 1) + half))
            def _():
                wait(tri_recv.at[half, s], tri_rs.at[half, s])

    tri_t = jnp.concatenate(
        [
            tri_recv[half].astype(F32)[:, 8 * g : 8 * g + 8].reshape(128, 128)
            for half in range(2)
            for g in range(2)
        ],
        1,
    )
    gain_col = jnp.broadcast_to(gain_mid[...], (128, 128)).T
    tri_normed = layer_norm(tri_t, jnp.concatenate([gain_col] * 4, 1), 0).astype(BF16)
    update = dot(tri_normed, w_tri_out[...], 0, 0)
    update = jnp.concatenate(
        [
            update[256 * half + 16 * j : 256 * half + 16 * j + 16]
            for j in range(16)
            for half in range(2)
        ],
        0,
    )
    pair_t = (pair_one_t[...] + gate_tri[...] * update).astype(BF16).astype(F32)
    pair_one_t[...] = pair_t

    normed_two = layer_norm(pair_t, gain_att[...]).astype(BF16)
    bias_t = dot(w_bias[...], normed_two, 1, 1)
    sub = lax.broadcasted_iota(jnp.int32, (16, 128), 0)
    for h in range(HEADS):
        base = jnp.zeros((16, 128), F32)
        for v in range(4):
            base = jnp.where(
                sub == v,
                jnp.broadcast_to(bias_t[h : h + 1, 128 * v : 128 * v + 128], (16, 128)),
                base,
            )
        for g in range(4):
            row = jnp.broadcast_to(mask[:, 128 * g : 128 * g + 128], (16, 128))
            bias_send[4 * h + g] = jnp.where(sub == 4, row, base).astype(BF16)
    bias_recv[r] = bias_send[r]

    @pl.loop(1, ROWS)
    def _(s):
        to = (r + s) & (ROWS - 1)
        send(bias_send.at[to], bias_recv.at[r], bias_ss.at[to], bias_rs.at[r], to, c)

    projected = dot(w_attend[...], normed_two, 0, 1)
    for h in range(HEADS):
        for part in range(3):
            rows = projected[128 * part + 32 * h : 128 * part + 32 * h + 32]
            if part == 0:
                rows = rows * (LOG2E / math.sqrt(HEAD_DIM))
            for g in range(4):
                qkv_send[4 * h + g, 32 * part : 32 * part + 32, :] = rows[
                    :, 128 * g : 128 * g + 128
                ].astype(BF16)
    qkv_recv[r] = qkv_send[r]

    @pl.loop(1, ROWS)
    def _(s):
        to = (r + s) & (ROWS - 1)
        send(qkv_send.at[to], qkv_recv.at[r], qkv_ss.at[to], qkv_rs.at[r], to, c)

    gate_att[...] = jax.nn.sigmoid(projected[384:])

    @pl.loop(1, ROWS)
    def _(s):
        of = (r + s) & (ROWS - 1)
        wait(bias_recv.at[of], bias_rs.at[of])

    pieces = [
        jnp.concatenate([bias_recv[4 * a + b].astype(F32) for a in range(4)], 0) for b in range(4)
    ]
    for q, piece in enumerate(swap_blocks(pieces, 32)):
        for a in range(4):
            for v in range(4):
                bias_work[a, 4 * v + q : 4 * v + q + 1, :] = piece[16 * a + v : 16 * a + v + 1]
            mask_cols[q, 0:1, 128 * a : 128 * a + 128] = piece[16 * a + 4 : 16 * a + 5]
    for a in range(4):
        bias_all[y, z, :, 128 * a : 128 * a + 128] = bias_work[a].astype(BF16)

    @pl.loop(1, ZS)
    def _(s):
        to = (z + s) & (ZS - 1)
        send(bias_all.at[y, z], bias_all.at[y, z], biasz_ss.at[to], biasz_rs.at[z], r, y * ZS + to)

    @pl.loop(1, ZS)
    def _(s):
        of = (z + s) & (ZS - 1)
        wait(bias_all.at[y, of], biasz_rs.at[of])

    bias_ring.start()
    bias_ring.turn(1)

    @pl.loop(1, ROWS)
    def _(s):
        of = (r + s) & (ROWS - 1)
        wait(qkv_recv.at[of], qkv_rs.at[of])

    bias_ring.turn(2)
    tail = (lax.broadcasted_iota(jnp.int32, (16, 512), 0) == 0).astype(BF16)
    for q in range(4):
        value_buf[q, 32:48, :] = tail
    for a in range(4):
        pieces = [qkv_recv[4 * a + b].astype(F32) for b in range(4)]
        for q, piece in enumerate(swap_blocks(pieces, 32)):
            piece = piece.astype(BF16)
            query_buf[q, a] = piece[:32]
            key_buf[q, :, 128 * a : 128 * a + 128] = piece[32:64]
            value_buf[q, 0:32, 128 * a : 128 * a + 128] = piece[64:]

    side = 1 - 2 * (y & 1)
    for step, apart in enumerate((0, -side, side, 2)):
        if step in (1, 3):
            bias_ring.turn(3 + step // 2)
        a = ((y >> 1) + 4 + apart) & 3
        bias_full[...] = bias_all[pl.ds(2 * a, 2)].astype(F32).reshape(128, 512) * LOG2E
        pieces = []
        for q in range(4):
            scores = dot(query_buf[q, a], key_buf[q], 0, 0) + bias_full[...]
            scores = jnp.where(mask_cols[q, 0:1, :] > 0.5, scores, MASKED)
            weight = jnp.exp2(scores - jnp.max(scores, 1, keepdims=True)).astype(BF16)
            total = dot(value_buf[q], weight, 1, 1)
            pieces.append(total[:32] / total[32:33])
        for b, piece in enumerate(swap_blocks(pieces, 32)):
            at = 4 * a + b
            att_send[at] = piece.astype(BF16)

            @pl.when(r != at)
            def _():
                send(att_send.at[at], att_recv.at[r], att_ss.at[at], att_rs.at[r], at, c)

            @pl.when(r == at)
            def _():
                att_recv[r] = att_send[at]

    @pl.loop(1, ROWS)
    def _(s):
        of = (r + s) & (ROWS - 1)
        wait(att_recv.at[of], att_rs.at[of])

    attended = jnp.concatenate(
        [
            jnp.concatenate([att_recv[4 * h + g].astype(F32) for g in range(4)], 1)
            for h in range(HEADS)
        ],
        0,
    )
    gated = (gate_att[...] * attended).astype(BF16)
    pair_two = (pair_one_t[...] + dot(gated, w_attend_out[...], 0, 0)).astype(BF16).astype(F32)
    normed_three = layer_norm(pair_two, gain_trans[...]).astype(BF16)
    for part in range(4):
        rows = slice(128 * part, 128 * part + 128)
        expanded = dot(normed_three[rows], w_trans_in[...], 1, 0)
        hidden = (jax.nn.silu(expanded[:, :512]) * expanded[:, 512:]).astype(BF16)
        work[rows, :] = pair_two[rows] + dot(hidden, w_trans_out[...], 1, 0)
    for i in range(32):
        out_ref[i] = work[pl.ds(i, 16, stride=32), :].astype(BF16)

    @pl.loop(1, ROWS)
    def _(s):
        to = (r + s) & (ROWS - 1)
        wait(edge_send.at[to], edge_ss.at[to])
        wait(bias_send.at[to], bias_ss.at[to])
        wait(qkv_send.at[to], qkv_ss.at[to])
        wait(att_send.at[to], att_ss.at[to])

    @pl.loop(1, ZS)
    def _(s):
        to = (z + s) & (ZS - 1)
        wait(bias_all.at[0, 0], biasz_ss.at[to])

    @pl.loop(0, YS)
    def _(s):
        for t in range(ZS):

            @pl.when(jnp.logical_or(2 * s + (z >> 1) != r, z != t))
            def _():
                wait(tri_send.at[s, t], tri_ss.at[s, t])

    for each in (far_ring, near_ring, bias_ring):
        each.sent()


def per_device(
    pair, pair_mask, gain_tri, w_left, w_right, w_tri_gate, gain_mid, w_tri_out, gain_att, w_attend,
    w_bias, w_attend_out, gain_trans, w_trans_in, w_trans_out,
):
    vmem = pl.BlockSpec(memory_space=pltpu.VMEM)
    dma = pltpu.SemaphoreType.DMA
    row = lambda gain: gain.reshape(1, 128)
    return pl.pallas_call(
        kernel,
        out_shape=pltpu.VMEM((32, 16, 128), BF16),
        in_specs=[pl.BlockSpec(memory_space=pltpu.HBM)] * 15,
        out_specs=vmem,
        scratch_shapes=[
            pltpu.VMEM((32, 16, 128), BF16),
            pltpu.VMEM((16, 32), jnp.int32),
            pltpu.VMEM((1, 128), F32),
            pltpu.VMEM((128, 256), BF16),
            pltpu.VMEM((128, 256), BF16),
            pltpu.VMEM((128, 128), BF16),
            pltpu.VMEM((1, 128), F32),
            pltpu.VMEM((128, 128), BF16),
            pltpu.VMEM((1, 128), F32),
            pltpu.VMEM((128, 512), BF16),
            pltpu.VMEM((4, 128), BF16),
            pltpu.VMEM((128, 128), BF16),
            pltpu.VMEM((1, 128), F32),
            pltpu.VMEM((128, 1024), BF16),
            pltpu.VMEM((512, 128), BF16),
            dma((15,)),
            pltpu.VMEM((512, 128), F32),
            pltpu.VMEM((16, 16, 512), BF16),
            pltpu.VMEM((16, 16, 512), BF16),
            pltpu.VMEM((4, 256, 128), F32),
            pltpu.VMEM((ZS, 8, 16, 512), BF16),
            pltpu.VMEM((YS, 8, 16, 512), BF16),
            pltpu.VMEM((512, 128), F32),
            pltpu.VMEM((512, 128), F32),
            pltpu.VMEM((YS, ZS, 16, 128), BF16),
            pltpu.VMEM((2, 16, 16, 128), BF16),
            pltpu.VMEM((16, 16, 128), BF16),
            pltpu.VMEM((16, 16, 128), BF16),
            pltpu.VMEM((4, 16, 128), F32),
            pltpu.VMEM((YS, ZS, 16, 512), BF16),
            pltpu.VMEM((128, 512), F32),
            pltpu.VMEM((4, 8, 512), F32),
            pltpu.VMEM((512, 128), F32),
            pltpu.VMEM((128, 512), F32),
            pltpu.VMEM((16, 96, 128), BF16),
            pltpu.VMEM((16, 96, 128), BF16),
            pltpu.VMEM((4, 4, 32, 128), BF16),
            pltpu.VMEM((4, 32, 512), BF16),
            pltpu.VMEM((4, 48, 512), BF16),
            pltpu.VMEM((16, 32, 128), BF16),
            pltpu.VMEM((16, 32, 128), BF16),
            dma((16,)), dma((16,)),
            dma((2, 5, 2)), dma((2, 5, 2)),
            dma((2, 5, 2)), dma((2, 5, 2)),
            dma((YS, ZS)), dma((2, 16)),
            dma((16,)), dma((16,)),
            dma((ZS,)), dma((ZS,)),
            dma((2, 5, 2)), dma((2, 5, 2)),
            dma((16,)), dma((16,)),
            dma((16,)), dma((16,)),
        ],
        compiler_params=pltpu.CompilerParams(
            collective_id=0, has_side_effects=True, vmem_limit_bytes=VMEM_LIMIT
        ),
    )(
        pair, pair_mask.T, row(gain_tri), w_left, w_right, w_tri_gate, row(gain_mid),
        w_tri_out, row(gain_att), w_attend, w_bias.T, w_attend_out, row(gain_trans), w_trans_in,
        w_trans_out,
    )


def solution(mesh):
    in_specs = (P("row", "col", None), P("row", "col")) + (P(),) * 13
    return jax.shard_map(
        per_device, mesh=mesh, in_specs=in_specs, out_specs=P("row", "col", None), check_vma=False
    )
```

```python
import functools
import math

import jax
import jax.numpy as jnp
from jax import lax
from jax.experimental import pallas as pl
from jax.experimental.pallas import tpu as pltpu
from jax.sharding import PartitionSpec as P

HEADS = 4
HEAD_DIM = 32
EPS = 1e-05
MASKED = -1000000000.0
LOG2E = math.log2(math.e)
ROWS = 16
YS = 8
ZS = 4
VMEM_LIMIT = 63 * 1024 * 1024
MESH = pl.DeviceIdType.MESH
F32 = jnp.float32
BF16 = jnp.bfloat16


def dot(lhs, rhs, lhs_dim, rhs_dim):
    return lax.dot_general(
        lhs, rhs, (((lhs_dim,), (rhs_dim,)), ((), ())), preferred_element_type=F32
    )


def layer_norm(inputs, gain_vec, axis=-1):
    center = inputs - jnp.mean(inputs, axis, keepdims=True)
    spread = jnp.mean(center * center, axis, keepdims=True)
    return center * lax.rsqrt(spread + EPS) * gain_vec


def swap_blocks(arrays, width):
    arrays = list(arrays)
    lane = lax.broadcasted_iota(jnp.int32, arrays[0].shape, 1)
    step = 1
    while step < len(arrays):
        shift = width * step
        odd = (lane & shift) != 0
        fresh = list(arrays)
        for low in range(len(arrays)):
            if low & step == 0:
                high = low | step
                fresh[low] = jnp.where(odd, pltpu.roll(arrays[high], shift, 1), arrays[low])
                fresh[high] = jnp.where(odd, arrays[high], pltpu.roll(arrays[low], 128 - shift, 1))
        arrays = fresh
        step *= 2
    return arrays


def kernel(
    pair_hbm, mask_hbm, gain_tri_hbm, w_left_hbm, w_right_hbm, w_tri_gate_hbm, gain_mid_hbm,
    w_tri_out_hbm, gain_att_hbm, w_attend_hbm, w_bias_hbm, w_attend_out_hbm, gain_trans_hbm,
    w_trans_in_hbm, w_trans_out_hbm,
    out_ref,
    pair_ref, mask_ref, gain_tri, w_left, w_right, w_tri_gate, gain_mid, w_tri_out, gain_att,
    w_attend, w_bias, w_attend_out, gain_trans, w_trans_in, w_trans_out, load_sems,
    work, edge_send, edge_recv, edge_work, near_all, far_all, gate_tri, tri_work, tri_send,
    tri_recv, bias_send, bias_recv, bias_work, bias_all, bias_full, mask_cols, pair_one_t, gate_att,
    qkv_send, qkv_recv, query_buf, key_buf, value_buf, normed_buf, att_work, att_send, att_recv,
    edge_ss, edge_rs, near_ss, near_rs, far_ss, far_rs, tri_ss, tri_rs, bias_ss, bias_rs,
    biasz_ss, biasz_rs, biasy_ss, biasy_rs, qkv_ss, qkv_rs, att_ss, att_rs,
):
    r = lax.axis_index("row")
    c = lax.axis_index("col")
    y = c >> 2
    z = c & (ZS - 1)
    up = ((y + 1) & (YS - 1)) * ZS + z
    down = ((y + YS - 1) & (YS - 1)) * ZS + z

    def send(src, dst, ssem, rsem, row, col):
        pltpu.make_async_remote_copy(
            src_ref=src, dst_ref=dst, send_sem=ssem, recv_sem=rsem,
            device_id=(row, col), device_id_type=MESH,
        ).start()

    def wait(ref, sem):
        pltpu.make_async_copy(ref, ref, sem).wait()

    loads = [
        pltpu.make_async_copy(src, dst, load_sems.at[at])
        for at, (src, dst) in enumerate(
            [
                (pair_hbm, pair_ref), (gain_tri_hbm, gain_tri), (mask_hbm, mask_ref),
                (w_left_hbm, w_left), (w_right_hbm, w_right), (w_tri_gate_hbm, w_tri_gate),
                (gain_mid_hbm, gain_mid), (w_tri_out_hbm, w_tri_out), (gain_att_hbm, gain_att),
                (w_bias_hbm, w_bias), (w_attend_hbm, w_attend), (w_attend_out_hbm, w_attend_out),
                (gain_trans_hbm, gain_trans), (w_trans_in_hbm, w_trans_in),
                (w_trans_out_hbm, w_trans_out),
            ]
        )
    ]
    for load in loads:
        load.start()

    barrier = pltpu.get_barrier_semaphore()

    def hello(row, col):
        pl.semaphore_signal(barrier, inc=1, device_id=(row, col), device_id_type=MESH)

    @pl.loop(1, ROWS)
    def _(s):
        hello((r + s) & (ROWS - 1), c)

    @pl.loop(1, ZS)
    def _(s):
        hello(r, y * ZS + ((z + s) & (ZS - 1)))

    hello(r, up)
    hello(r, down)

    for load in loads[:5]:
        load.wait()
    work[...] = pair_ref[...].astype(F32).reshape(512, 128)
    pair_t = jnp.concatenate([work[pl.ds(j, 32, stride=16), :] for j in range(16)], 0)
    pair_one_t[...] = pair_t
    normed_t = layer_norm(pair_t, gain_tri[...]).astype(BF16)
    lane = lax.broadcasted_iota(jnp.int32, (32, 512), 1)
    spread = lax.broadcasted_iota(jnp.int32, (32, 512), 0) == (lane & 31)
    mask = dot(mask_ref[...].astype(F32).astype(BF16), spread.astype(F32).astype(BF16), 1, 0)
    lane = lax.broadcasted_iota(jnp.int32, (16, 512), 1)
    own = lax.broadcasted_iota(jnp.int32, (16, 512), 0) == (lane >> 5)
    mask = jnp.sum(jnp.where(own, mask, 0.0), 0, keepdims=True)
    sides = []
    for weight in (w_right, w_left):
        projected = dot(weight[...], normed_t, 0, 1)
        sides.append((mask * jax.nn.sigmoid(projected[:128]) * projected[128:]).reshape(ROWS, 8, 512))
    edge_send[...] = jnp.concatenate(sides, 1).astype(BF16)
    edge_recv[r] = edge_send[r]

    pl.semaphore_wait(barrier, (ROWS - 1) + (ZS - 1) + 2)

    @pl.loop(1, ROWS)
    def _(s):
        to = (r + s) & (ROWS - 1)
        send(edge_send.at[to], edge_recv.at[r], edge_ss.at[to], edge_rs.at[r], to, c)

    for load in loads[5:]:
        load.wait()
    gate_tri[...] = jax.nn.sigmoid(dot(normed_t, w_tri_gate[...], 1, 0))

    @pl.loop(1, ROWS)
    def _(s):
        of = (r + s) & (ROWS - 1)
        wait(edge_recv.at[of], edge_rs.at[of])

    for v in range(4):
        pieces = [
            jnp.concatenate(
                [edge_recv[4 * a + b, :, 128 * v : 128 * v + 128].astype(F32) for a in range(4)], 0
            )
            for b in range(4)
        ]
        for q, piece in enumerate(swap_blocks(pieces, 32)):
            for a in range(4):
                edge_work.at[a][pl.ds(4 * v + q, 16, stride=16), :] = piece[16 * a : 16 * a + 16]
    for a in range(4):
        block = edge_work[a].astype(BF16).reshape(2, 8, 16, 128)
        near_all[z, :, :, 128 * a : 128 * a + 128] = block[0]
        far_all[y, :, :, 128 * a : 128 * a + 128] = block[1]

    class Ring:
        def __init__(self, buf, ss, rs, size, me, to):
            self.buf, self.ss, self.rs, self.size, self.me, self.to = buf, ss, rs, size, me, to
            self.half = buf.shape[1] // 2

        def part(self, block, chunk):
            return self.buf.at[block & (self.size - 1), pl.ds(chunk * self.half, self.half)]

        def send(self, step, chunk, way):
            block = self.me + self.size - step + 1 if way == 0 else self.me + step - 1
            part = self.part(block, chunk)
            row, col = self.to[way]
            send(part, part, self.ss.at[way, step, chunk], self.rs.at[way, step, chunk], row, col)

        def land(self, step, chunk, way):
            block = self.me + self.size - step if way == 0 else self.me + step
            wait(self.part(block, chunk), self.rs.at[way, step, chunk])

        def start(self):
            for chunk in range(2):
                for way in range(2):
                    self.send(1, chunk, way)

        def turn(self, step, chunks=(0, 1)):
            last = self.size // 2
            for chunk in chunks:
                for way in range(2):
                    if step == last and way != chunk:
                        continue
                    self.land(step, chunk, way)
                    if step < last - 1 or (step == last - 1 and way == chunk):
                        self.send(step + 1, chunk, way)

        def sent(self):
            for step in range(1, self.size // 2 + 1):
                for chunk in range(2):
                    for way in range(2):
                        if step < self.size // 2 or way == chunk:
                            wait(self.part(0, 0), self.ss.at[way, step, chunk])

    y_ring = ((r, up), (r, down))
    far_ring = Ring(far_all, far_ss, far_rs, YS, y, y_ring)
    near_ring = Ring(
        near_all, near_ss, near_rs, ZS, z,
        ((r, y * ZS + ((z + 1) & (ZS - 1))), (r, y * ZS + ((z + ZS - 1) & (ZS - 1)))),
    )
    bias_ring = Ring(bias_all, biasy_ss, biasy_rs, YS, y, y_ring)
    far_ring.start()
    near_ring.start()
    far_ring.turn(1)
    near_ring.turn(1, (0,))
    far_ring.turn(2)
    near_ring.turn(1, (1,))
    far_ring.turn(3)
    near_ring.turn(2)
    def reply(slot, piece):
        yy = (y + YS + slot - 3) & (YS - 1)
        tri_send[yy] = piece.astype(BF16).reshape(ZS, 16, 128)
        row = 2 * yy + (z >> 1)
        half = z & 1
        for t in (1, 2, 3):
            zz = (z + t) & (ZS - 1)
            send(
                tri_send.at[yy, zz], tri_recv.at[half, r], tri_ss.at[yy, zz], tri_rs.at[half, r],
                row, y * ZS + zz,
            )

        @pl.when(row != r)
        def _():
            send(
                tri_send.at[yy, z], tri_recv.at[half, r], tri_ss.at[yy, z], tri_rs.at[half, r],
                row, c,
            )

        @pl.when(row == r)
        def _():
            tri_recv[half, r] = tri_send[yy, z]

    def products(slots):
        for ch in range(8):
            rights = jnp.concatenate([near_all[s, ch] for s in range(ZS)], 0)
            lefts = [far_all[(y + YS + s - 3) & (YS - 1), ch] for s in slots]
            found = dot(rights, jnp.concatenate(lefts, 0), 1, 1)
            tri_work[64 * ch : 64 * ch + 64, 0 : 16 * len(lefts)] = found
        return [
            jnp.concatenate([tri_work[pl.ds(8 * g + m, 8, stride=64), :] for g in range(8)], 0)
            for m in range(8)
        ]

    tri_work[...] = jnp.zeros_like(tri_work)
    pieces = swap_blocks(products(range(7)), 16)
    for slot in (2, 4, 1, 5, 0, 6, 3):
        reply(slot, pieces[slot])
    far_ring.turn(4)
    pieces = products([7])
    lane = lax.broadcasted_iota(jnp.int32, pieces[0].shape, 1) >> 4
    merged = pieces[0]
    for m in range(1, 8):
        merged = jnp.where(lane == m, pltpu.roll(pieces[m], 16 * m, 1), merged)
    reply(7, merged)

    @pl.loop(0, ROWS)
    def _(s):
        for half in range(2):

            @pl.when(jnp.logical_or(s != r, z != 2 * (r & 1) + half))
            def _():
                wait(tri_recv.at[half, s], tri_rs.at[half, s])

    tri_t = jnp.concatenate(
        [
            tri_recv[half].astype(F32)[:, 8 * g : 8 * g + 8].reshape(128, 128)
            for half in range(2)
            for g in range(2)
        ],
        1,
    )
    gain_col = jnp.broadcast_to(gain_mid[...], (128, 128)).T
    tri_normed = layer_norm(tri_t, jnp.concatenate([gain_col] * 4, 1), 0).astype(BF16)
    update = dot(tri_normed, w_tri_out[...], 0, 0)
    update = jnp.concatenate(
        [
            update[256 * half + 16 * j : 256 * half + 16 * j + 16]
            for j in range(16)
            for half in range(2)
        ],
        0,
    )
    pair_t = (pair_one_t[...] + gate_tri[...] * update).astype(BF16).astype(F32)
    pair_one_t[...] = pair_t

    normed_two = layer_norm(pair_t, gain_att[...]).astype(BF16)
    bias_t = dot(w_bias[...], normed_two, 1, 1)
    sub = lax.broadcasted_iota(jnp.int32, (16, 128), 0)
    for h in range(HEADS):
        base = jnp.zeros((16, 128), F32)
        for v in range(4):
            base = jnp.where(
                sub == v,
                jnp.broadcast_to(bias_t[h : h + 1, 128 * v : 128 * v + 128], (16, 128)),
                base,
            )
        for g in range(4):
            row = jnp.broadcast_to(mask[:, 128 * g : 128 * g + 128], (16, 128))
            bias_send[4 * h + g] = jnp.where(sub == 4, row, base).astype(BF16)
    bias_recv[r] = bias_send[r]

    @pl.loop(1, ROWS)
    def _(s):
        to = (r + s) & (ROWS - 1)
        send(bias_send.at[to], bias_recv.at[r], bias_ss.at[to], bias_rs.at[r], to, c)

    projected = dot(w_attend[...], normed_two, 0, 1)
    for h in range(HEADS):
        for part in range(3):
            rows = projected[128 * part + 32 * h : 128 * part + 32 * h + 32]
            if part == 0:
                rows = rows * (LOG2E / math.sqrt(HEAD_DIM))
            for g in range(4):
                qkv_send[4 * h + g, 32 * part : 32 * part + 32, :] = rows[
                    :, 128 * g : 128 * g + 128
                ].astype(BF16)
    qkv_recv[r] = qkv_send[r]

    @pl.loop(1, ROWS)
    def _(s):
        to = (r + s) & (ROWS - 1)
        send(qkv_send.at[to], qkv_recv.at[r], qkv_ss.at[to], qkv_rs.at[r], to, c)

    gate_att[...] = jax.nn.sigmoid(projected[384:])

    @pl.loop(1, ROWS)
    def _(s):
        of = (r + s) & (ROWS - 1)
        wait(bias_recv.at[of], bias_rs.at[of])

    pieces = [
        jnp.concatenate([bias_recv[4 * a + b].astype(F32) for a in range(4)], 0) for b in range(4)
    ]
    for q, piece in enumerate(swap_blocks(pieces, 32)):
        for a in range(4):
            for v in range(4):
                bias_work[a, 4 * v + q : 4 * v + q + 1, :] = piece[16 * a + v : 16 * a + v + 1]
            mask_cols[q, 0:1, 128 * a : 128 * a + 128] = piece[16 * a + 4 : 16 * a + 5]
    for a in range(4):
        bias_all[y, z, :, 128 * a : 128 * a + 128] = bias_work[a].astype(BF16)

    @pl.loop(1, ZS)
    def _(s):
        to = (z + s) & (ZS - 1)
        send(bias_all.at[y, z], bias_all.at[y, z], biasz_ss.at[to], biasz_rs.at[z], r, y * ZS + to)

    @pl.loop(1, ZS)
    def _(s):
        of = (z + s) & (ZS - 1)
        wait(bias_all.at[y, of], biasz_rs.at[of])

    bias_ring.start()
    bias_ring.turn(1)

    @pl.loop(1, ROWS)
    def _(s):
        of = (r + s) & (ROWS - 1)
        wait(qkv_recv.at[of], qkv_rs.at[of])

    bias_ring.turn(2)
    tail = (lax.broadcasted_iota(jnp.int32, (16, 512), 0) == 0).astype(BF16)
    for q in range(4):
        value_buf[q, 32:48, :] = tail
    for a in range(4):
        pieces = [qkv_recv[4 * a + b].astype(F32) for b in range(4)]
        for q, piece in enumerate(swap_blocks(pieces, 32)):
            piece = piece.astype(BF16)
            query_buf[q, a] = piece[:32]
            key_buf[q, :, 128 * a : 128 * a + 128] = piece[32:64]
            value_buf[q, 0:32, 128 * a : 128 * a + 128] = piece[64:]

    side = 1 - 2 * (y & 1)
    for step, apart in enumerate((0, -side, side, 2)):
        if step in (1, 3):
            bias_ring.turn(3 + step // 2)
        a = ((y >> 1) + 4 + apart) & 3
        bias_full[...] = bias_all[pl.ds(2 * a, 2)].astype(F32).reshape(128, 512) * LOG2E

        @pl.loop(0, 4)
        def _(q):
            scores = dot(query_buf[q, a], key_buf[q], 0, 0) + bias_full[...]
            scores = jnp.where(mask_cols[q, 0:1, :] > 0.5, scores, MASKED)
            weight = jnp.exp2(scores - jnp.max(scores, 1, keepdims=True)).astype(BF16)
            total = dot(value_buf[q], weight, 1, 1)
            att_work[q] = total[:32] / total[32:33]

        for b, piece in enumerate(swap_blocks([att_work[q] for q in range(4)], 32)):
            at = 4 * a + b
            att_send[at] = piece.astype(BF16)

            @pl.when(r != at)
            def _():
                send(att_send.at[at], att_recv.at[r], att_ss.at[at], att_rs.at[r], at, c)

            @pl.when(r == at)
            def _():
                att_recv[r] = att_send[at]

    @pl.loop(1, ROWS)
    def _(s):
        of = (r + s) & (ROWS - 1)
        wait(att_recv.at[of], att_rs.at[of])

    attended = jnp.concatenate(
        [
            jnp.concatenate([att_recv[4 * h + g].astype(F32) for g in range(4)], 1)
            for h in range(HEADS)
        ],
        0,
    )
    gated = (gate_att[...] * attended).astype(BF16)
    pair_two = (pair_one_t[...] + dot(gated, w_attend_out[...], 0, 0)).astype(BF16).astype(F32)
    normed_three = layer_norm(pair_two, gain_trans[...]).astype(BF16)
    work[...] = pair_two
    normed_buf[...] = normed_three

    @pl.loop(0, 4)
    def _(part):
        rows = pl.ds(pl.multiple_of(128 * part, 128), 128)
        expanded = dot(normed_buf[rows, :], w_trans_in[...], 1, 0)
        hidden = (jax.nn.silu(expanded[:, :512]) * expanded[:, 512:]).astype(BF16)
        work[rows, :] = work[rows, :] + dot(hidden, w_trans_out[...], 1, 0)

    for i in range(32):
        out_ref[i] = work[pl.ds(i, 16, stride=32), :].astype(BF16)

    @pl.loop(1, ROWS)
    def _(s):
        to = (r + s) & (ROWS - 1)
        wait(edge_send.at[to], edge_ss.at[to])
        wait(bias_send.at[to], bias_ss.at[to])
        wait(qkv_send.at[to], qkv_ss.at[to])
        wait(att_send.at[to], att_ss.at[to])

    @pl.loop(1, ZS)
    def _(s):
        to = (z + s) & (ZS - 1)
        wait(bias_all.at[0, 0], biasz_ss.at[to])

    @pl.loop(0, YS)
    def _(s):
        for t in range(ZS):

            @pl.when(jnp.logical_or(2 * s + (z >> 1) != r, z != t))
            def _():
                wait(tri_send.at[s, t], tri_ss.at[s, t])

    for each in (far_ring, near_ring, bias_ring):
        each.sent()


def per_device(
    pair, pair_mask, gain_tri, w_left, w_right, w_tri_gate, gain_mid, w_tri_out, gain_att, w_attend,
    w_bias, w_attend_out, gain_trans, w_trans_in, w_trans_out,
):
    vmem = pl.BlockSpec(memory_space=pltpu.VMEM)
    dma = pltpu.SemaphoreType.DMA
    row = lambda gain: gain.reshape(1, 128)
    return pl.pallas_call(
        kernel,
        out_shape=pltpu.VMEM((32, 16, 128), BF16),
        in_specs=[pl.BlockSpec(memory_space=pltpu.HBM)] * 15,
        out_specs=vmem,
        scratch_shapes=[
            pltpu.VMEM((32, 16, 128), BF16),
            pltpu.VMEM((16, 32), jnp.int32),
            pltpu.VMEM((1, 128), F32),
            pltpu.VMEM((128, 256), BF16),
            pltpu.VMEM((128, 256), BF16),
            pltpu.VMEM((128, 128), BF16),
            pltpu.VMEM((1, 128), F32),
            pltpu.VMEM((128, 128), BF16),
            pltpu.VMEM((1, 128), F32),
            pltpu.VMEM((128, 512), BF16),
            pltpu.VMEM((4, 128), BF16),
            pltpu.VMEM((128, 128), BF16),
            pltpu.VMEM((1, 128), F32),
            pltpu.VMEM((128, 1024), BF16),
            pltpu.VMEM((512, 128), BF16),
            dma((15,)),
            pltpu.VMEM((512, 128), F32),
            pltpu.VMEM((16, 16, 512), BF16),
            pltpu.VMEM((16, 16, 512), BF16),
            pltpu.VMEM((4, 256, 128), F32),
            pltpu.VMEM((ZS, 8, 16, 512), BF16),
            pltpu.VMEM((YS, 8, 16, 512), BF16),
            pltpu.VMEM((512, 128), F32),
            pltpu.VMEM((512, 128), F32),
            pltpu.VMEM((YS, ZS, 16, 128), BF16),
            pltpu.VMEM((2, 16, 16, 128), BF16),
            pltpu.VMEM((16, 16, 128), BF16),
            pltpu.VMEM((16, 16, 128), BF16),
            pltpu.VMEM((4, 16, 128), F32),
            pltpu.VMEM((YS, ZS, 16, 512), BF16),
            pltpu.VMEM((128, 512), F32),
            pltpu.VMEM((4, 8, 512), F32),
            pltpu.VMEM((512, 128), F32),
            pltpu.VMEM((128, 512), F32),
            pltpu.VMEM((16, 96, 128), BF16),
            pltpu.VMEM((16, 96, 128), BF16),
            pltpu.VMEM((4, 4, 32, 128), BF16),
            pltpu.VMEM((4, 32, 512), BF16),
            pltpu.VMEM((4, 48, 512), BF16),
            pltpu.VMEM((512, 128), BF16),
            pltpu.VMEM((4, 32, 128), F32),
            pltpu.VMEM((16, 32, 128), BF16),
            pltpu.VMEM((16, 32, 128), BF16),
            dma((16,)), dma((16,)),
            dma((2, 5, 2)), dma((2, 5, 2)),
            dma((2, 5, 2)), dma((2, 5, 2)),
            dma((YS, ZS)), dma((2, 16)),
            dma((16,)), dma((16,)),
            dma((ZS,)), dma((ZS,)),
            dma((2, 5, 2)), dma((2, 5, 2)),
            dma((16,)), dma((16,)),
            dma((16,)), dma((16,)),
        ],
        compiler_params=pltpu.CompilerParams(
            collective_id=0, has_side_effects=True, vmem_limit_bytes=VMEM_LIMIT
        ),
    )(
        pair, pair_mask.T, row(gain_tri), w_left, w_right, w_tri_gate, row(gain_mid),
        w_tri_out, row(gain_att), w_attend, w_bias.T, w_attend_out, row(gain_trans), w_trans_in,
        w_trans_out,
    )


def solution(mesh):
    in_specs = (P("row", "col", None), P("row", "col")) + (P(),) * 13
    return jax.shard_map(
        per_device, mesh=mesh, in_specs=in_specs, out_specs=P("row", "col", None), check_vma=False
    )
```

```python
import functools
import math

import jax
import jax.numpy as jnp
from jax import lax
from jax.experimental import pallas as pl
from jax.experimental.pallas import tpu as pltpu
from jax.sharding import PartitionSpec as P

HEADS = 4
HEAD_DIM = 32
EPS = 1e-05
MASKED = -1000000000.0
LOG2E = math.log2(math.e)
ROWS = 16
YS = 8
ZS = 4
VMEM_LIMIT = 63 * 1024 * 1024
MESH = pl.DeviceIdType.MESH
F32 = jnp.float32
BF16 = jnp.bfloat16


def dot(lhs, rhs, lhs_dim, rhs_dim):
    return lax.dot_general(
        lhs, rhs, (((lhs_dim,), (rhs_dim,)), ((), ())), preferred_element_type=F32
    )


def layer_norm(inputs, gain_vec, axis=-1):
    center = inputs - jnp.mean(inputs, axis, keepdims=True)
    spread = jnp.mean(center * center, axis, keepdims=True)
    return center * lax.rsqrt(spread + EPS) * gain_vec


def swap_blocks(arrays, width):
    arrays = list(arrays)
    lane = lax.broadcasted_iota(jnp.int32, arrays[0].shape, 1)
    step = 1
    while step < len(arrays):
        shift = width * step
        odd = (lane & shift) != 0
        fresh = list(arrays)
        for low in range(len(arrays)):
            if low & step == 0:
                high = low | step
                fresh[low] = jnp.where(odd, pltpu.roll(arrays[high], shift, 1), arrays[low])
                fresh[high] = jnp.where(odd, arrays[high], pltpu.roll(arrays[low], 128 - shift, 1))
        arrays = fresh
        step *= 2
    return arrays


def kernel(
    pair_hbm, mask_hbm, gain_tri_hbm, w_left_hbm, w_right_hbm, w_tri_gate_hbm, gain_mid_hbm,
    w_tri_out_hbm, gain_att_hbm, w_attend_hbm, w_bias_hbm, w_attend_out_hbm, gain_trans_hbm,
    w_trans_in_hbm, w_trans_out_hbm,
    out_ref,
    pair_ref, mask_ref, gain_tri, w_left, w_right, w_tri_gate, gain_mid, w_tri_out, gain_att,
    w_attend, w_bias, w_attend_out, gain_trans, w_trans_in, w_trans_out, load_sems,
    work, edge_send, edge_recv, edge_work, near_all, far_all, gate_tri, tri_work, tri_send,
    tri_recv, mask_send, mask_recv, bias_send, bias_recv, bias_work, bias_all, bias_full, mask_cols, pair_one_t, gate_att,
    qkv_send, qkv_recv, query_buf, key_buf, value_buf, att_send, att_recv,
    edge_ss, edge_rs, near_ss, near_rs, far_ss, far_rs, tri_ss, tri_rs, bias_ss, bias_rs,
    biasc_ss, biasc_rs, pair_ss, pair_rs, mask_ss, mask_rs, qkv_ss, qkv_rs, att_ss, att_rs,
):
    r = lax.axis_index("row")
    c = lax.axis_index("col")
    y = c >> 2
    z = c & (ZS - 1)
    up = ((y + 1) & (YS - 1)) * ZS + z
    down = ((y + YS - 1) & (YS - 1)) * ZS + z

    def send(src, dst, ssem, rsem, row, col):
        pltpu.make_async_remote_copy(
            src_ref=src, dst_ref=dst, send_sem=ssem, recv_sem=rsem,
            device_id=(row, col), device_id_type=MESH,
        ).start()

    def wait(ref, sem):
        pltpu.make_async_copy(ref, ref, sem).wait()

    loads = [
        pltpu.make_async_copy(src, dst, load_sems.at[at])
        for at, (src, dst) in enumerate(
            [
                (pair_hbm, pair_ref), (gain_tri_hbm, gain_tri), (mask_hbm, mask_ref),
                (w_left_hbm, w_left), (w_right_hbm, w_right), (w_tri_gate_hbm, w_tri_gate),
                (gain_mid_hbm, gain_mid), (w_tri_out_hbm, w_tri_out), (gain_att_hbm, gain_att),
                (w_bias_hbm, w_bias), (w_attend_hbm, w_attend), (w_attend_out_hbm, w_attend_out),
                (gain_trans_hbm, gain_trans), (w_trans_in_hbm, w_trans_in),
                (w_trans_out_hbm, w_trans_out),
            ]
        )
    ]
    for load in loads:
        load.start()

    barrier = pltpu.get_barrier_semaphore()

    def hello(row, col):
        pl.semaphore_signal(barrier, inc=1, device_id=(row, col), device_id_type=MESH)

    @pl.loop(1, ROWS)
    def _(s):
        hello((r + s) & (ROWS - 1), c)

    @pl.loop(1, ZS)
    def _(s):
        hello(r, y * ZS + ((z + s) & (ZS - 1)))

    hello(r, up)
    hello(r, down)

    for load in loads[:5]:
        load.wait()
    work[...] = pair_ref[...].astype(F32).reshape(512, 128)
    pair_t = jnp.concatenate([work[pl.ds(j, 32, stride=16), :] for j in range(16)], 0)
    pair_one_t[...] = pair_t
    normed_t = layer_norm(pair_t, gain_tri[...]).astype(BF16)
    lane = lax.broadcasted_iota(jnp.int32, (32, 512), 1)
    spread = lax.broadcasted_iota(jnp.int32, (32, 512), 0) == (lane & 31)
    mask = dot(mask_ref[...].astype(F32).astype(BF16), spread.astype(F32).astype(BF16), 1, 0)
    lane = lax.broadcasted_iota(jnp.int32, (16, 512), 1)
    own = lax.broadcasted_iota(jnp.int32, (16, 512), 0) == (lane >> 5)
    mask = jnp.sum(jnp.where(own, mask, 0.0), 0, keepdims=True)
    sides = []
    for weight in (w_right, w_left):
        projected = dot(weight[...], normed_t, 0, 1)
        sides.append((mask * jax.nn.sigmoid(projected[:128]) * projected[128:]).reshape(ROWS, 8, 512))
    edge_send[...] = jnp.concatenate(sides, 1).astype(BF16)
    edge_recv[r] = edge_send[r]

    pl.semaphore_wait(barrier, (ROWS - 1) + (ZS - 1) + 2)

    @pl.loop(1, ROWS)
    def _(s):
        to = (r + s) & (ROWS - 1)
        send(edge_send.at[to], edge_recv.at[r], edge_ss.at[to], edge_rs.at[r], to, c)

    for load in loads[5:]:
        load.wait()
    gate_tri[...] = jax.nn.sigmoid(dot(normed_t, w_tri_gate[...], 1, 0))

    @pl.loop(1, ROWS)
    def _(s):
        of = (r + s) & (ROWS - 1)
        wait(edge_recv.at[of], edge_rs.at[of])

    for v in range(4):
        pieces = [
            jnp.concatenate(
                [edge_recv[4 * a + b, :, 128 * v : 128 * v + 128].astype(F32) for a in range(4)], 0
            )
            for b in range(4)
        ]
        for q, piece in enumerate(swap_blocks(pieces, 32)):
            for a in range(4):
                edge_work.at[a][pl.ds(4 * v + q, 16, stride=16), :] = piece[16 * a : 16 * a + 16]
    for a in range(4):
        block = edge_work[a].astype(BF16).reshape(2, 8, 16, 128)
        near_all[z, :, :, 128 * a : 128 * a + 128] = block[0]
        far_all[y, :, :, 128 * a : 128 * a + 128] = block[1]

    class Ring:
        def __init__(self, buf, ss, rs, size, me, to):
            self.buf, self.ss, self.rs, self.size, self.me, self.to = buf, ss, rs, size, me, to
            self.half = buf.shape[1] // 2

        def part(self, block, chunk):
            return self.buf.at[block & (self.size - 1), pl.ds(chunk * self.half, self.half)]

        def send(self, step, chunk, way):
            block = self.me + self.size - step + 1 if way == 0 else self.me + step - 1
            part = self.part(block, chunk)
            row, col = self.to[way]
            send(part, part, self.ss.at[way, step, chunk], self.rs.at[way, step, chunk], row, col)

        def land(self, step, chunk, way):
            block = self.me + self.size - step if way == 0 else self.me + step
            wait(self.part(block, chunk), self.rs.at[way, step, chunk])

        def start(self):
            for chunk in range(2):
                for way in range(2):
                    self.send(1, chunk, way)

        def turn(self, step, chunks=(0, 1)):
            last = self.size // 2
            for chunk in chunks:
                for way in range(2):
                    if step == last and way != chunk:
                        continue
                    self.land(step, chunk, way)
                    if step < last - 1 or (step == last - 1 and way == chunk):
                        self.send(step + 1, chunk, way)

        def sent(self):
            for step in range(1, self.size // 2 + 1):
                for chunk in range(2):
                    for way in range(2):
                        if step < self.size // 2 or way == chunk:
                            wait(self.part(0, 0), self.ss.at[way, step, chunk])

    y_ring = ((r, up), (r, down))
    far_ring = Ring(far_all, far_ss, far_rs, YS, y, y_ring)
    near_ring = Ring(
        near_all, near_ss, near_rs, ZS, z,
        ((r, y * ZS + ((z + 1) & (ZS - 1))), (r, y * ZS + ((z + ZS - 1) & (ZS - 1)))),
    )
    far_ring.start()
    near_ring.start()
    sub = lax.broadcasted_iota(jnp.int32, (16, 128), 0)
    for g in range(4):
        part = jnp.broadcast_to(mask[:, 128 * g : 128 * g + 128], (16, 128)).astype(BF16)
        for h in range(HEADS):
            mask_send[4 * h + g] = part
    mask_recv[r] = mask_send[r]

    @pl.loop(1, ROWS)
    def _(s):
        to = (r + s) & (ROWS - 1)
        send(mask_send.at[to], mask_recv.at[r], mask_ss.at[to], mask_rs.at[r], to, c)

    far_ring.turn(1)
    near_ring.turn(1, (0,))
    far_ring.turn(2)
    near_ring.turn(1, (1,))

    @pl.loop(1, ROWS)
    def _(s):
        of = (r + s) & (ROWS - 1)
        wait(mask_recv.at[of], mask_rs.at[of])

    pieces = [
        jnp.concatenate([mask_recv[4 * a + b].astype(F32)[:8] for a in range(4)], 0)
        for b in range(4)
    ]
    for q, piece in enumerate(swap_blocks(pieces, 32)):
        for a in range(4):
            mask_cols[q, :, 128 * a : 128 * a + 128] = piece[8 * a : 8 * a + 8]

    far_ring.turn(3)
    near_ring.turn(2)
    def reply(slot, piece):
        yy = (y + YS + slot - 3) & (YS - 1)
        tri_send[yy] = piece.astype(BF16).reshape(ZS, 16, 128)
        row = 2 * yy + (z >> 1)
        half = z & 1
        for t in (1, 2, 3):
            zz = (z + t) & (ZS - 1)
            send(
                tri_send.at[yy, zz], tri_recv.at[half, r], tri_ss.at[yy, zz], tri_rs.at[half, r],
                row, y * ZS + zz,
            )

        @pl.when(row != r)
        def _():
            send(
                tri_send.at[yy, z], tri_recv.at[half, r], tri_ss.at[yy, z], tri_rs.at[half, r],
                row, c,
            )

        @pl.when(row == r)
        def _():
            tri_recv[half, r] = tri_send[yy, z]

    def products(slots):
        for ch in range(8):
            rights = jnp.concatenate([near_all[s, ch] for s in range(ZS)], 0)
            lefts = [far_all[(y + YS + s - 3) & (YS - 1), ch] for s in slots]
            found = dot(rights, jnp.concatenate(lefts, 0), 1, 1)
            tri_work[64 * ch : 64 * ch + 64, 0 : 16 * len(lefts)] = found
        return [
            jnp.concatenate([tri_work[pl.ds(8 * g + m, 8, stride=64), :] for g in range(8)], 0)
            for m in range(8)
        ]

    tri_work[...] = jnp.zeros_like(tri_work)
    pieces = swap_blocks(products(range(7)), 16)
    for slot in (2, 4, 1, 5, 0, 6, 3):
        reply(slot, pieces[slot])
    far_ring.turn(4)
    pieces = products([7])
    lane = lax.broadcasted_iota(jnp.int32, pieces[0].shape, 1) >> 4
    merged = pieces[0]
    for m in range(1, 8):
        merged = jnp.where(lane == m, pltpu.roll(pieces[m], 16 * m, 1), merged)
    reply(7, merged)

    @pl.loop(0, ROWS)
    def _(s):
        for half in range(2):

            @pl.when(jnp.logical_or(s != r, z != 2 * (r & 1) + half))
            def _():
                wait(tri_recv.at[half, s], tri_rs.at[half, s])

    tri_t = jnp.concatenate(
        [
            tri_recv[half].astype(F32)[:, 8 * g : 8 * g + 8].reshape(128, 128)
            for half in range(2)
            for g in range(2)
        ],
        1,
    )
    gain_col = jnp.broadcast_to(gain_mid[...], (128, 128)).T
    tri_normed = layer_norm(tri_t, jnp.concatenate([gain_col] * 4, 1), 0).astype(BF16)
    update = dot(tri_normed, w_tri_out[...], 0, 0)
    update = jnp.concatenate(
        [
            update[256 * half + 16 * j : 256 * half + 16 * j + 16]
            for j in range(16)
            for half in range(2)
        ],
        0,
    )
    pair_t = (pair_one_t[...] + gate_tri[...] * update).astype(BF16).astype(F32)
    pair_one_t[...] = pair_t

    normed_two = layer_norm(pair_t, gain_att[...]).astype(BF16)
    bias_t = dot(w_bias[...], normed_two, 1, 1)
    for h in range(HEADS):
        base = jnp.zeros((16, 128), F32)
        for v in range(4):
            base = jnp.where(
                sub == v,
                jnp.broadcast_to(bias_t[h : h + 1, 128 * v : 128 * v + 128], (16, 128)),
                base,
            )
        bias_send[h] = base.astype(BF16)
    upper = r >> 3
    half = r & 1

    @pl.loop(0, 8)
    def _(s):
        m = ((r >> 1) + s) & 7
        to = 2 * m + upper

        @pl.when(to != r)
        def _():
            send(
                bias_send.at[m >> 1], bias_recv.at[r & 7], bias_ss.at[m], bias_rs.at[r & 7], to, c
            )

        @pl.when(to == r)
        def _():
            bias_recv[r & 7] = bias_send[m >> 1]

    projected = dot(w_attend[...], normed_two, 0, 1)
    for h in range(HEADS):
        for part in range(3):
            rows = projected[128 * part + 32 * h : 128 * part + 32 * h + 32]
            if part == 0:
                rows = rows * (LOG2E / math.sqrt(HEAD_DIM))
            for g in range(4):
                qkv_send[4 * h + g, 32 * part : 32 * part + 32, :] = rows[
                    :, 128 * g : 128 * g + 128
                ].astype(BF16)
    qkv_recv[r] = qkv_send[r]

    @pl.loop(1, ROWS)
    def _(s):
        to = (r + s) & (ROWS - 1)
        send(qkv_send.at[to], qkv_recv.at[r], qkv_ss.at[to], qkv_rs.at[r], to, c)

    gate_att[...] = jax.nn.sigmoid(projected[384:])

    @pl.loop(0, 8)
    def _(s):
        @pl.when(8 * half + s != r)
        def _():
            wait(bias_recv.at[s], bias_rs.at[s])

    pieces = [
        jnp.concatenate([bias_recv[4 * a + b].astype(F32)[:8] for a in range(2)], 0)
        for b in range(4)
    ]
    for q, piece in enumerate(swap_blocks(pieces, 32)):
        for a in range(2):
            for v in range(4):
                bias_work[a, 4 * v + q : 4 * v + q + 1, :] = piece[8 * a + v : 8 * a + v + 1]
    for a in range(2):
        bias_all[half, c, :, 128 * a : 128 * a + 128] = bias_work[a].astype(BF16)

    for near in (0, 1, 7, 2, 6, 3, 5, 4):
        for t in range(ZS):
            if near or t:
                to = ((y + near) & (YS - 1)) * ZS + ((z + t) & (ZS - 1))
                part = bias_all.at[half, c]
                send(part, part, biasc_ss.at[to], biasc_rs.at[c], r, to)

    @pl.loop(1, ROWS)
    def _(s):
        of = (r + s) & (ROWS - 1)
        wait(qkv_recv.at[of], qkv_rs.at[of])

    side = 1 - 2 * (y & 1)
    order = [((y >> 1) + 4 + apart) & 3 for apart in (0, -side, side, 2)]

    def hand_over(a):
        @pl.loop(0, 8)
        def _(s):
            of = 8 * a + s

            @pl.when(of != c)
            def _():
                wait(bias_all.at[half, of], biasc_rs.at[of])

        part = bias_all.at[half, pl.ds(8 * a, 8)]
        send(part, part, pair_ss.at[a], pair_rs.at[half, a], r ^ 1, c)

    hand_over(order[0])

    tail = (lax.broadcasted_iota(jnp.int32, (16, 512), 0) == 0).astype(BF16)
    for q in range(4):
        value_buf[q, 32:48, :] = tail
    for a in range(4):
        pieces = [qkv_recv[4 * a + b].astype(F32) for b in range(4)]
        for q, piece in enumerate(swap_blocks(pieces, 32)):
            piece = piece.astype(BF16)
            query_buf[q, a] = piece[:32]
            key_buf[q, :, 128 * a : 128 * a + 128] = piece[32:64]
            value_buf[q, 0:32, 128 * a : 128 * a + 128] = piece[64:]

    for step, a in enumerate(order):
        if step < 3:
            hand_over(order[step + 1])
        wait(bias_all.at[1 - half, pl.ds(8 * a, 8)], pair_rs.at[1 - half, a])
        for s in range(2):
            bias_full[:, 256 * s : 256 * s + 256] = (
                bias_all[s, pl.ds(8 * a, 8)].astype(F32).reshape(128, 256) * LOG2E
            )
        pieces = []
        for q in range(4):
            scores = dot(query_buf[q, a], key_buf[q], 0, 0) + bias_full[...]
            scores = jnp.where(mask_cols[q, 0:1, :] > 0.5, scores, MASKED)
            weight = jnp.exp2(scores - jnp.max(scores, 1, keepdims=True)).astype(BF16)
            total = dot(value_buf[q], weight, 1, 1)
            pieces.append(total[:32] / total[32:33])
        for b, piece in enumerate(swap_blocks(pieces, 32)):
            at = 4 * a + b
            att_send[at] = piece.astype(BF16)

            @pl.when(r != at)
            def _():
                send(att_send.at[at], att_recv.at[r], att_ss.at[at], att_rs.at[r], at, c)

            @pl.when(r == at)
            def _():
                att_recv[r] = att_send[at]

    @pl.loop(1, ROWS)
    def _(s):
        of = (r + s) & (ROWS - 1)
        wait(att_recv.at[of], att_rs.at[of])

    attended = jnp.concatenate(
        [
            jnp.concatenate([att_recv[4 * h + g].astype(F32) for g in range(4)], 1)
            for h in range(HEADS)
        ],
        0,
    )
    gated = (gate_att[...] * attended).astype(BF16)
    pair_two = (pair_one_t[...] + dot(gated, w_attend_out[...], 0, 0)).astype(BF16).astype(F32)
    normed_three = layer_norm(pair_two, gain_trans[...]).astype(BF16)
    for part in range(4):
        rows = slice(128 * part, 128 * part + 128)
        expanded = dot(normed_three[rows], w_trans_in[...], 1, 0)
        hidden = (jax.nn.silu(expanded[:, :512]) * expanded[:, 512:]).astype(BF16)
        work[rows, :] = pair_two[rows] + dot(hidden, w_trans_out[...], 1, 0)
    for i in range(32):
        out_ref[i] = work[pl.ds(i, 16, stride=32), :].astype(BF16)

    @pl.loop(1, ROWS)
    def _(s):
        to = (r + s) & (ROWS - 1)
        wait(edge_send.at[to], edge_ss.at[to])
        wait(mask_send.at[to], mask_ss.at[to])
        wait(qkv_send.at[to], qkv_ss.at[to])
        wait(att_send.at[to], att_ss.at[to])

    @pl.loop(0, 8)
    def _(s):
        @pl.when(2 * s + upper != r)
        def _():
            wait(bias_send.at[s >> 1], bias_ss.at[s])

    @pl.loop(0, YS * ZS)
    def _(s):
        @pl.when(s != c)
        def _():
            wait(bias_all.at[half, c], biasc_ss.at[s])

    for a in range(4):
        wait(bias_all.at[half, pl.ds(8 * a, 8)], pair_ss.at[a])

    @pl.loop(0, YS)
    def _(s):
        for t in range(ZS):

            @pl.when(jnp.logical_or(2 * s + (z >> 1) != r, z != t))
            def _():
                wait(tri_send.at[s, t], tri_ss.at[s, t])

    for each in (far_ring, near_ring):
        each.sent()


def per_device(
    pair, pair_mask, gain_tri, w_left, w_right, w_tri_gate, gain_mid, w_tri_out, gain_att, w_attend,
    w_bias, w_attend_out, gain_trans, w_trans_in, w_trans_out,
):
    vmem = pl.BlockSpec(memory_space=pltpu.VMEM)
    dma = pltpu.SemaphoreType.DMA
    row = lambda gain: gain.reshape(1, 128)
    return pl.pallas_call(
        kernel,
        out_shape=pltpu.VMEM((32, 16, 128), BF16),
        in_specs=[pl.BlockSpec(memory_space=pltpu.HBM)] * 15,
        out_specs=vmem,
        scratch_shapes=[
            pltpu.VMEM((32, 16, 128), BF16),
            pltpu.VMEM((16, 32), jnp.int32),
            pltpu.VMEM((1, 128), F32),
            pltpu.VMEM((128, 256), BF16),
            pltpu.VMEM((128, 256), BF16),
            pltpu.VMEM((128, 128), BF16),
            pltpu.VMEM((1, 128), F32),
            pltpu.VMEM((128, 128), BF16),
            pltpu.VMEM((1, 128), F32),
            pltpu.VMEM((128, 512), BF16),
            pltpu.VMEM((4, 128), BF16),
            pltpu.VMEM((128, 128), BF16),
            pltpu.VMEM((1, 128), F32),
            pltpu.VMEM((128, 1024), BF16),
            pltpu.VMEM((512, 128), BF16),
            dma((15,)),
            pltpu.VMEM((512, 128), F32),
            pltpu.VMEM((16, 16, 512), BF16),
            pltpu.VMEM((16, 16, 512), BF16),
            pltpu.VMEM((4, 256, 128), F32),
            pltpu.VMEM((ZS, 8, 16, 512), BF16),
            pltpu.VMEM((YS, 8, 16, 512), BF16),
            pltpu.VMEM((512, 128), F32),
            pltpu.VMEM((512, 128), F32),
            pltpu.VMEM((YS, ZS, 16, 128), BF16),
            pltpu.VMEM((2, 16, 16, 128), BF16),
            pltpu.VMEM((16, 16, 128), BF16),
            pltpu.VMEM((16, 16, 128), BF16),
            pltpu.VMEM((4, 16, 128), BF16),
            pltpu.VMEM((8, 16, 128), BF16),
            pltpu.VMEM((2, 16, 128), F32),
            pltpu.VMEM((2, YS * ZS, 16, 256), BF16),
            pltpu.VMEM((128, 512), F32),
            pltpu.VMEM((4, 8, 512), F32),
            pltpu.VMEM((512, 128), F32),
            pltpu.VMEM((128, 512), F32),
            pltpu.VMEM((16, 96, 128), BF16),
            pltpu.VMEM((16, 96, 128), BF16),
            pltpu.VMEM((4, 4, 32, 128), BF16),
            pltpu.VMEM((4, 32, 512), BF16),
            pltpu.VMEM((4, 48, 512), BF16),
            pltpu.VMEM((16, 32, 128), BF16),
            pltpu.VMEM((16, 32, 128), BF16),
            dma((16,)), dma((16,)),
            dma((2, 5, 2)), dma((2, 5, 2)),
            dma((2, 5, 2)), dma((2, 5, 2)),
            dma((YS, ZS)), dma((2, 16)),
            dma((8,)), dma((8,)),
            dma((YS * ZS,)), dma((YS * ZS,)),
            dma((4,)), dma((2, 4)),
            dma((16,)), dma((16,)),
            dma((16,)), dma((16,)),
            dma((16,)), dma((16,)),
        ],
        compiler_params=pltpu.CompilerParams(
            collective_id=0, has_side_effects=True, vmem_limit_bytes=VMEM_LIMIT
        ),
    )(
        pair, pair_mask.T, row(gain_tri), w_left, w_right, w_tri_gate, row(gain_mid),
        w_tri_out, row(gain_att), w_attend, w_bias.T, w_attend_out, row(gain_trans), w_trans_in,
        w_trans_out,
    )


def solution(mesh):
    in_specs = (P("row", "col", None), P("row", "col")) + (P(),) * 13
    return jax.shard_map(
        per_device, mesh=mesh, in_specs=in_specs, out_specs=P("row", "col", None), check_vma=False
    )
```

```python
import functools
import math

import jax
import jax.numpy as jnp
from jax import lax
from jax.experimental import pallas as pl
from jax.experimental.pallas import tpu as pltpu
from jax.sharding import PartitionSpec as P

HEADS = 4
HEAD_DIM = 32
EPS = 1e-05
MASKED = -1000000000.0
LOG2E = math.log2(math.e)
ROWS = 16
YS = 8
ZS = 4
VMEM_LIMIT = 63 * 1024 * 1024
MESH = pl.DeviceIdType.MESH
F32 = jnp.float32
BF16 = jnp.bfloat16


def dot(lhs, rhs, lhs_dim, rhs_dim):
    return lax.dot_general(
        lhs, rhs, (((lhs_dim,), (rhs_dim,)), ((), ())), preferred_element_type=F32
    )


def layer_norm(inputs, gain_vec, axis=-1):
    center = inputs - jnp.mean(inputs, axis, keepdims=True)
    spread = jnp.mean(center * center, axis, keepdims=True)
    return center * lax.rsqrt(spread + EPS) * gain_vec


def swap_blocks(arrays, width):
    arrays = list(arrays)
    lane = lax.broadcasted_iota(jnp.int32, arrays[0].shape, 1)
    step = 1
    while step < len(arrays):
        shift = width * step
        odd = (lane & shift) != 0
        fresh = list(arrays)
        for low in range(len(arrays)):
            if low & step == 0:
                high = low | step
                fresh[low] = jnp.where(odd, pltpu.roll(arrays[high], shift, 1), arrays[low])
                fresh[high] = jnp.where(odd, arrays[high], pltpu.roll(arrays[low], 128 - shift, 1))
        arrays = fresh
        step *= 2
    return arrays


def kernel(
    pair_hbm, mask_hbm, gain_tri_hbm, w_left_hbm, w_right_hbm, w_tri_gate_hbm, gain_mid_hbm,
    w_tri_out_hbm, gain_att_hbm, w_attend_hbm, w_bias_hbm, w_attend_out_hbm, gain_trans_hbm,
    w_trans_in_hbm, w_trans_out_hbm,
    out_ref,
    pair_ref, mask_ref, gain_tri, w_left, w_right, w_tri_gate, gain_mid, w_tri_out, gain_att,
    w_attend, w_bias, w_attend_out, gain_trans, w_trans_in, w_trans_out, load_sems,
    work, edge_send, edge_recv, edge_work, near_all, far_all, gate_tri, tri_work, tri_send,
    tri_recv, mask_send, mask_recv, bias_send, bias_recv, bias_work, bias_all, bias_full, mask_cols, pair_one_t, gate_att,
    qkv_send, qkv_recv, query_buf, key_buf, value_buf, att_send, att_recv,
    edge_ss, edge_rs, near_ss, near_rs, far_ss, far_rs, tri_ss, tri_rs, bias_ss, bias_rs,
    biasc_ss, biasc_rs, pair_ss, pair_rs, mask_ss, mask_rs, qkv_ss, qkv_rs, att_ss, att_rs,
):
    r = lax.axis_index("row")
    c = lax.axis_index("col")
    y = c >> 2
    z = c & (ZS - 1)
    up = ((y + 1) & (YS - 1)) * ZS + z
    down = ((y + YS - 1) & (YS - 1)) * ZS + z

    def send(src, dst, ssem, rsem, row, col):
        pltpu.make_async_remote_copy(
            src_ref=src, dst_ref=dst, send_sem=ssem, recv_sem=rsem,
            device_id=(row, col), device_id_type=MESH,
        ).start()

    def wait(ref, sem):
        pltpu.make_async_copy(ref, ref, sem).wait()

    loads = [
        pltpu.make_async_copy(src, dst, load_sems.at[at])
        for at, (src, dst) in enumerate(
            [
                (pair_hbm, pair_ref), (gain_tri_hbm, gain_tri), (mask_hbm, mask_ref),
                (w_left_hbm, w_left), (w_right_hbm, w_right), (w_tri_gate_hbm, w_tri_gate),
                (gain_mid_hbm, gain_mid), (w_tri_out_hbm, w_tri_out), (gain_att_hbm, gain_att),
                (w_bias_hbm, w_bias), (w_attend_hbm, w_attend), (w_attend_out_hbm, w_attend_out),
                (gain_trans_hbm, gain_trans), (w_trans_in_hbm, w_trans_in),
                (w_trans_out_hbm, w_trans_out),
            ]
        )
    ]
    for load in loads:
        load.start()

    barrier = pltpu.get_barrier_semaphore()

    def hello(row, col):
        pl.semaphore_signal(barrier, inc=1, device_id=(row, col), device_id_type=MESH)

    @pl.loop(1, ROWS)
    def _(s):
        hello((r + s) & (ROWS - 1), c)

    @pl.loop(1, ZS)
    def _(s):
        hello(r, y * ZS + ((z + s) & (ZS - 1)))

    hello(r, up)
    hello(r, down)

    for load in loads[:5]:
        load.wait()
    work[...] = pair_ref[...].astype(F32).reshape(512, 128)
    pair_t = jnp.concatenate([work[pl.ds(j, 32, stride=16), :] for j in range(16)], 0)
    pair_one_t[...] = pair_t
    normed_t = layer_norm(pair_t, gain_tri[...]).astype(BF16)
    lane = lax.broadcasted_iota(jnp.int32, (32, 512), 1)
    spread = lax.broadcasted_iota(jnp.int32, (32, 512), 0) == (lane & 31)
    mask = dot(mask_ref[...].astype(F32).astype(BF16), spread.astype(F32).astype(BF16), 1, 0)
    lane = lax.broadcasted_iota(jnp.int32, (16, 512), 1)
    own = lax.broadcasted_iota(jnp.int32, (16, 512), 0) == (lane >> 5)
    mask = jnp.sum(jnp.where(own, mask, 0.0), 0, keepdims=True)
    sides = []
    for weight in (w_right, w_left):
        projected = dot(weight[...], normed_t, 0, 1)
        sides.append((mask * jax.nn.sigmoid(projected[:128]) * projected[128:]).reshape(ROWS, 8, 512))
    edge_send[...] = jnp.concatenate(sides, 1).astype(BF16)
    edge_recv[r] = edge_send[r]

    pl.semaphore_wait(barrier, (ROWS - 1) + (ZS - 1) + 2)

    @pl.loop(1, ROWS)
    def _(s):
        to = (r + s) & (ROWS - 1)
        send(edge_send.at[to], edge_recv.at[r], edge_ss.at[to], edge_rs.at[r], to, c)

    for load in loads[5:]:
        load.wait()
    gate_tri[...] = jax.nn.sigmoid(dot(normed_t, w_tri_gate[...], 1, 0))

    @pl.loop(1, ROWS)
    def _(s):
        of = (r + s) & (ROWS - 1)
        wait(edge_recv.at[of], edge_rs.at[of])

    for v in range(4):
        pieces = [
            jnp.concatenate(
                [edge_recv[4 * a + b, :, 128 * v : 128 * v + 128].astype(F32) for a in range(4)], 0
            )
            for b in range(4)
        ]
        for q, piece in enumerate(swap_blocks(pieces, 32)):
            for a in range(4):
                edge_work.at[a][pl.ds(4 * v + q, 16, stride=16), :] = piece[16 * a : 16 * a + 16]
    for a in range(4):
        block = edge_work[a].astype(BF16).reshape(2, 8, 16, 128)
        near_all[z, :, :, 128 * a : 128 * a + 128] = block[0]
        far_all[y, :, :, 128 * a : 128 * a + 128] = block[1]

    class Ring:
        def __init__(self, buf, ss, rs, size, me, to, pieces):
            self.buf, self.ss, self.rs, self.size, self.me, self.to = buf, ss, rs, size, me, to
            self.pieces, self.extent = pieces, buf.shape[1] // pieces

        def part(self, block, chunk):
            at = block & (self.size - 1)
            return self.buf.at[at, pl.ds(chunk * self.extent, self.extent)]

        def takes(self, step, chunk, way):
            return step < self.size // 2 or 2 * chunk // self.pieces == way

        def send(self, step, chunk, way):
            block = self.me + self.size - step + 1 if way == 0 else self.me + step - 1
            part = self.part(block, chunk)
            row, col = self.to[way]
            send(part, part, self.ss.at[way, step, chunk], self.rs.at[way, step, chunk], row, col)

        def land(self, step, chunk, way):
            block = self.me + self.size - step if way == 0 else self.me + step
            wait(self.part(block, chunk), self.rs.at[way, step, chunk])

        def each(self, step, chunks=None):
            for chunk in range(self.pieces) if chunks is None else chunks:
                for way in range(2):
                    if self.takes(step, chunk, way):
                        yield chunk, way

        def start(self):
            for chunk, way in self.each(1):
                self.send(1, chunk, way)

        def turn(self, step, chunks=None):
            for chunk, way in self.each(step, chunks):
                self.land(step, chunk, way)
                if step < self.size // 2 and self.takes(step + 1, chunk, way):
                    self.send(step + 1, chunk, way)

        def sent(self):
            for step in range(1, self.size // 2 + 1):
                for chunk, way in self.each(step):
                    wait(self.part(0, 0), self.ss.at[way, step, chunk])

    y_ring = ((r, up), (r, down))
    far_ring = Ring(far_all, far_ss, far_rs, YS, y, y_ring, 4)
    near_ring = Ring(
        near_all, near_ss, near_rs, ZS, z,
        ((r, y * ZS + ((z + 1) & (ZS - 1))), (r, y * ZS + ((z + ZS - 1) & (ZS - 1)))),
        2,
    )
    far_ring.start()
    near_ring.start()
    sub = lax.broadcasted_iota(jnp.int32, (16, 128), 0)
    for g in range(4):
        part = jnp.broadcast_to(mask[:, 128 * g : 128 * g + 128], (16, 128)).astype(BF16)
        for h in range(HEADS):
            mask_send[4 * h + g] = part
    mask_recv[r] = mask_send[r]

    @pl.loop(1, ROWS)
    def _(s):
        to = (r + s) & (ROWS - 1)
        send(mask_send.at[to], mask_recv.at[r], mask_ss.at[to], mask_rs.at[r], to, c)

    far_ring.turn(1)
    near_ring.turn(1, (0,))
    far_ring.turn(2)
    near_ring.turn(1, (1,))

    @pl.loop(1, ROWS)
    def _(s):
        of = (r + s) & (ROWS - 1)
        wait(mask_recv.at[of], mask_rs.at[of])

    pieces = [
        jnp.concatenate([mask_recv[4 * a + b].astype(F32)[:8] for a in range(4)], 0)
        for b in range(4)
    ]
    for q, piece in enumerate(swap_blocks(pieces, 32)):
        for a in range(4):
            mask_cols[q, :, 128 * a : 128 * a + 128] = piece[8 * a : 8 * a + 8]

    far_ring.turn(3)
    near_ring.turn(2)
    def reply(slot, piece):
        yy = (y + YS + slot - 3) & (YS - 1)
        tri_send[yy] = piece.astype(BF16).reshape(ZS, 16, 128)
        row = 2 * yy + (z >> 1)
        half = z & 1
        for t in (1, 2, 3):
            zz = (z + t) & (ZS - 1)
            send(
                tri_send.at[yy, zz], tri_recv.at[half, r], tri_ss.at[yy, zz], tri_rs.at[half, r],
                row, y * ZS + zz,
            )

        @pl.when(row != r)
        def _():
            send(
                tri_send.at[yy, z], tri_recv.at[half, r], tri_ss.at[yy, z], tri_rs.at[half, r],
                row, c,
            )

        @pl.when(row == r)
        def _():
            tri_recv[half, r] = tri_send[yy, z]

    def products(slots):
        for ch in range(8):
            rights = jnp.concatenate([near_all[s, ch] for s in range(ZS)], 0)
            lefts = [far_all[(y + YS + s - 3) & (YS - 1), ch] for s in slots]
            found = dot(rights, jnp.concatenate(lefts, 0), 1, 1)
            tri_work[64 * ch : 64 * ch + 64, 0 : 16 * len(lefts)] = found
        return [
            jnp.concatenate([tri_work[pl.ds(8 * g + m, 8, stride=64), :] for g in range(8)], 0)
            for m in range(8)
        ]

    tri_work[...] = jnp.zeros_like(tri_work)
    pieces = swap_blocks(products(range(7)), 16)
    for slot in (2, 4, 1, 5, 0, 6, 3):
        reply(slot, pieces[slot])
    far_ring.turn(4)
    pieces = products([7])
    lane = lax.broadcasted_iota(jnp.int32, pieces[0].shape, 1) >> 4
    merged = pieces[0]
    for m in range(1, 8):
        merged = jnp.where(lane == m, pltpu.roll(pieces[m], 16 * m, 1), merged)
    reply(7, merged)

    @pl.loop(0, ROWS)
    def _(s):
        for half in range(2):

            @pl.when(jnp.logical_or(s != r, z != 2 * (r & 1) + half))
            def _():
                wait(tri_recv.at[half, s], tri_rs.at[half, s])

    tri_t = jnp.concatenate(
        [
            tri_recv[half].astype(F32)[:, 8 * g : 8 * g + 8].reshape(128, 128)
            for half in range(2)
            for g in range(2)
        ],
        1,
    )
    gain_col = jnp.broadcast_to(gain_mid[...], (128, 128)).T
    tri_normed = layer_norm(tri_t, jnp.concatenate([gain_col] * 4, 1), 0).astype(BF16)
    update = dot(tri_normed, w_tri_out[...], 0, 0)
    update = jnp.concatenate(
        [
            update[256 * half + 16 * j : 256 * half + 16 * j + 16]
            for j in range(16)
            for half in range(2)
        ],
        0,
    )
    pair_t = (pair_one_t[...] + gate_tri[...] * update).astype(BF16).astype(F32)
    pair_one_t[...] = pair_t

    normed_two = layer_norm(pair_t, gain_att[...]).astype(BF16)
    bias_t = dot(w_bias[...], normed_two, 1, 1)
    for h in range(HEADS):
        base = jnp.zeros((16, 128), F32)
        for v in range(4):
            base = jnp.where(
                sub == v,
                jnp.broadcast_to(bias_t[h : h + 1, 128 * v : 128 * v + 128], (16, 128)),
                base,
            )
        bias_send[h] = base.astype(BF16)
    upper = r >> 3
    half = r & 1

    @pl.loop(0, 8)
    def _(s):
        m = ((r >> 1) + s) & 7
        to = 2 * m + upper

        @pl.when(to != r)
        def _():
            send(
                bias_send.at[m >> 1], bias_recv.at[r & 7], bias_ss.at[m], bias_rs.at[r & 7], to, c
            )

        @pl.when(to == r)
        def _():
            bias_recv[r & 7] = bias_send[m >> 1]

    projected = dot(w_attend[...], normed_two, 0, 1)
    for h in range(HEADS):
        for part in range(3):
            rows = projected[128 * part + 32 * h : 128 * part + 32 * h + 32]
            if part == 0:
                rows = rows * (LOG2E / math.sqrt(HEAD_DIM))
            for g in range(4):
                qkv_send[4 * h + g, 32 * part : 32 * part + 32, :] = rows[
                    :, 128 * g : 128 * g + 128
                ].astype(BF16)
    qkv_recv[r] = qkv_send[r]

    @pl.loop(1, ROWS)
    def _(s):
        to = (r + s) & (ROWS - 1)
        send(qkv_send.at[to], qkv_recv.at[r], qkv_ss.at[to], qkv_rs.at[r], to, c)

    gate_att[...] = jax.nn.sigmoid(projected[384:])

    @pl.loop(0, 8)
    def _(s):
        @pl.when(8 * half + s != r)
        def _():
            wait(bias_recv.at[s], bias_rs.at[s])

    pieces = [
        jnp.concatenate([bias_recv[4 * a + b].astype(F32)[:8] for a in range(2)], 0)
        for b in range(4)
    ]
    for q, piece in enumerate(swap_blocks(pieces, 32)):
        for a in range(2):
            for v in range(4):
                bias_work[a, 4 * v + q : 4 * v + q + 1, :] = piece[8 * a + v : 8 * a + v + 1]
    for a in range(2):
        bias_all[half, c, :, 128 * a : 128 * a + 128] = bias_work[a].astype(BF16)

    for near in (0, 1, 7, 2, 6, 3, 5, 4):
        for t in range(ZS):
            if near or t:
                to = ((y + near) & (YS - 1)) * ZS + ((z + t) & (ZS - 1))
                part = bias_all.at[half, c]
                send(part, part, biasc_ss.at[to], biasc_rs.at[c], r, to)

    side = 1 - 2 * (y & 1)
    order = [((y >> 1) + 4 + apart) & 3 for apart in (0, -side, side, 2)]

    def hand_over(a):
        @pl.loop(0, 8)
        def _(s):
            of = 8 * a + s

            @pl.when(of != c)
            def _():
                wait(bias_all.at[half, of], biasc_rs.at[of])

        part = bias_all.at[half, pl.ds(8 * a, 8)]
        send(part, part, pair_ss.at[a], pair_rs.at[half, a], r ^ 1, c)

    hand_over(order[0])
    hand_over(order[1])

    @pl.loop(1, ROWS)
    def _(s):
        of = (r + s) & (ROWS - 1)
        wait(qkv_recv.at[of], qkv_rs.at[of])

    tail = (lax.broadcasted_iota(jnp.int32, (16, 512), 0) == 0).astype(BF16)
    for q in range(4):
        value_buf[q, 32:48, :] = tail
    for a in range(4):
        pieces = [qkv_recv[4 * a + b].astype(F32) for b in range(4)]
        for q, piece in enumerate(swap_blocks(pieces, 32)):
            piece = piece.astype(BF16)
            query_buf[q, a] = piece[:32]
            key_buf[q, :, 128 * a : 128 * a + 128] = piece[32:64]
            value_buf[q, 0:32, 128 * a : 128 * a + 128] = piece[64:]

    for step, a in enumerate(order):
        if step < 2:
            hand_over(order[step + 2])
        wait(bias_all.at[1 - half, pl.ds(8 * a, 8)], pair_rs.at[1 - half, a])
        for s in range(2):
            bias_full[:, 256 * s : 256 * s + 256] = (
                bias_all[s, pl.ds(8 * a, 8)].astype(F32).reshape(128, 256) * LOG2E
            )
        pieces = []
        for q in range(4):
            raw = dot(query_buf[q, a], key_buf[q], 0, 0)
            present = mask_cols[q, 0:1, :] > 0.5
            weights = []
            for t in range(0, 128, 32):
                scores = raw[t : t + 32] + bias_full[t : t + 32, :]
                scores = jnp.where(present, scores, MASKED)
                top = jnp.max(scores, 1, keepdims=True)
                weights.append(jnp.exp2(scores - top).astype(BF16))
            total = dot(value_buf[q], jnp.concatenate(weights, 0), 1, 1)
            pieces.append(total[:32] / total[32:33])
        for b, piece in enumerate(swap_blocks(pieces, 32)):
            at = 4 * a + b
            att_send[at] = piece.astype(BF16)

            @pl.when(r != at)
            def _():
                send(att_send.at[at], att_recv.at[r], att_ss.at[at], att_rs.at[r], at, c)

            @pl.when(r == at)
            def _():
                att_recv[r] = att_send[at]

    @pl.loop(1, ROWS)
    def _(s):
        of = (r + s) & (ROWS - 1)
        wait(att_recv.at[of], att_rs.at[of])

    attended = jnp.concatenate(
        [
            jnp.concatenate([att_recv[4 * h + g].astype(F32) for g in range(4)], 1)
            for h in range(HEADS)
        ],
        0,
    )
    gated = (gate_att[...] * attended).astype(BF16)
    pair_two = (pair_one_t[...] + dot(gated, w_attend_out[...], 0, 0)).astype(BF16).astype(F32)
    normed_three = layer_norm(pair_two, gain_trans[...]).astype(BF16)
    for part in range(4):
        rows = slice(128 * part, 128 * part + 128)
        expanded = dot(normed_three[rows], w_trans_in[...], 1, 0)
        hidden = jnp.concatenate(
            [
                (
                    jax.nn.silu(expanded[t : t + 16, :512]) * expanded[t : t + 16, 512:]
                ).astype(BF16)
                for t in range(0, 128, 16)
            ],
            0,
        )
        work[rows, :] = pair_two[rows] + dot(hidden, w_trans_out[...], 1, 0)
    for i in range(32):
        out_ref[i] = work[pl.ds(i, 16, stride=32), :].astype(BF16)

    @pl.loop(1, ROWS)
    def _(s):
        to = (r + s) & (ROWS - 1)
        wait(edge_send.at[to], edge_ss.at[to])
        wait(mask_send.at[to], mask_ss.at[to])
        wait(qkv_send.at[to], qkv_ss.at[to])
        wait(att_send.at[to], att_ss.at[to])

    @pl.loop(0, 8)
    def _(s):
        @pl.when(2 * s + upper != r)
        def _():
            wait(bias_send.at[s >> 1], bias_ss.at[s])

    @pl.loop(0, YS * ZS)
    def _(s):
        @pl.when(s != c)
        def _():
            wait(bias_all.at[half, c], biasc_ss.at[s])

    for a in range(4):
        wait(bias_all.at[half, pl.ds(8 * a, 8)], pair_ss.at[a])

    @pl.loop(0, YS)
    def _(s):
        for t in range(ZS):

            @pl.when(jnp.logical_or(2 * s + (z >> 1) != r, z != t))
            def _():
                wait(tri_send.at[s, t], tri_ss.at[s, t])

    for each in (far_ring, near_ring):
        each.sent()


def per_device(
    pair, pair_mask, gain_tri, w_left, w_right, w_tri_gate, gain_mid, w_tri_out, gain_att, w_attend,
    w_bias, w_attend_out, gain_trans, w_trans_in, w_trans_out,
):
    vmem = pl.BlockSpec(memory_space=pltpu.VMEM)
    dma = pltpu.SemaphoreType.DMA
    row = lambda gain: gain.reshape(1, 128)
    return pl.pallas_call(
        kernel,
        out_shape=pltpu.VMEM((32, 16, 128), BF16),
        in_specs=[pl.BlockSpec(memory_space=pltpu.HBM)] * 15,
        out_specs=vmem,
        scratch_shapes=[
            pltpu.VMEM((32, 16, 128), BF16),
            pltpu.VMEM((16, 32), jnp.int32),
            pltpu.VMEM((1, 128), F32),
            pltpu.VMEM((128, 256), BF16),
            pltpu.VMEM((128, 256), BF16),
            pltpu.VMEM((128, 128), BF16),
            pltpu.VMEM((1, 128), F32),
            pltpu.VMEM((128, 128), BF16),
            pltpu.VMEM((1, 128), F32),
            pltpu.VMEM((128, 512), BF16),
            pltpu.VMEM((4, 128), BF16),
            pltpu.VMEM((128, 128), BF16),
            pltpu.VMEM((1, 128), F32),
            pltpu.VMEM((128, 1024), BF16),
            pltpu.VMEM((512, 128), BF16),
            dma((15,)),
            pltpu.VMEM((512, 128), F32),
            pltpu.VMEM((16, 16, 512), BF16),
            pltpu.VMEM((16, 16, 512), BF16),
            pltpu.VMEM((4, 256, 128), F32),
            pltpu.VMEM((ZS, 8, 16, 512), BF16),
            pltpu.VMEM((YS, 8, 16, 512), BF16),
            pltpu.VMEM((512, 128), F32),
            pltpu.VMEM((512, 128), F32),
            pltpu.VMEM((YS, ZS, 16, 128), BF16),
            pltpu.VMEM((2, 16, 16, 128), BF16),
            pltpu.VMEM((16, 16, 128), BF16),
            pltpu.VMEM((16, 16, 128), BF16),
            pltpu.VMEM((4, 16, 128), BF16),
            pltpu.VMEM((8, 16, 128), BF16),
            pltpu.VMEM((2, 16, 128), F32),
            pltpu.VMEM((2, YS * ZS, 16, 256), BF16),
            pltpu.VMEM((128, 512), F32),
            pltpu.VMEM((4, 8, 512), F32),
            pltpu.VMEM((512, 128), F32),
            pltpu.VMEM((128, 512), F32),
            pltpu.VMEM((16, 96, 128), BF16),
            pltpu.VMEM((16, 96, 128), BF16),
            pltpu.VMEM((4, 4, 32, 128), BF16),
            pltpu.VMEM((4, 32, 512), BF16),
            pltpu.VMEM((4, 48, 512), BF16),
            pltpu.VMEM((16, 32, 128), BF16),
            pltpu.VMEM((16, 32, 128), BF16),
            dma((16,)), dma((16,)),
            dma((2, 5, 2)), dma((2, 5, 2)),
            dma((2, 5, 4)), dma((2, 5, 4)),
            dma((YS, ZS)), dma((2, 16)),
            dma((8,)), dma((8,)),
            dma((YS * ZS,)), dma((YS * ZS,)),
            dma((4,)), dma((2, 4)),
            dma((16,)), dma((16,)),
            dma((16,)), dma((16,)),
            dma((16,)), dma((16,)),
        ],
        compiler_params=pltpu.CompilerParams(
            collective_id=0, has_side_effects=True, vmem_limit_bytes=VMEM_LIMIT
        ),
    )(
        pair, pair_mask.T, row(gain_tri), w_left, w_right, w_tri_gate, row(gain_mid),
        w_tri_out, row(gain_att), w_attend, w_bias.T, w_attend_out, row(gain_trans), w_trans_in,
        w_trans_out,
    )


def solution(mesh):
    in_specs = (P("row", "col", None), P("row", "col")) + (P(),) * 13
    return jax.shard_map(
        per_device, mesh=mesh, in_specs=in_specs, out_specs=P("row", "col", None), check_vma=False
    )
```

```python
import functools
import math

import jax
import jax.numpy as jnp
from jax import lax
from jax.experimental import pallas as pl
from jax.experimental.pallas import tpu as pltpu
from jax.sharding import PartitionSpec as P

HEADS = 4
HEAD_DIM = 32
EPS = 1e-05
MASKED = -1e30
LOG2E = math.log2(math.e)
ROWS = 16
YS = 8
ZS = 4
VMEM_LIMIT = 63 * 1024 * 1024
MESH = pl.DeviceIdType.MESH
F32 = jnp.float32
BF16 = jnp.bfloat16


def dot(lhs, rhs, lhs_dim, rhs_dim):
    return lax.dot_general(
        lhs, rhs, (((lhs_dim,), (rhs_dim,)), ((), ())), preferred_element_type=F32
    )


def layer_norm(inputs, gain_vec, axis=-1):
    center = inputs - jnp.mean(inputs, axis, keepdims=True)
    spread = jnp.mean(center * center, axis, keepdims=True)
    return center * lax.rsqrt(spread + EPS) * gain_vec


def swap_blocks(arrays, width):
    arrays = list(arrays)
    lane = lax.broadcasted_iota(jnp.int32, arrays[0].shape, 1)
    step = 1
    while step < len(arrays):
        shift = width * step
        odd = (lane & shift) != 0
        fresh = list(arrays)
        for low in range(len(arrays)):
            if low & step == 0:
                high = low | step
                fresh[low] = jnp.where(odd, pltpu.roll(arrays[high], shift, 1), arrays[low])
                fresh[high] = jnp.where(odd, arrays[high], pltpu.roll(arrays[low], 128 - shift, 1))
        arrays = fresh
        step *= 2
    return arrays


def kernel(
    pair_hbm, mask_hbm, gain_tri_hbm, w_left_hbm, w_right_hbm, w_tri_gate_hbm, gain_mid_hbm,
    w_tri_out_hbm, gain_att_hbm, w_attend_hbm, w_bias_hbm, w_attend_out_hbm, gain_trans_hbm,
    w_trans_in_hbm, w_trans_out_hbm,
    out_ref,
    pair_ref, mask_ref, gain_tri, w_left, w_right, w_tri_gate, gain_mid, w_tri_out, gain_att,
    w_attend, w_bias, w_attend_out, gain_trans, w_trans_in, w_trans_out, load_sems,
    work, edge_send, edge_recv, edge_work, near_all, far_all, gate_tri, tri_work, tri_send,
    tri_recv, mask_send, mask_recv, bias_send, bias_recv, bias_work, bias_all, bias_full, mask_cols, pair_one_t, gate_att,
    qkv_send, qkv_recv, query_buf, key_buf, value_buf, att_send, att_recv,
    edge_ss, edge_rs, near_ss, near_rs, far_ss, far_rs, tri_ss, tri_rs, bias_ss, bias_rs,
    biasc_ss, biasc_rs, pair_ss, pair_rs, mask_ss, mask_rs, qkv_ss, qkv_rs, att_ss, att_rs,
):
    r = lax.axis_index("row")
    c = lax.axis_index("col")
    y = c >> 2
    z = c & (ZS - 1)
    up = ((y + 1) & (YS - 1)) * ZS + z
    down = ((y + YS - 1) & (YS - 1)) * ZS + z

    def send(src, dst, ssem, rsem, row, col):
        pltpu.make_async_remote_copy(
            src_ref=src, dst_ref=dst, send_sem=ssem, recv_sem=rsem,
            device_id=(row, col), device_id_type=MESH,
        ).start()

    def wait(ref, sem):
        pltpu.make_async_copy(ref, ref, sem).wait()

    loads = [
        pltpu.make_async_copy(src, dst, load_sems.at[at])
        for at, (src, dst) in enumerate(
            [
                (pair_hbm, pair_ref), (gain_tri_hbm, gain_tri), (mask_hbm, mask_ref),
                (w_left_hbm, w_left), (w_right_hbm, w_right), (w_tri_gate_hbm, w_tri_gate),
                (gain_mid_hbm, gain_mid), (w_tri_out_hbm, w_tri_out), (gain_att_hbm, gain_att),
                (w_bias_hbm, w_bias), (w_attend_hbm, w_attend), (w_attend_out_hbm, w_attend_out),
                (gain_trans_hbm, gain_trans), (w_trans_in_hbm, w_trans_in),
                (w_trans_out_hbm, w_trans_out),
            ]
        )
    ]
    for load in loads[:5]:
        load.start()

    barrier = pltpu.get_barrier_semaphore()

    def hello(row, col):
        pl.semaphore_signal(barrier, inc=1, device_id=(row, col), device_id_type=MESH)

    @pl.loop(1, ROWS)
    def _(s):
        hello((r + s) & (ROWS - 1), c)

    @pl.loop(1, ZS)
    def _(s):
        hello(r, y * ZS + ((z + s) & (ZS - 1)))

    hello(r, up)
    hello(r, down)

    for load in loads[5:]:
        load.start()

    for load in loads[:5]:
        load.wait()
    work[...] = pair_ref[...].astype(F32).reshape(512, 128)
    pair_t = jnp.concatenate([work[pl.ds(j, 32, stride=16), :] for j in range(16)], 0)
    pair_one_t[...] = pair_t
    normed_t = layer_norm(pair_t, gain_tri[...]).astype(BF16)
    lane = lax.broadcasted_iota(jnp.int32, (32, 512), 1)
    spread = lax.broadcasted_iota(jnp.int32, (32, 512), 0) == (lane & 31)
    mask = dot(mask_ref[...].astype(F32).astype(BF16), spread.astype(F32).astype(BF16), 1, 0)
    lane = lax.broadcasted_iota(jnp.int32, (16, 512), 1)
    own = lax.broadcasted_iota(jnp.int32, (16, 512), 0) == (lane >> 5)
    mask = jnp.sum(jnp.where(own, mask, 0.0), 0, keepdims=True)
    sides = []
    for weight in (w_right, w_left):
        projected = dot(weight[...], normed_t, 0, 1)
        sides.append((mask * jax.nn.sigmoid(projected[:128]) * projected[128:]).reshape(ROWS, 8, 512))
    edge_send[...] = jnp.concatenate(sides, 1).astype(BF16)
    edge_recv[r] = edge_send[r]

    pl.semaphore_wait(barrier, (ROWS - 1) + (ZS - 1) + 2)

    for s in range(1, ROWS):
        to = (r + s) & (ROWS - 1)
        send(edge_send.at[to], edge_recv.at[r], edge_ss, edge_rs, to, c)

    for load in loads[5:]:
        load.wait()
    gate_tri[...] = jax.nn.sigmoid(dot(normed_t, w_tri_gate[...], 1, 0))

    wait(edge_recv.at[pl.ds(0, ROWS - 1)], edge_rs)

    for v in range(4):
        pieces = [
            jnp.concatenate(
                [edge_recv[4 * a + b, :, 128 * v : 128 * v + 128].astype(F32) for a in range(4)], 0
            )
            for b in range(4)
        ]
        for q, piece in enumerate(swap_blocks(pieces, 32)):
            for a in range(4):
                edge_work.at[a][pl.ds(4 * v + q, 16, stride=16), :] = piece[16 * a : 16 * a + 16]
    for a in range(4):
        block = edge_work[a].astype(BF16).reshape(2, 8, 16, 128)
        near_all[z, :, :, 128 * a : 128 * a + 128] = block[0]
        far_all[y, :, :, 128 * a : 128 * a + 128] = block[1]

    class Ring:
        def __init__(self, buf, ss, rs, size, me, to, pieces):
            self.buf, self.ss, self.rs, self.size, self.me, self.to = buf, ss, rs, size, me, to
            self.pieces, self.extent = pieces, buf.shape[1] // pieces

        def part(self, block, chunk):
            at = block & (self.size - 1)
            return self.buf.at[at, pl.ds(chunk * self.extent, self.extent)]

        def takes(self, step, chunk, way):
            return step < self.size // 2 or 2 * chunk // self.pieces == way

        def send(self, step, chunk, way):
            block = self.me + self.size - step + 1 if way == 0 else self.me + step - 1
            part = self.part(block, chunk)
            row, col = self.to[way]
            send(part, part, self.ss, self.rs.at[way, step, chunk], row, col)

        def land(self, step, chunk, way):
            block = self.me + self.size - step if way == 0 else self.me + step
            wait(self.part(block, chunk), self.rs.at[way, step, chunk])

        def each(self, step, chunks=None):
            for chunk in range(self.pieces) if chunks is None else chunks:
                for way in range(2):
                    if self.takes(step, chunk, way):
                        yield chunk, way

        def start(self):
            for chunk, way in self.each(1):
                self.send(1, chunk, way)

        def turn(self, step, chunks=None):
            for chunk, way in self.each(step, chunks):
                self.land(step, chunk, way)
                if step < self.size // 2 and self.takes(step + 1, chunk, way):
                    self.send(step + 1, chunk, way)

        def sent(self):
            wait(self.buf.at[pl.ds(0, self.size - 1)], self.ss)

    y_ring = ((r, up), (r, down))
    far_ring = Ring(far_all, far_ss, far_rs, YS, y, y_ring, 4)
    near_ring = Ring(
        near_all, near_ss, near_rs, ZS, z,
        ((r, y * ZS + ((z + 1) & (ZS - 1))), (r, y * ZS + ((z + ZS - 1) & (ZS - 1)))),
        2,
    )
    far_ring.start()
    near_ring.start()
    sub = lax.broadcasted_iota(jnp.int32, (16, 128), 0)
    for g in range(4):
        part = jnp.broadcast_to(mask[:, 128 * g : 128 * g + 128], (16, 128)).astype(BF16)
        for h in range(HEADS):
            mask_send[4 * h + g] = part
    mask_recv[r] = mask_send[r]

    for s in range(1, ROWS):
        to = (r + s) & (ROWS - 1)
        send(mask_send.at[to], mask_recv.at[r], mask_ss, mask_rs, to, c)

    far_ring.turn(1)
    near_ring.turn(1, (0,))
    far_ring.turn(2)
    near_ring.turn(1, (1,))

    wait(mask_recv.at[pl.ds(0, ROWS - 1)], mask_rs)

    pieces = [
        jnp.concatenate([mask_recv[4 * a + b].astype(F32)[:8] for a in range(4)], 0)
        for b in range(4)
    ]
    for q, piece in enumerate(swap_blocks(pieces, 32)):
        for a in range(4):
            mask_cols[q, :, 128 * a : 128 * a + 128] = piece[8 * a : 8 * a + 8]

    far_ring.turn(3)
    near_ring.turn(2)
    def reply(slot, piece):
        yy = (y + YS + slot - 3) & (YS - 1)
        tri_send[yy] = piece.astype(BF16).reshape(ZS, 16, 128)
        row = 2 * yy + (z >> 1)
        half = z & 1
        for t in (1, 2, 3):
            zz = (z + t) & (ZS - 1)
            send(
                tri_send.at[yy, zz], tri_recv.at[half, r], tri_ss, tri_rs,
                row, y * ZS + zz,
            )

        @pl.when(row != r)
        def _():
            send(
                tri_send.at[yy, z], tri_recv.at[half, r], tri_ss, tri_rs,
                row, c,
            )

        @pl.when(row == r)
        def _():
            pltpu.make_async_copy(tri_send.at[yy, z], tri_recv.at[half, r], tri_rs).start()

    def products(slots):
        for ch in range(8):
            rights = jnp.concatenate([near_all[s, ch] for s in range(ZS)], 0)
            lefts = [far_all[(y + YS + s - 3) & (YS - 1), ch] for s in slots]
            found = dot(rights, jnp.concatenate(lefts, 0), 1, 1)
            tri_work[64 * ch : 64 * ch + 64, 0 : 16 * len(lefts)] = found
        return [
            jnp.concatenate([tri_work[pl.ds(8 * g + m, 8, stride=64), :] for g in range(8)], 0)
            for m in range(8)
        ]

    tri_work[...] = jnp.zeros_like(tri_work)
    pieces = swap_blocks(products(range(7)), 16)
    for slot in (2, 4, 1, 5, 0, 6, 3):
        reply(slot, pieces[slot])
    far_ring.turn(4)
    pieces = products([7])
    lane = lax.broadcasted_iota(jnp.int32, pieces[0].shape, 1) >> 4
    merged = pieces[0]
    for m in range(1, 8):
        merged = jnp.where(lane == m, pltpu.roll(pieces[m], 16 * m, 1), merged)
    reply(7, merged)

    wait(edge_send.at[pl.ds(0, ROWS - 1)], edge_ss)
    wait(mask_send.at[pl.ds(0, ROWS - 1)], mask_ss)
    far_ring.sent()
    near_ring.sent()
    wait(tri_recv, tri_rs)

    tri_t = jnp.concatenate(
        [
            tri_recv[half].astype(F32)[:, 8 * g : 8 * g + 8].reshape(128, 128)
            for half in range(2)
            for g in range(2)
        ],
        1,
    )
    gain_col = jnp.broadcast_to(gain_mid[...], (128, 128)).T
    tri_normed = layer_norm(tri_t, jnp.concatenate([gain_col] * 4, 1), 0).astype(BF16)
    update = dot(tri_normed, w_tri_out[...], 0, 0)
    update = jnp.concatenate(
        [
            update[256 * half + 16 * j : 256 * half + 16 * j + 16]
            for j in range(16)
            for half in range(2)
        ],
        0,
    )
    pair_t = (pair_one_t[...] + gate_tri[...] * update).astype(BF16).astype(F32)
    pair_one_t[...] = pair_t

    normed_two = layer_norm(pair_t, gain_att[...]).astype(BF16)
    bias_t = dot(w_bias[...], normed_two, 1, 1)
    for h in range(HEADS):
        base = jnp.zeros((16, 128), F32)
        for v in range(4):
            base = jnp.where(
                sub == v,
                jnp.broadcast_to(bias_t[h : h + 1, 128 * v : 128 * v + 128], (16, 128)),
                base,
            )
        bias_send[h] = base.astype(BF16)
    upper = r >> 3
    half = r & 1

    own = bias_send.at[r >> 2]
    mine = bias_recv.at[r & 7]

    @pl.when(upper != half)
    def _():
        send(own, mine, bias_ss, bias_rs, r ^ 1, c)

    @pl.when(upper == half)
    def _():
        pltpu.make_async_copy(own, mine, bias_rs).start()

    for s in range(1, 8):
        m = ((r >> 1) + s) & 7
        send(bias_send.at[m >> 1], mine, bias_ss, bias_rs, 2 * m + upper, c)

    projected = dot(w_attend[...], normed_two, 0, 1)
    for h in range(HEADS):
        for part in range(3):
            rows = projected[128 * part + 32 * h : 128 * part + 32 * h + 32]
            if part == 0:
                rows = rows * (LOG2E / math.sqrt(HEAD_DIM))
            for g in range(4):
                qkv_send[4 * h + g, 32 * part : 32 * part + 32, :] = rows[
                    :, 128 * g : 128 * g + 128
                ].astype(BF16)
    qkv_recv[r] = qkv_send[r]

    for s in range(1, ROWS):
        to = (r + s) & (ROWS - 1)
        send(qkv_send.at[to], qkv_recv.at[r], qkv_ss, qkv_rs, to, c)

    gate_att[...] = jax.nn.sigmoid(projected[384:])

    wait(bias_recv, bias_rs)

    pieces = [
        jnp.concatenate([bias_recv[4 * a + b].astype(F32)[:8] for a in range(2)], 0)
        for b in range(4)
    ]
    for q, piece in enumerate(swap_blocks(pieces, 32)):
        for a in range(2):
            for v in range(4):
                bias_work[a, 4 * v + q : 4 * v + q + 1, :] = piece[8 * a + v : 8 * a + v + 1]
    for a in range(2):
        bias_all[half, c, :, 128 * a : 128 * a + 128] = bias_work[a].astype(BF16)

    for near in (0, 1, 7, 2, 6, 3, 5, 4):
        for t in range(ZS):
            if near or t:
                to = ((y + near) & (YS - 1)) * ZS + ((z + t) & (ZS - 1))
                part = bias_all.at[half, c]
                send(part, part, biasc_ss, biasc_rs.at[c >> 3], r, to)

    side = 1 - 2 * (y & 1)
    order = [((y >> 1) + 4 + apart) & 3 for apart in (0, -side, side, 2)]

    def hand_over(a, count=8):
        wait(bias_all.at[half, pl.ds(8 * a, count)], biasc_rs.at[a])
        part = bias_all.at[half, pl.ds(8 * a, 8)]
        send(part, part, pair_ss, pair_rs.at[half, a], r ^ 1, c)

    hand_over(order[0], 7)
    hand_over(order[1])

    wait(qkv_recv.at[pl.ds(0, ROWS - 1)], qkv_rs)

    tail = (lax.broadcasted_iota(jnp.int32, (16, 512), 0) == 0).astype(BF16)
    first = lax.broadcasted_iota(jnp.int32, (16, 128), 0) == 0
    for q in range(4):
        value_buf[q, 32:48, :] = tail
    for a in range(4):
        pieces = [qkv_recv[4 * a + b].astype(F32) for b in range(4)]
        for q, piece in enumerate(swap_blocks(pieces, 32)):
            query_buf[q, a, 0:32, :] = piece[:32].astype(BF16)
            query_buf[q, a, 32:48, :] = tail[:, :128]
            value_buf[q, 0:32, 128 * a : 128 * a + 128] = piece[64:].astype(BF16)
            present = mask_cols[q, :, 128 * a : 128 * a + 128]
            absent = jnp.concatenate([present, present], 0) < 0.5
            extra = jnp.where(jnp.logical_and(first, absent), MASKED, 0.0)
            keys = jnp.concatenate([piece[32:64], extra], 0)
            key_buf[q, 128 * a : 128 * a + 128, :] = keys.T.astype(BF16)

    for step, a in enumerate(order):
        if step < 2:
            hand_over(order[step + 2])
        wait(bias_all.at[1 - half, pl.ds(8 * a, 8)], pair_rs.at[1 - half, a])
        for s in range(2):
            block = bias_all[s, pl.ds(8 * a, 8)].astype(F32).reshape(128, 256) * LOG2E
            bias_full[256 * s : 256 * s + 256, :] = block.T
        pieces = []
        for q in range(4):
            scores = dot(key_buf[q], query_buf[q, a], 1, 0) + bias_full[...]
            weight = jnp.exp2(scores - jnp.max(scores, 0, keepdims=True)).astype(BF16)
            total = dot(value_buf[q], weight, 1, 0)
            pieces.append(total[:32] / total[32:33])
        for b, piece in enumerate(swap_blocks(pieces, 32)):
            at = 4 * a + b
            att_send[at] = piece.astype(BF16)

            @pl.when(r != at)
            def _():
                send(att_send.at[at], att_recv.at[r], att_ss, att_rs, at, c)

            @pl.when(r == at)
            def _():
                att_recv[r] = att_send[at]

    @pl.when(upper != half)
    def _():
        wait(bias_recv, bias_ss)

    @pl.when(upper == half)
    def _():
        wait(bias_recv.at[pl.ds(0, 7)], bias_ss)

    to_self = (2 * (r >> 1) + (z >> 1)) == r

    @pl.when(jnp.logical_not(to_self))
    def _():
        wait(tri_send, tri_ss)

    @pl.when(to_self)
    def _():
        wait(tri_send.at[pl.ds(0, YS - 1)], tri_ss)
        wait(tri_send.at[0, pl.ds(0, ZS - 1)], tri_ss)

    wait(qkv_send.at[pl.ds(0, ROWS - 1)], qkv_ss)
    wait(bias_all.at[half, pl.ds(0, YS * ZS - 1)], biasc_ss)
    wait(bias_all.at[half], pair_ss)
    wait(att_send.at[pl.ds(0, ROWS - 1)], att_ss)
    wait(att_recv.at[pl.ds(0, ROWS - 1)], att_rs)

    attended = jnp.concatenate(
        [
            jnp.concatenate([att_recv[4 * h + g].astype(F32) for g in range(4)], 1)
            for h in range(HEADS)
        ],
        0,
    )
    gated = (gate_att[...] * attended).astype(BF16)
    pair_two = (pair_one_t[...] + dot(gated, w_attend_out[...], 0, 0)).astype(BF16).astype(F32)
    normed_three = layer_norm(pair_two, gain_trans[...]).astype(BF16)
    for part in range(4):
        rows = slice(128 * part, 128 * part + 128)
        expanded = dot(normed_three[rows], w_trans_in[...], 1, 0)
        hidden = jnp.concatenate(
            [
                (
                    jax.nn.silu(expanded[t : t + 16, :512]) * expanded[t : t + 16, 512:]
                ).astype(BF16)
                for t in range(0, 128, 16)
            ],
            0,
        )
        work[rows, :] = pair_two[rows] + dot(hidden, w_trans_out[...], 1, 0)
    for i in range(32):
        out_ref[i] = work[pl.ds(i, 16, stride=32), :].astype(BF16)


def per_device(
    pair, pair_mask, gain_tri, w_left, w_right, w_tri_gate, gain_mid, w_tri_out, gain_att, w_attend,
    w_bias, w_attend_out, gain_trans, w_trans_in, w_trans_out,
):
    vmem = pl.BlockSpec(memory_space=pltpu.VMEM)
    dma = pltpu.SemaphoreType.DMA
    row = lambda gain: gain.reshape(1, 128)
    return pl.pallas_call(
        kernel,
        out_shape=pltpu.VMEM((32, 16, 128), BF16),
        in_specs=[pl.BlockSpec(memory_space=pltpu.HBM)] * 15,
        out_specs=vmem,
        scratch_shapes=[
            pltpu.VMEM((32, 16, 128), BF16),
            pltpu.VMEM((16, 32), jnp.int32),
            pltpu.VMEM((1, 128), F32),
            pltpu.VMEM((128, 256), BF16),
            pltpu.VMEM((128, 256), BF16),
            pltpu.VMEM((128, 128), BF16),
            pltpu.VMEM((1, 128), F32),
            pltpu.VMEM((128, 128), BF16),
            pltpu.VMEM((1, 128), F32),
            pltpu.VMEM((128, 512), BF16),
            pltpu.VMEM((4, 128), BF16),
            pltpu.VMEM((128, 128), BF16),
            pltpu.VMEM((1, 128), F32),
            pltpu.VMEM((128, 1024), BF16),
            pltpu.VMEM((512, 128), BF16),
            dma((15,)),
            pltpu.VMEM((512, 128), F32),
            pltpu.VMEM((16, 16, 512), BF16),
            pltpu.VMEM((16, 16, 512), BF16),
            pltpu.VMEM((4, 256, 128), F32),
            pltpu.VMEM((ZS, 8, 16, 512), BF16),
            pltpu.VMEM((YS, 8, 16, 512), BF16),
            pltpu.VMEM((512, 128), F32),
            pltpu.VMEM((512, 128), F32),
            pltpu.VMEM((YS, ZS, 16, 128), BF16),
            pltpu.VMEM((2, 16, 16, 128), BF16),
            pltpu.VMEM((16, 16, 128), BF16),
            pltpu.VMEM((16, 16, 128), BF16),
            pltpu.VMEM((4, 16, 128), BF16),
            pltpu.VMEM((8, 16, 128), BF16),
            pltpu.VMEM((2, 16, 128), F32),
            pltpu.VMEM((2, YS * ZS, 16, 256), BF16),
            pltpu.VMEM((512, 128), F32),
            pltpu.VMEM((4, 8, 512), F32),
            pltpu.VMEM((512, 128), F32),
            pltpu.VMEM((128, 512), F32),
            pltpu.VMEM((16, 96, 128), BF16),
            pltpu.VMEM((16, 96, 128), BF16),
            pltpu.VMEM((4, 4, 48, 128), BF16),
            pltpu.VMEM((4, 512, 48), BF16),
            pltpu.VMEM((4, 48, 512), BF16),
            pltpu.VMEM((16, 32, 128), BF16),
            pltpu.VMEM((16, 32, 128), BF16),
            dma(()), dma(()),
            dma(()), dma((2, 3, 2)),
            dma(()), dma((2, 5, 4)),
            dma(()), dma(()),
            dma(()), dma(()),
            dma(()), dma((4,)),
            dma(()), dma((2, 4)),
            dma(()), dma(()),
            dma(()), dma(()),
            dma(()), dma(()),
        ],
        compiler_params=pltpu.CompilerParams(
            collective_id=0, has_side_effects=True, vmem_limit_bytes=VMEM_LIMIT
        ),
    )(
        pair, pair_mask.T, row(gain_tri), w_left, w_right, w_tri_gate, row(gain_mid),
        w_tri_out, row(gain_att), w_attend, w_bias.T, w_attend_out, row(gain_trans), w_trans_in,
        w_trans_out,
    )


def solution(mesh):
    in_specs = (P("row", "col", None), P("row", "col")) + (P(),) * 13
    return jax.shard_map(
        per_device, mesh=mesh, in_specs=in_specs, out_specs=P("row", "col", None), check_vma=False
    )
```

```python
import functools
import math

import jax
import jax.numpy as jnp
from jax import lax
from jax.experimental import pallas as pl
from jax.experimental.pallas import tpu as pltpu
from jax.sharding import PartitionSpec as P

HEADS = 4
HEAD_DIM = 32
EPS = 1e-05
MASKED = -1e30
LOG2E = math.log2(math.e)
ROWS = 16
YS = 8
ZS = 4
VMEM_LIMIT = 63 * 1024 * 1024
MESH = pl.DeviceIdType.MESH
F32 = jnp.float32
BF16 = jnp.bfloat16


def dot(lhs, rhs, lhs_dim, rhs_dim):
    return lax.dot_general(
        lhs, rhs, (((lhs_dim,), (rhs_dim,)), ((), ())), preferred_element_type=F32
    )


def layer_norm(inputs, gain_vec, axis=-1):
    center = inputs - jnp.mean(inputs, axis, keepdims=True)
    spread = jnp.mean(center * center, axis, keepdims=True)
    return center * lax.rsqrt(spread + EPS) * gain_vec


def swap_blocks(arrays, width):
    arrays = list(arrays)
    lane = lax.broadcasted_iota(jnp.int32, arrays[0].shape, 1)
    step = 1
    while step < len(arrays):
        shift = width * step
        odd = (lane & shift) != 0
        fresh = list(arrays)
        for low in range(len(arrays)):
            if low & step == 0:
                high = low | step
                fresh[low] = jnp.where(odd, pltpu.roll(arrays[high], shift, 1), arrays[low])
                fresh[high] = jnp.where(odd, arrays[high], pltpu.roll(arrays[low], 128 - shift, 1))
        arrays = fresh
        step *= 2
    return arrays


def kernel(
    pair_hbm, mask_hbm, gain_tri_hbm, w_left_hbm, w_right_hbm, w_tri_gate_hbm, gain_mid_hbm,
    w_tri_out_hbm, gain_att_hbm, w_attend_hbm, w_bias_hbm, w_attend_out_hbm, gain_trans_hbm,
    w_trans_in_hbm, w_trans_out_hbm,
    out_ref,
    pair_ref, mask_ref, gain_tri, w_left, w_right, w_tri_gate, gain_mid, w_tri_out, gain_att,
    w_attend, w_bias, w_attend_out, gain_trans, w_trans_in, w_trans_out, load_sems,
    work, edge_send, edge_recv, edge_work, near_all, far_all, gate_tri, tri_work, tri_send,
    tri_recv, mask_send, mask_recv, bias_send, bias_recv, bias_work, bias_all, bias_full, mask_cols, pair_one_t, gate_att,
    qkv_send, qkv_recv, query_buf, key_buf, value_buf, att_send, att_recv,
    edge_ss, edge_rs, near_ss, near_rs, far_ss, far_rs, tri_ss, tri_rs, bias_ss, bias_rs,
    biasc_ss, biasc_rs, pair_ss, pair_rs, mask_ss, mask_rs, qkv_ss, qkv_rs, att_ss, att_rs,
):
    r = lax.axis_index("row")
    c = lax.axis_index("col")
    y = c >> 2
    z = c & (ZS - 1)
    up = ((y + 1) & (YS - 1)) * ZS + z
    down = ((y + YS - 1) & (YS - 1)) * ZS + z

    def send(src, dst, ssem, rsem, row, col):
        pltpu.make_async_remote_copy(
            src_ref=src, dst_ref=dst, send_sem=ssem, recv_sem=rsem,
            device_id=(row, col), device_id_type=MESH,
        ).start()

    def wait(ref, sem):
        pltpu.make_async_copy(ref, ref, sem).wait()

    loads = [
        pltpu.make_async_copy(src, dst, load_sems.at[at])
        for at, (src, dst) in enumerate(
            [
                (pair_hbm, pair_ref), (gain_tri_hbm, gain_tri), (mask_hbm, mask_ref),
                (w_left_hbm, w_left), (w_right_hbm, w_right), (w_tri_gate_hbm, w_tri_gate),
                (gain_mid_hbm, gain_mid), (w_tri_out_hbm, w_tri_out), (gain_att_hbm, gain_att),
                (w_bias_hbm, w_bias), (w_attend_hbm, w_attend), (w_attend_out_hbm, w_attend_out),
                (gain_trans_hbm, gain_trans), (w_trans_in_hbm, w_trans_in),
                (w_trans_out_hbm, w_trans_out),
            ]
        )
    ]
    for load in loads[:5]:
        load.start()

    barrier = pltpu.get_barrier_semaphore()

    def hello(row, col):
        pl.semaphore_signal(barrier, inc=1, device_id=(row, col), device_id_type=MESH)

    @pl.loop(1, ROWS)
    def _(s):
        hello((r + s) & (ROWS - 1), c)

    @pl.loop(1, ZS)
    def _(s):
        hello(r, y * ZS + ((z + s) & (ZS - 1)))

    hello(r, up)
    hello(r, down)

    for load in loads[5:]:
        load.start()

    for load in loads[:5]:
        load.wait()
    work[...] = pair_ref[...].astype(F32).reshape(512, 128)
    pair_t = jnp.concatenate([work[pl.ds(j, 32, stride=16), :] for j in range(16)], 0)
    pair_one_t[...] = pair_t
    normed_t = layer_norm(pair_t, gain_tri[...]).astype(BF16)
    lane = lax.broadcasted_iota(jnp.int32, (32, 512), 1)
    spread = lax.broadcasted_iota(jnp.int32, (32, 512), 0) == (lane & 31)
    mask = dot(mask_ref[...].astype(F32).astype(BF16), spread.astype(F32).astype(BF16), 1, 0)
    lane = lax.broadcasted_iota(jnp.int32, (16, 512), 1)
    own = lax.broadcasted_iota(jnp.int32, (16, 512), 0) == (lane >> 5)
    mask = jnp.sum(jnp.where(own, mask, 0.0), 0, keepdims=True)
    sides = []
    for weight in (w_right, w_left):
        projected = dot(weight[...], normed_t, 0, 1)
        sides.append((mask * jax.nn.sigmoid(projected[:128]) * projected[128:]).reshape(ROWS, 8, 512))
    edge_send[...] = jnp.concatenate(sides, 1).astype(BF16)
    pl.semaphore_wait(barrier, (ROWS - 1) + (ZS - 1) + 2)

    for s in range(1, ROWS):
        to = (r + s) & (ROWS - 1)
        send(edge_send.at[to], edge_recv.at[r], edge_ss, edge_rs, to, c)
    edge_recv[r] = edge_send[r]

    for load in loads[5:]:
        load.wait()
    gate_tri[...] = jax.nn.sigmoid(dot(normed_t, w_tri_gate[...], 1, 0))

    wait(edge_recv.at[pl.ds(0, ROWS - 1)], edge_rs)

    for v in range(4):
        pieces = [
            jnp.concatenate(
                [edge_recv[4 * a + b, :, 128 * v : 128 * v + 128].astype(F32) for a in range(4)], 0
            )
            for b in range(4)
        ]
        for q, piece in enumerate(swap_blocks(pieces, 32)):
            for a in range(4):
                edge_work.at[a][pl.ds(4 * v + q, 16, stride=16), :] = piece[16 * a : 16 * a + 16]
    for a in range(4):
        block = edge_work[a].astype(BF16).reshape(2, 8, 16, 128)
        near_all[z, :, :, 128 * a : 128 * a + 128] = block[0]
        far_all[y, :, :, 128 * a : 128 * a + 128] = block[1]

    class Ring:
        def __init__(self, buf, ss, rs, size, me, to, pieces):
            self.buf, self.ss, self.rs, self.size, self.me, self.to = buf, ss, rs, size, me, to
            self.pieces, self.extent = pieces, buf.shape[1] // pieces

        def part(self, block, chunk):
            at = block & (self.size - 1)
            return self.buf.at[at, pl.ds(chunk * self.extent, self.extent)]

        def takes(self, step, chunk, way):
            return step < self.size // 2 or 2 * chunk // self.pieces == way

        def send(self, step, chunk, way):
            block = self.me + self.size - step + 1 if way == 0 else self.me + step - 1
            part = self.part(block, chunk)
            row, col = self.to[way]
            send(part, part, self.ss, self.rs.at[way, step, chunk], row, col)

        def land(self, step, chunk, way):
            block = self.me + self.size - step if way == 0 else self.me + step
            wait(self.part(block, chunk), self.rs.at[way, step, chunk])

        def each(self, step, chunks=None):
            for chunk in range(self.pieces) if chunks is None else chunks:
                for way in range(2):
                    if self.takes(step, chunk, way):
                        yield chunk, way

        def start(self):
            for chunk, way in self.each(1):
                self.send(1, chunk, way)

        def turn(self, step, chunks=None):
            for chunk, way in self.each(step, chunks):
                self.land(step, chunk, way)
                if step < self.size // 2 and self.takes(step + 1, chunk, way):
                    self.send(step + 1, chunk, way)

        def sent(self):
            wait(self.buf.at[pl.ds(0, self.size - 1)], self.ss)

    y_ring = ((r, up), (r, down))
    far_ring = Ring(far_all, far_ss, far_rs, YS, y, y_ring, 2)
    near_ring = Ring(
        near_all, near_ss, near_rs, ZS, z,
        ((r, y * ZS + ((z + 1) & (ZS - 1))), (r, y * ZS + ((z + ZS - 1) & (ZS - 1)))),
        2,
    )
    far_ring.start()
    near_ring.start()
    sub = lax.broadcasted_iota(jnp.int32, (16, 128), 0)
    for g in range(4):
        part = jnp.broadcast_to(mask[:, 128 * g : 128 * g + 128], (16, 128)).astype(BF16)
        for h in range(HEADS):
            mask_send[4 * h + g] = part
    mask_recv[r] = mask_send[r]

    for s in range(1, ROWS):
        to = (r + s) & (ROWS - 1)
        send(mask_send.at[to], mask_recv.at[r], mask_ss, mask_rs, to, c)

    far_ring.turn(1)
    near_ring.turn(1, (0,))
    far_ring.turn(2)
    near_ring.turn(1, (1,))

    wait(mask_recv.at[pl.ds(0, ROWS - 1)], mask_rs)

    pieces = [
        jnp.concatenate([mask_recv[4 * a + b].astype(F32)[:8] for a in range(4)], 0)
        for b in range(4)
    ]
    for q, piece in enumerate(swap_blocks(pieces, 32)):
        for a in range(4):
            mask_cols[q, :, 128 * a : 128 * a + 128] = piece[8 * a : 8 * a + 8]

    far_ring.turn(3)
    near_ring.turn(2)
    def reply(slot, piece):
        yy = (y + YS + slot - 3) & (YS - 1)
        tri_send[yy] = piece.astype(BF16).reshape(ZS, 16, 128)
        row = 2 * yy + (z >> 1)
        half = z & 1
        for t in (1, 2, 3):
            zz = (z + t) & (ZS - 1)
            send(
                tri_send.at[yy, zz], tri_recv.at[half, r], tri_ss, tri_rs,
                row, y * ZS + zz,
            )

    def reply_here(slot):
        yy = (y + YS + slot - 3) & (YS - 1)
        row = 2 * yy + (z >> 1)
        half = z & 1

        @pl.when(row != r)
        def _():
            send(
                tri_send.at[yy, z], tri_recv.at[half, r], tri_ss, tri_rs,
                row, c,
            )

        @pl.when(row == r)
        def _():
            pltpu.make_async_copy(tri_send.at[yy, z], tri_recv.at[half, r], tri_rs).start()

    def products(slots):
        for ch in range(8):
            rights = jnp.concatenate([near_all[s, ch] for s in range(ZS)], 0)
            lefts = [far_all[(y + YS + s - 3) & (YS - 1), ch] for s in slots]
            found = dot(rights, jnp.concatenate(lefts, 0), 1, 1)
            tri_work[64 * ch : 64 * ch + 64, 0 : 16 * len(lefts)] = found
        return [
            jnp.concatenate([tri_work[pl.ds(8 * g + m, 8, stride=64), :] for g in range(8)], 0)
            for m in range(8)
        ]

    tri_work[...] = jnp.zeros_like(tri_work)
    pieces = swap_blocks(products(range(7)), 16)
    for slot in (2, 4, 1, 5, 0, 6, 3):
        reply(slot, pieces[slot])
    for slot in (2, 4, 1, 5, 0, 6, 3):
        reply_here(slot)
    far_ring.turn(4)
    pieces = products([7])
    lane = lax.broadcasted_iota(jnp.int32, pieces[0].shape, 1) >> 4
    merged = pieces[0]
    for m in range(1, 8):
        merged = jnp.where(lane == m, pltpu.roll(pieces[m], 16 * m, 1), merged)
    reply(7, merged)
    reply_here(7)

    wait(edge_send.at[pl.ds(0, ROWS - 1)], edge_ss)
    wait(mask_send.at[pl.ds(0, ROWS - 1)], mask_ss)
    far_ring.sent()
    near_ring.sent()
    wait(tri_recv, tri_rs)

    tri_t = jnp.concatenate(
        [
            tri_recv[half].astype(F32)[:, 8 * g : 8 * g + 8].reshape(128, 128)
            for half in range(2)
            for g in range(2)
        ],
        1,
    )
    gain_col = jnp.broadcast_to(gain_mid[...], (128, 128)).T
    tri_normed = layer_norm(tri_t, jnp.concatenate([gain_col] * 4, 1), 0).astype(BF16)
    update = dot(tri_normed, w_tri_out[...], 0, 0)
    update = jnp.concatenate(
        [
            update[256 * half + 16 * j : 256 * half + 16 * j + 16]
            for j in range(16)
            for half in range(2)
        ],
        0,
    )
    pair_t = (pair_one_t[...] + gate_tri[...] * update).astype(BF16).astype(F32)
    pair_one_t[...] = pair_t

    normed_two = layer_norm(pair_t, gain_att[...]).astype(BF16)
    bias_t = dot(w_bias[...], normed_two, 1, 1)
    for h in range(HEADS):
        base = jnp.zeros((16, 128), F32)
        for v in range(4):
            base = jnp.where(
                sub == v,
                jnp.broadcast_to(bias_t[h : h + 1, 128 * v : 128 * v + 128], (16, 128)),
                base,
            )
        bias_send[h] = base.astype(BF16)
    upper = r >> 3
    half = r & 1

    own = bias_send.at[r >> 2]
    mine = bias_recv.at[r & 7]

    @pl.when(upper != half)
    def _():
        send(own, mine, bias_ss, bias_rs, r ^ 1, c)

    @pl.when(upper == half)
    def _():
        pltpu.make_async_copy(own, mine, bias_rs).start()

    for s in range(1, 8):
        m = ((r >> 1) + s) & 7
        send(bias_send.at[m >> 1], mine, bias_ss, bias_rs, 2 * m + upper, c)

    projected = dot(w_attend[...], normed_two, 0, 1)
    for h in range(HEADS):
        for part in range(3):
            rows = projected[128 * part + 32 * h : 128 * part + 32 * h + 32]
            if part == 0:
                rows = rows * (LOG2E / math.sqrt(HEAD_DIM))
            for g in range(4):
                qkv_send[4 * h + g, 32 * part : 32 * part + 32, :] = rows[
                    :, 128 * g : 128 * g + 128
                ].astype(BF16)
    for s in range(1, ROWS):
        to = (r + s) & (ROWS - 1)
        send(qkv_send.at[to], qkv_recv.at[r], qkv_ss, qkv_rs, to, c)
    qkv_recv[r] = qkv_send[r]

    gate_att[...] = jax.nn.sigmoid(projected[384:])

    wait(bias_recv, bias_rs)

    pieces = [
        jnp.concatenate([bias_recv[4 * a + b].astype(F32)[:8] for a in range(2)], 0)
        for b in range(4)
    ]
    for q, piece in enumerate(swap_blocks(pieces, 32)):
        for a in range(2):
            for v in range(4):
                bias_work[a, 4 * v + q : 4 * v + q + 1, :] = piece[8 * a + v : 8 * a + v + 1]
    for a in range(2):
        bias_all[half, c, :, 128 * a : 128 * a + 128] = bias_work[a].astype(BF16)

    for near in (0, 1, 7, 2, 6, 3, 5, 4):
        for t in range(ZS):
            if near or t:
                to = ((y + near) & (YS - 1)) * ZS + ((z + t) & (ZS - 1))
                part = bias_all.at[half, c]
                send(part, part, biasc_ss, biasc_rs.at[c >> 3], r, to)

    side = 1 - 2 * (y & 1)
    order = [((y >> 1) + 4 + apart) & 3 for apart in (0, -side, side, 2)]

    def hand_over(a, count=8):
        wait(bias_all.at[half, pl.ds(8 * a, count)], biasc_rs.at[a])
        part = bias_all.at[half, pl.ds(8 * a, 8)]
        send(part, part, pair_ss, pair_rs.at[half, a], r ^ 1, c)

    hand_over(order[0], 7)
    hand_over(order[1])

    wait(qkv_recv.at[pl.ds(0, ROWS - 1)], qkv_rs)

    tail = (lax.broadcasted_iota(jnp.int32, (16, 512), 0) == 0).astype(BF16)
    first = lax.broadcasted_iota(jnp.int32, (16, 128), 0) == 0
    for q in range(4):
        value_buf[q, 32:48, :] = tail
    for a in range(4):
        pieces = [qkv_recv[4 * a + b].astype(F32) for b in range(4)]
        for q, piece in enumerate(swap_blocks(pieces, 32)):
            query_buf[q, a, 0:32, :] = piece[:32].astype(BF16)
            query_buf[q, a, 32:48, :] = tail[:, :128]
            value_buf[q, 0:32, 128 * a : 128 * a + 128] = piece[64:].astype(BF16)
            present = mask_cols[q, :, 128 * a : 128 * a + 128]
            absent = jnp.concatenate([present, present], 0) < 0.5
            extra = jnp.where(jnp.logical_and(first, absent), MASKED, 0.0)
            keys = jnp.concatenate([piece[32:64], extra], 0)
            key_buf[q, 128 * a : 128 * a + 128, :] = keys.T.astype(BF16)

    for step, a in enumerate(order):
        wait(bias_all.at[1 - half, pl.ds(8 * a, 8)], pair_rs.at[1 - half, a])
        for s in range(2):
            block = bias_all[s, pl.ds(8 * a, 8)].astype(F32).reshape(128, 256) * LOG2E
            bias_full[256 * s : 256 * s + 256, :] = block.T
        pieces = []
        for q in range(4):
            scores = dot(key_buf[q], query_buf[q, a], 1, 0) + bias_full[...]
            weight = jnp.exp2(scores - jnp.max(scores, 0, keepdims=True)).astype(BF16)
            total = dot(value_buf[q], weight, 1, 0)
            pieces.append(total[:32] / total[32:33])
        for b, piece in enumerate(swap_blocks(pieces, 32)):
            att_send[4 * a + b] = piece.astype(BF16)
        for t in (1, 2, 3):
            at = 4 * a + ((r + t) & 3)
            send(att_send.at[at], att_recv.at[r], att_ss, att_rs, at, c)
        at = 4 * a + (r & 3)

        @pl.when(r != at)
        def _():
            send(att_send.at[at], att_recv.at[r], att_ss, att_rs, at, c)

        @pl.when(r == at)
        def _():
            att_recv[r] = att_send[at]

        if step < 2:
            hand_over(order[step + 2])

    @pl.when(upper != half)
    def _():
        wait(bias_recv, bias_ss)

    @pl.when(upper == half)
    def _():
        wait(bias_recv.at[pl.ds(0, 7)], bias_ss)

    to_self = (2 * (r >> 1) + (z >> 1)) == r

    @pl.when(jnp.logical_not(to_self))
    def _():
        wait(tri_send, tri_ss)

    @pl.when(to_self)
    def _():
        wait(tri_send.at[pl.ds(0, YS - 1)], tri_ss)
        wait(tri_send.at[0, pl.ds(0, ZS - 1)], tri_ss)

    wait(qkv_send.at[pl.ds(0, ROWS - 1)], qkv_ss)
    wait(bias_all.at[half, pl.ds(0, YS * ZS - 1)], biasc_ss)
    wait(bias_all.at[half], pair_ss)
    wait(att_send.at[pl.ds(0, ROWS - 1)], att_ss)
    wait(att_recv.at[pl.ds(0, ROWS - 1)], att_rs)

    attended = jnp.concatenate(
        [
            jnp.concatenate([att_recv[4 * h + g].astype(F32) for g in range(4)], 1)
            for h in range(HEADS)
        ],
        0,
    )
    gated = (gate_att[...] * attended).astype(BF16)
    pair_two = (pair_one_t[...] + dot(gated, w_attend_out[...], 0, 0)).astype(BF16).astype(F32)
    normed_three = layer_norm(pair_two, gain_trans[...]).astype(BF16)
    for part in range(4):
        rows = slice(128 * part, 128 * part + 128)
        expanded = dot(normed_three[rows], w_trans_in[...], 1, 0)
        hidden = jnp.concatenate(
            [
                (
                    jax.nn.silu(expanded[t : t + 16, :512]) * expanded[t : t + 16, 512:]
                ).astype(BF16)
                for t in range(0, 128, 16)
            ],
            0,
        )
        work[rows, :] = pair_two[rows] + dot(hidden, w_trans_out[...], 1, 0)
    for i in range(32):
        out_ref[i] = work[pl.ds(i, 16, stride=32), :].astype(BF16)


def per_device(
    pair, pair_mask, gain_tri, w_left, w_right, w_tri_gate, gain_mid, w_tri_out, gain_att, w_attend,
    w_bias, w_attend_out, gain_trans, w_trans_in, w_trans_out,
):
    vmem = pl.BlockSpec(memory_space=pltpu.VMEM)
    dma = pltpu.SemaphoreType.DMA
    row = lambda gain: gain.reshape(1, 128)
    return pl.pallas_call(
        kernel,
        out_shape=pltpu.VMEM((32, 16, 128), BF16),
        in_specs=[pl.BlockSpec(memory_space=pltpu.HBM)] * 15,
        out_specs=vmem,
        scratch_shapes=[
            pltpu.VMEM((32, 16, 128), BF16),
            pltpu.VMEM((16, 32), jnp.int32),
            pltpu.VMEM((1, 128), F32),
            pltpu.VMEM((128, 256), BF16),
            pltpu.VMEM((128, 256), BF16),
            pltpu.VMEM((128, 128), BF16),
            pltpu.VMEM((1, 128), F32),
            pltpu.VMEM((128, 128), BF16),
            pltpu.VMEM((1, 128), F32),
            pltpu.VMEM((128, 512), BF16),
            pltpu.VMEM((4, 128), BF16),
            pltpu.VMEM((128, 128), BF16),
            pltpu.VMEM((1, 128), F32),
            pltpu.VMEM((128, 1024), BF16),
            pltpu.VMEM((512, 128), BF16),
            dma((15,)),
            pltpu.VMEM((512, 128), F32),
            pltpu.VMEM((16, 16, 512), BF16),
            pltpu.VMEM((16, 16, 512), BF16),
            pltpu.VMEM((4, 256, 128), F32),
            pltpu.VMEM((ZS, 8, 16, 512), BF16),
            pltpu.VMEM((YS, 8, 16, 512), BF16),
            pltpu.VMEM((512, 128), F32),
            pltpu.VMEM((512, 128), F32),
            pltpu.VMEM((YS, ZS, 16, 128), BF16),
            pltpu.VMEM((2, 16, 16, 128), BF16),
            pltpu.VMEM((16, 16, 128), BF16),
            pltpu.VMEM((16, 16, 128), BF16),
            pltpu.VMEM((4, 16, 128), BF16),
            pltpu.VMEM((8, 16, 128), BF16),
            pltpu.VMEM((2, 16, 128), F32),
            pltpu.VMEM((2, YS * ZS, 16, 256), BF16),
            pltpu.VMEM((512, 128), F32),
            pltpu.VMEM((4, 8, 512), F32),
            pltpu.VMEM((512, 128), F32),
            pltpu.VMEM((128, 512), F32),
            pltpu.VMEM((16, 96, 128), BF16),
            pltpu.VMEM((16, 96, 128), BF16),
            pltpu.VMEM((4, 4, 48, 128), BF16),
            pltpu.VMEM((4, 512, 48), BF16),
            pltpu.VMEM((4, 48, 512), BF16),
            pltpu.VMEM((16, 32, 128), BF16),
            pltpu.VMEM((16, 32, 128), BF16),
            dma(()), dma(()),
            dma(()), dma((2, 3, 2)),
            dma(()), dma((2, 5, 2)),
            dma(()), dma(()),
            dma(()), dma(()),
            dma(()), dma((4,)),
            dma(()), dma((2, 4)),
            dma(()), dma(()),
            dma(()), dma(()),
            dma(()), dma(()),
        ],
        compiler_params=pltpu.CompilerParams(
            collective_id=0, has_side_effects=True, vmem_limit_bytes=VMEM_LIMIT
        ),
    )(
        pair, pair_mask.T, row(gain_tri), w_left, w_right, w_tri_gate, row(gain_mid),
        w_tri_out, row(gain_att), w_attend, w_bias.T, w_attend_out, row(gain_trans), w_trans_in,
        w_trans_out,
    )


def solution(mesh):
    in_specs = (P("row", "col", None), P("row", "col")) + (P(),) * 13
    return jax.shard_map(
        per_device, mesh=mesh, in_specs=in_specs, out_specs=P("row", "col", None), check_vma=False
    )
```

```python
import functools
import math

import jax
import jax.numpy as jnp
from jax import lax
from jax.experimental import pallas as pl
from jax.experimental.pallas import tpu as pltpu
from jax.sharding import PartitionSpec as P

HEADS = 4
HEAD_DIM = 32
EPS = 1e-05
MASKED = -1e30
LOG2E = math.log2(math.e)
ROWS = 16
YS = 8
ZS = 4
VMEM_LIMIT = 63 * 1024 * 1024
MESH = pl.DeviceIdType.MESH
F32 = jnp.float32
BF16 = jnp.bfloat16


def dot(lhs, rhs, lhs_dim, rhs_dim):
    return lax.dot_general(
        lhs, rhs, (((lhs_dim,), (rhs_dim,)), ((), ())), preferred_element_type=F32
    )


def layer_norm(inputs, gain_vec, axis=-1):
    center = inputs - jnp.mean(inputs, axis, keepdims=True)
    spread = jnp.mean(center * center, axis, keepdims=True)
    return center * lax.rsqrt(spread + EPS) * gain_vec


def swap_blocks(arrays, width):
    arrays = list(arrays)
    lane = lax.broadcasted_iota(jnp.int32, arrays[0].shape, 1)
    step = 1
    while step < len(arrays):
        shift = width * step
        odd = (lane & shift) != 0
        fresh = list(arrays)
        for low in range(len(arrays)):
            if low & step == 0:
                high = low | step
                fresh[low] = jnp.where(odd, pltpu.roll(arrays[high], shift, 1), arrays[low])
                fresh[high] = jnp.where(odd, arrays[high], pltpu.roll(arrays[low], 128 - shift, 1))
        arrays = fresh
        step *= 2
    return arrays


def kernel(
    pair_hbm, mask_hbm, gain_tri_hbm, w_left_hbm, w_right_hbm, w_tri_gate_hbm, gain_mid_hbm,
    w_tri_out_hbm, gain_att_hbm, w_attend_hbm, w_bias_hbm, w_attend_out_hbm, gain_trans_hbm,
    w_trans_in_hbm, w_trans_out_hbm,
    out_ref,
    pair_ref, mask_ref, gain_tri, w_left, w_right, w_tri_gate, gain_mid, w_tri_out, gain_att,
    w_attend, w_bias, w_attend_out, gain_trans, w_trans_in, w_trans_out, load_sems,
    work, edge_send, edge_recv, edge_work, near_all, far_all, gate_tri, tri_work, tri_send,
    tri_recv, mask_send, mask_recv, bias_send, bias_recv, bias_work, bias_all, bias_full, mask_cols, pair_one_t, gate_att,
    qkv_send, qkv_recv, query_buf, key_buf, value_buf, att_send, att_recv,
    edge_ss, edge_rs, near_ss, near_rs, far_ss, far_rs, tri_ss, tri_rs, bias_ss, bias_rs,
    biasz_ss, biasz_rs, biasc_ss, biasc_rs, pair_ss, pair_rs, mask_ss, mask_rs, qkv_ss, qkv_rs, att_ss, att_rs,
):
    r = lax.axis_index("row")
    c = lax.axis_index("col")
    y = c >> 2
    z = c & (ZS - 1)
    up = ((y + 1) & (YS - 1)) * ZS + z
    down = ((y + YS - 1) & (YS - 1)) * ZS + z

    def send(src, dst, ssem, rsem, row, col):
        pltpu.make_async_remote_copy(
            src_ref=src, dst_ref=dst, send_sem=ssem, recv_sem=rsem,
            device_id=(row, col), device_id_type=MESH,
        ).start()

    def wait(ref, sem):
        pltpu.make_async_copy(ref, ref, sem).wait()

    loads = [
        pltpu.make_async_copy(src, dst, load_sems.at[at])
        for at, (src, dst) in enumerate(
            [
                (pair_hbm, pair_ref), (gain_tri_hbm, gain_tri), (mask_hbm, mask_ref),
                (w_left_hbm, w_left), (w_right_hbm, w_right), (w_tri_gate_hbm, w_tri_gate),
                (gain_mid_hbm, gain_mid), (w_tri_out_hbm, w_tri_out), (gain_att_hbm, gain_att),
                (w_bias_hbm, w_bias), (w_attend_hbm, w_attend), (w_attend_out_hbm, w_attend_out),
                (gain_trans_hbm, gain_trans), (w_trans_in_hbm, w_trans_in),
                (w_trans_out_hbm, w_trans_out),
            ]
        )
    ]
    for load in loads[:5]:
        load.start()

    barrier = pltpu.get_barrier_semaphore()

    def hello(row, col):
        pl.semaphore_signal(barrier, inc=1, device_id=(row, col), device_id_type=MESH)

    @pl.loop(1, ROWS)
    def _(s):
        hello((r + s) & (ROWS - 1), c)

    @pl.loop(1, ZS)
    def _(s):
        hello(r, y * ZS + ((z + s) & (ZS - 1)))

    hello(r, up)
    hello(r, down)

    for load in loads[5:]:
        load.start()

    for load in loads[:5]:
        load.wait()
    work[...] = pair_ref[...].astype(F32).reshape(512, 128)
    pair_t = jnp.concatenate([work[pl.ds(j, 32, stride=16), :] for j in range(16)], 0)
    pair_one_t[...] = pair_t
    normed_t = layer_norm(pair_t, gain_tri[...]).astype(BF16)
    lane = lax.broadcasted_iota(jnp.int32, (32, 512), 1)
    spread = lax.broadcasted_iota(jnp.int32, (32, 512), 0) == (lane & 31)
    mask = dot(mask_ref[...].astype(F32).astype(BF16), spread.astype(F32).astype(BF16), 1, 0)
    lane = lax.broadcasted_iota(jnp.int32, (16, 512), 1)
    own = lax.broadcasted_iota(jnp.int32, (16, 512), 0) == (lane >> 5)
    mask = jnp.sum(jnp.where(own, mask, 0.0), 0, keepdims=True)
    sides = []
    for weight in (w_right, w_left):
        projected = dot(weight[...], normed_t, 0, 1)
        sides.append((mask * jax.nn.sigmoid(projected[:128]) * projected[128:]).reshape(ROWS, 8, 512))
    edge_send[...] = jnp.concatenate(sides, 1).astype(BF16)
    pl.semaphore_wait(barrier, (ROWS - 1) + (ZS - 1) + 2)

    for s in range(1, ROWS):
        to = (r + s) & (ROWS - 1)
        send(edge_send.at[to], edge_recv.at[r], edge_ss, edge_rs, to, c)
    edge_recv[r] = edge_send[r]

    for load in loads[5:]:
        load.wait()
    gate_tri[...] = jax.nn.sigmoid(dot(normed_t, w_tri_gate[...], 1, 0))

    wait(edge_recv.at[pl.ds(0, ROWS - 1)], edge_rs)

    for v in range(4):
        pieces = [
            jnp.concatenate(
                [edge_recv[4 * a + b, :, 128 * v : 128 * v + 128].astype(F32) for a in range(4)], 0
            )
            for b in range(4)
        ]
        for q, piece in enumerate(swap_blocks(pieces, 32)):
            for a in range(4):
                edge_work.at[a][pl.ds(4 * v + q, 16, stride=16), :] = piece[16 * a : 16 * a + 16]
    for a in range(4):
        block = edge_work[a].astype(BF16).reshape(2, 8, 16, 128)
        near_all[z, :, :, 128 * a : 128 * a + 128] = block[0]
        far_all[y, :, :, 128 * a : 128 * a + 128] = block[1]

    class Ring:
        def __init__(self, buf, ss, rs, size, me, to, pieces):
            self.buf, self.ss, self.rs, self.size, self.me, self.to = buf, ss, rs, size, me, to
            self.pieces, self.extent = pieces, buf.shape[1] // pieces

        def part(self, block, chunk):
            at = block & (self.size - 1)
            return self.buf.at[at, pl.ds(chunk * self.extent, self.extent)]

        def takes(self, step, chunk, way):
            return step < self.size // 2 or 2 * chunk // self.pieces == way

        def send(self, step, chunk, way):
            block = self.me + self.size - step + 1 if way == 0 else self.me + step - 1
            part = self.part(block, chunk)
            row, col = self.to[way]
            send(part, part, self.ss, self.rs.at[way, step, chunk], row, col)

        def land(self, step, chunk, way):
            block = self.me + self.size - step if way == 0 else self.me + step
            wait(self.part(block, chunk), self.rs.at[way, step, chunk])

        def each(self, step, chunks=None):
            for chunk in range(self.pieces) if chunks is None else chunks:
                for way in range(2):
                    if self.takes(step, chunk, way):
                        yield chunk, way

        def start(self):
            for chunk, way in self.each(1):
                self.send(1, chunk, way)

        def turn(self, step, chunks=None):
            for chunk, way in self.each(step, chunks):
                self.land(step, chunk, way)
                if step < self.size // 2 and self.takes(step + 1, chunk, way):
                    self.send(step + 1, chunk, way)

        def sent(self):
            wait(self.buf.at[pl.ds(0, self.size - 1)], self.ss)

    y_ring = ((r, up), (r, down))
    far_ring = Ring(far_all, far_ss, far_rs, YS, y, y_ring, 2)
    near_ring = Ring(
        near_all, near_ss, near_rs, ZS, z,
        ((r, y * ZS + ((z + 1) & (ZS - 1))), (r, y * ZS + ((z + ZS - 1) & (ZS - 1)))),
        2,
    )
    far_ring.start()
    near_ring.start()
    sub = lax.broadcasted_iota(jnp.int32, (16, 128), 0)
    for g in range(4):
        part = jnp.broadcast_to(mask[:, 128 * g : 128 * g + 128], (16, 128)).astype(BF16)
        for h in range(HEADS):
            mask_send[4 * h + g] = part
    mask_recv[r] = mask_send[r]

    for s in range(1, ROWS):
        to = (r + s) & (ROWS - 1)
        send(mask_send.at[to], mask_recv.at[r], mask_ss, mask_rs, to, c)

    far_ring.turn(1)
    near_ring.turn(1, (0,))
    far_ring.turn(2)
    near_ring.turn(1, (1,))

    wait(mask_recv.at[pl.ds(0, ROWS - 1)], mask_rs)

    pieces = [
        jnp.concatenate([mask_recv[4 * a + b].astype(F32)[:8] for a in range(4)], 0)
        for b in range(4)
    ]
    for q, piece in enumerate(swap_blocks(pieces, 32)):
        for a in range(4):
            mask_cols[q, :, 128 * a : 128 * a + 128] = piece[8 * a : 8 * a + 8]

    far_ring.turn(3)
    near_ring.turn(2)
    def reply(slot, piece):
        yy = (y + YS + slot - 3) & (YS - 1)
        tri_send[yy] = piece.astype(BF16).reshape(ZS, 16, 128)
        row = 2 * yy + (z >> 1)
        half = z & 1
        for t in (1, 2, 3):
            zz = (z + t) & (ZS - 1)
            send(
                tri_send.at[yy, zz], tri_recv.at[half, r], tri_ss, tri_rs,
                row, y * ZS + zz,
            )

    def reply_here(slot):
        yy = (y + YS + slot - 3) & (YS - 1)
        row = 2 * yy + (z >> 1)
        half = z & 1

        @pl.when(row != r)
        def _():
            send(
                tri_send.at[yy, z], tri_recv.at[half, r], tri_ss, tri_rs,
                row, c,
            )

        @pl.when(row == r)
        def _():
            pltpu.make_async_copy(tri_send.at[yy, z], tri_recv.at[half, r], tri_rs).start()

    def products(slots):
        for ch in range(8):
            rights = jnp.concatenate([near_all[s, ch] for s in range(ZS)], 0)
            lefts = [far_all[(y + YS + s - 3) & (YS - 1), ch] for s in slots]
            found = dot(rights, jnp.concatenate(lefts, 0), 1, 1)
            tri_work[64 * ch : 64 * ch + 64, 0 : 16 * len(lefts)] = found
        return [
            jnp.concatenate([tri_work[pl.ds(8 * g + m, 8, stride=64), :] for g in range(8)], 0)
            for m in range(8)
        ]

    tri_work[...] = jnp.zeros_like(tri_work)
    pieces = swap_blocks(products(range(7)), 16)
    for slot in (2, 4, 1, 5, 0, 6, 3):
        reply(slot, pieces[slot])
    for slot in (2, 4, 1, 5, 0, 6, 3):
        reply_here(slot)
    far_ring.turn(4)
    pieces = products([7])
    lane = lax.broadcasted_iota(jnp.int32, pieces[0].shape, 1) >> 4
    merged = pieces[0]
    for m in range(1, 8):
        merged = jnp.where(lane == m, pltpu.roll(pieces[m], 16 * m, 1), merged)
    reply(7, merged)
    reply_here(7)

    wait(edge_send.at[pl.ds(0, ROWS - 1)], edge_ss)
    wait(mask_send.at[pl.ds(0, ROWS - 1)], mask_ss)
    far_ring.sent()
    near_ring.sent()
    wait(tri_recv, tri_rs)

    tri_t = jnp.concatenate(
        [
            tri_recv[half].astype(F32)[:, 8 * g : 8 * g + 8].reshape(128, 128)
            for half in range(2)
            for g in range(2)
        ],
        1,
    )
    gain_col = jnp.broadcast_to(gain_mid[...], (128, 128)).T
    tri_normed = layer_norm(tri_t, jnp.concatenate([gain_col] * 4, 1), 0).astype(BF16)
    update = dot(tri_normed, w_tri_out[...], 0, 0)
    update = jnp.concatenate(
        [
            update[256 * half + 16 * j : 256 * half + 16 * j + 16]
            for j in range(16)
            for half in range(2)
        ],
        0,
    )
    pair_t = (pair_one_t[...] + gate_tri[...] * update).astype(BF16).astype(F32)
    pair_one_t[...] = pair_t

    normed_two = layer_norm(pair_t, gain_att[...]).astype(BF16)
    bias_t = dot(w_bias[...], normed_two, 1, 1)
    for h in range(HEADS):
        base = jnp.zeros((16, 128), F32)
        for v in range(4):
            base = jnp.where(
                sub == v,
                jnp.broadcast_to(bias_t[h : h + 1, 128 * v : 128 * v + 128], (16, 128)),
                base,
            )
        bias_send[h] = base.astype(BF16)
    upper = r >> 3
    half = r & 1

    own = bias_send.at[r >> 2]
    mine = bias_recv.at[r & 7]

    @pl.when(upper != half)
    def _():
        send(own, mine, bias_ss, bias_rs, r ^ 1, c)

    @pl.when(upper == half)
    def _():
        pltpu.make_async_copy(own, mine, bias_rs).start()

    for s in range(1, 8):
        m = ((r >> 1) + s) & 7
        send(bias_send.at[m >> 1], mine, bias_ss, bias_rs, 2 * m + upper, c)

    projected = dot(w_attend[...], normed_two, 0, 1)
    for h in range(HEADS):
        for part in range(3):
            rows = projected[128 * part + 32 * h : 128 * part + 32 * h + 32]
            if part == 0:
                rows = rows * (LOG2E / math.sqrt(HEAD_DIM))
            for g in range(4):
                qkv_send[4 * h + g, 32 * part : 32 * part + 32, :] = rows[
                    :, 128 * g : 128 * g + 128
                ].astype(BF16)
    for s in range(1, ROWS):
        to = (r + s) & (ROWS - 1)
        send(qkv_send.at[to], qkv_recv.at[r], qkv_ss, qkv_rs, to, c)
    qkv_recv[r] = qkv_send[r]

    gate_att[...] = jax.nn.sigmoid(projected[384:])

    wait(bias_recv, bias_rs)

    pieces = [
        jnp.concatenate([bias_recv[4 * a + b].astype(F32)[:8] for a in range(2)], 0)
        for b in range(4)
    ]
    for q, piece in enumerate(swap_blocks(pieces, 32)):
        for a in range(2):
            for v in range(4):
                bias_work[a, 4 * v + q : 4 * v + q + 1, :] = piece[8 * a + v : 8 * a + v + 1]
    for a in range(2):
        bias_all[half, c, :, 128 * a : 128 * a + 128] = bias_work[a].astype(BF16)

    for t in (1, 2, 3):
        part = bias_all.at[half, c]
        send(part, part, biasz_ss, biasz_rs, r, y * ZS + ((z + t) & (ZS - 1)))
    four = bias_all.at[half, pl.ds(y * ZS, ZS)]
    wait(bias_all.at[half, pl.ds(0, ZS - 1)], biasz_rs)
    for near in (1, 7, 2, 6, 3, 5, 4):
        to = ((y + near) & (YS - 1)) * ZS + z
        send(four, four, biasc_ss, biasc_rs.at[y >> 1], r, to)

    side = 1 - 2 * (y & 1)
    order = [((y >> 1) + 4 + apart) & 3 for apart in (0, -side, side, 2)]

    def hand_over(a, count=8):
        wait(bias_all.at[half, pl.ds(8 * a, count)], biasc_rs.at[a])
        part = bias_all.at[half, pl.ds(8 * a, 8)]
        send(part, part, pair_ss, pair_rs.at[half, a], r ^ 1, c)

    hand_over(order[0], 4)
    hand_over(order[1])

    wait(qkv_recv.at[pl.ds(0, ROWS - 1)], qkv_rs)

    tail = (lax.broadcasted_iota(jnp.int32, (16, 512), 0) == 0).astype(BF16)
    first = lax.broadcasted_iota(jnp.int32, (16, 128), 0) == 0
    for q in range(4):
        value_buf[q, 32:48, :] = tail
    for a in range(4):
        pieces = [qkv_recv[4 * a + b].astype(F32) for b in range(4)]
        for q, piece in enumerate(swap_blocks(pieces, 32)):
            query_buf[q, a, 0:32, :] = piece[:32].astype(BF16)
            query_buf[q, a, 32:48, :] = tail[:, :128]
            value_buf[q, 0:32, 128 * a : 128 * a + 128] = piece[64:].astype(BF16)
            present = mask_cols[q, :, 128 * a : 128 * a + 128]
            absent = jnp.concatenate([present, present], 0) < 0.5
            extra = jnp.where(jnp.logical_and(first, absent), MASKED, 0.0)
            keys = jnp.concatenate([piece[32:64], extra], 0)
            key_buf[q, 128 * a : 128 * a + 128, :] = keys.T.astype(BF16)

    for step, a in enumerate(order):
        wait(bias_all.at[1 - half, pl.ds(8 * a, 8)], pair_rs.at[1 - half, a])
        for s in range(2):
            block = bias_all[s, pl.ds(8 * a, 8)].astype(F32).reshape(128, 256) * LOG2E
            bias_full[256 * s : 256 * s + 256, :] = block.T
        pieces = []
        for q in range(4):
            scores = dot(key_buf[q], query_buf[q, a], 1, 0) + bias_full[...]
            weight = jnp.exp2(scores - jnp.max(scores, 0, keepdims=True)).astype(BF16)
            total = dot(value_buf[q], weight, 1, 0)
            pieces.append(total[:32] / total[32:33])
        for b, piece in enumerate(swap_blocks(pieces, 32)):
            att_send[4 * a + b] = piece.astype(BF16)
        for t in (1, 2, 3):
            at = 4 * a + ((r + t) & 3)
            send(att_send.at[at], att_recv.at[r], att_ss, att_rs, at, c)
        at = 4 * a + (r & 3)

        @pl.when(r != at)
        def _():
            send(att_send.at[at], att_recv.at[r], att_ss, att_rs, at, c)

        @pl.when(r == at)
        def _():
            att_recv[r] = att_send[at]

        if step < 2:
            hand_over(order[step + 2])

    @pl.when(upper != half)
    def _():
        wait(bias_recv, bias_ss)

    @pl.when(upper == half)
    def _():
        wait(bias_recv.at[pl.ds(0, 7)], bias_ss)

    to_self = (2 * (r >> 1) + (z >> 1)) == r

    @pl.when(jnp.logical_not(to_self))
    def _():
        wait(tri_send, tri_ss)

    @pl.when(to_self)
    def _():
        wait(tri_send.at[pl.ds(0, YS - 1)], tri_ss)
        wait(tri_send.at[0, pl.ds(0, ZS - 1)], tri_ss)

    wait(qkv_send.at[pl.ds(0, ROWS - 1)], qkv_ss)
    wait(bias_all.at[half, pl.ds(0, ZS - 1)], biasz_ss)
    wait(bias_all.at[half, pl.ds(0, (YS - 1) * ZS)], biasc_ss)
    wait(bias_all.at[half], pair_ss)
    wait(att_send.at[pl.ds(0, ROWS - 1)], att_ss)
    wait(att_recv.at[pl.ds(0, ROWS - 1)], att_rs)

    attended = jnp.concatenate(
        [
            jnp.concatenate([att_recv[4 * h + g].astype(F32) for g in range(4)], 1)
            for h in range(HEADS)
        ],
        0,
    )
    gated = (gate_att[...] * attended).astype(BF16)
    pair_two = (pair_one_t[...] + dot(gated, w_attend_out[...], 0, 0)).astype(BF16).astype(F32)
    normed_three = layer_norm(pair_two, gain_trans[...]).astype(BF16)
    for part in range(4):
        rows = slice(128 * part, 128 * part + 128)
        expanded = dot(normed_three[rows], w_trans_in[...], 1, 0)
        hidden = jnp.concatenate(
            [
                (
                    jax.nn.silu(expanded[t : t + 16, :512]) * expanded[t : t + 16, 512:]
                ).astype(BF16)
                for t in range(0, 128, 16)
            ],
            0,
        )
        work[rows, :] = pair_two[rows] + dot(hidden, w_trans_out[...], 1, 0)
    for i in range(32):
        out_ref[i] = work[pl.ds(i, 16, stride=32), :].astype(BF16)


def per_device(
    pair, pair_mask, gain_tri, w_left, w_right, w_tri_gate, gain_mid, w_tri_out, gain_att, w_attend,
    w_bias, w_attend_out, gain_trans, w_trans_in, w_trans_out,
):
    vmem = pl.BlockSpec(memory_space=pltpu.VMEM)
    dma = pltpu.SemaphoreType.DMA
    row = lambda gain: gain.reshape(1, 128)
    return pl.pallas_call(
        kernel,
        out_shape=pltpu.VMEM((32, 16, 128), BF16),
        in_specs=[pl.BlockSpec(memory_space=pltpu.HBM)] * 15,
        out_specs=vmem,
        scratch_shapes=[
            pltpu.VMEM((32, 16, 128), BF16),
            pltpu.VMEM((16, 32), jnp.int32),
            pltpu.VMEM((1, 128), F32),
            pltpu.VMEM((128, 256), BF16),
            pltpu.VMEM((128, 256), BF16),
            pltpu.VMEM((128, 128), BF16),
            pltpu.VMEM((1, 128), F32),
            pltpu.VMEM((128, 128), BF16),
            pltpu.VMEM((1, 128), F32),
            pltpu.VMEM((128, 512), BF16),
            pltpu.VMEM((4, 128), BF16),
            pltpu.VMEM((128, 128), BF16),
            pltpu.VMEM((1, 128), F32),
            pltpu.VMEM((128, 1024), BF16),
            pltpu.VMEM((512, 128), BF16),
            dma((15,)),
            pltpu.VMEM((512, 128), F32),
            pltpu.VMEM((16, 16, 512), BF16),
            pltpu.VMEM((16, 16, 512), BF16),
            pltpu.VMEM((4, 256, 128), F32),
            pltpu.VMEM((ZS, 8, 16, 512), BF16),
            pltpu.VMEM((YS, 8, 16, 512), BF16),
            pltpu.VMEM((512, 128), F32),
            pltpu.VMEM((512, 128), F32),
            pltpu.VMEM((YS, ZS, 16, 128), BF16),
            pltpu.VMEM((2, 16, 16, 128), BF16),
            pltpu.VMEM((16, 16, 128), BF16),
            pltpu.VMEM((16, 16, 128), BF16),
            pltpu.VMEM((4, 16, 128), BF16),
            pltpu.VMEM((8, 16, 128), BF16),
            pltpu.VMEM((2, 16, 128), F32),
            pltpu.VMEM((2, YS * ZS, 16, 256), BF16),
            pltpu.VMEM((512, 128), F32),
            pltpu.VMEM((4, 8, 512), F32),
            pltpu.VMEM((512, 128), F32),
            pltpu.VMEM((128, 512), F32),
            pltpu.VMEM((16, 96, 128), BF16),
            pltpu.VMEM((16, 96, 128), BF16),
            pltpu.VMEM((4, 4, 48, 128), BF16),
            pltpu.VMEM((4, 512, 48), BF16),
            pltpu.VMEM((4, 48, 512), BF16),
            pltpu.VMEM((16, 32, 128), BF16),
            pltpu.VMEM((16, 32, 128), BF16),
            dma(()), dma(()),
            dma(()), dma((2, 3, 2)),
            dma(()), dma((2, 5, 2)),
            dma(()), dma(()),
            dma(()), dma(()),
            dma(()), dma(()),
            dma(()), dma((4,)),
            dma(()), dma((2, 4)),
            dma(()), dma(()),
            dma(()), dma(()),
            dma(()), dma(()),
        ],
        compiler_params=pltpu.CompilerParams(
            collective_id=0, has_side_effects=True, vmem_limit_bytes=VMEM_LIMIT
        ),
    )(
        pair, pair_mask.T, row(gain_tri), w_left, w_right, w_tri_gate, row(gain_mid),
        w_tri_out, row(gain_att), w_attend, w_bias.T, w_attend_out, row(gain_trans), w_trans_in,
        w_trans_out,
    )


def solution(mesh):
    in_specs = (P("row", "col", None), P("row", "col")) + (P(),) * 13
    return jax.shard_map(
        per_device, mesh=mesh, in_specs=in_specs, out_specs=P("row", "col", None), check_vma=False
    )
```
